32 devices in a mesh: groups: 2 (over y), seq: 4 (over z), expert: 4 (over x, core), tensor: 1.
Axes of the slice: x: 2, y: 2, z: 4, core: 2. Of those that a mesh axis runs over, the one named last changes fastest.
Arguments:
- text_tokens: bfloat16 [1024, 2560], P(('groups', 'seq', 'expert'), 'tensor'), parts along dimension 0, may hold values from -6 to 6
- panels: bfloat16 [512, 8, 2560], P(('groups', 'seq', 'expert'), None, 'tensor'), parts along dimension 0, may hold values from -6 to 6
- panel_target: int32 [512], P(('groups', 'seq', 'expert')), parts along dimension 0, may hold values from 0 to 255, as said below
- expert_ids: int32 [5120, 6], P(('groups', 'seq', 'expert')), parts along dimension 0, may hold values from 0 to 15, all different within a row; in each aligned block of 160 rows (0 to 159, 160 to 319, ...) at most 120 rows name the same one
- gate_weights: float32 [5120, 6], P(('groups', 'seq', 'expert')), parts along dimension 0, may hold values from 0.05 to 0.5
- gate_up_weight: bfloat16 [16, 2, 1408, 2560], P(('seq', 'expert'), None, 'tensor'), may hold values from -0.125 to 0.125
- down_weight: bfloat16 [16, 1408, 2560], P(('seq', 'expert'), 'tensor'), may hold values from -0.15625 to 0.15625
Outputs:
- mixed_out: bfloat16 [5120, 2560], P(('groups', 'seq', 'expert'), 'tensor'), parts along dimension 0
The draws below stay inside these ranges and needn't reach their ends.
There are 2 independent parts, one for each index of `groups`. The reference program is written for one: setup_inputs(seed, part) draws one part's arguments, and reference() takes and returns one part's arrays. A program takes and returns all parts, laid end to end along the dimension named above; an argument that names none is the same for every part. Nothing has to cross between parts.
Inputs may be any that keep to these rules, and one draw needn't show every extreme that they name: `panel_target`: every value appears once. A panel held by owner index d targets an owner with the same index along expert (d % 4 equal). One owner sends at most 6 of its panels to one owner, and exactly 6 to some owner. `expert_ids`: the 6 experts of a token differ. Among the 160 tokens of one owner (aligned blocks of rows), no expert is named more than 120 times.
All inputs are finite; a program needn't handle non-finite values.
Results may differ from the reference program's by a relative error of at most 0.0057.
Values may be sent and summed in bfloat16 or wider, within the bound.
No kernel may reach another device: no remote copies, remote signals or barrier semaphores. Data moves between devices by JAX's collectives and lax.ppermute only.
A program may use at most 128 MiB of HBM per device.

```python
import math
import jax
import jax.numpy as jnp
import numpy as np
from jax import lax

D = 2560
FF = 1408
TOPK = 6
PANEL_ROWS = 8
PAN_DEV = 16
TXT_DEV = 32
EXPERTS = 16
TOK_DEV = 160
TOKENS = 2560
TEXT_ROWS = 512
NPANELS = 256
CAP_P = 6
CAP_E = 120
N_SEQ = 4
N_EXPERT = 4


def draw_panel_target(key, part):
    key = jax.random.fold_in(key, 7)
    first_key, second_key, third_key = jax.random.split(key, 3)
    shifts = jax.vmap(lambda subkey: jax.random.permutation(subkey, N_SEQ))(jax.random.split(first_key, N_EXPERT))
    slot_perm = jax.vmap(lambda subkey: jax.random.permutation(subkey, PAN_DEV))(jax.random.split(second_key, N_EXPERT))
    local_order = jax.vmap(lambda subkey: jax.random.permutation(subkey, PAN_DEV))(jax.random.split(third_key, N_SEQ * N_EXPERT)).reshape(N_SEQ, N_EXPERT, PAN_DEV).astype(jnp.int32)
    run_index = local_order // CAP_P
    shifts_all = jnp.broadcast_to(shifts[None, :, :], (N_SEQ, N_EXPERT, N_SEQ)).astype(jnp.int32)
    shift_taken = jnp.take_along_axis(shifts_all, run_index, axis=2)
    seq_index = jnp.arange(N_SEQ, dtype=jnp.int32)[:, None, None]
    owner_seq = (seq_index + shift_taken) % N_SEQ
    slots_all = jnp.broadcast_to(slot_perm[None, :, :], (N_SEQ, N_EXPERT, PAN_DEV)).astype(jnp.int32)
    slot_taken = jnp.take_along_axis(slots_all, local_order, axis=2)
    owner_index = owner_seq * N_EXPERT + jnp.arange(N_EXPERT, dtype=jnp.int32)[None, :, None]
    return (owner_index * PAN_DEV + slot_taken).reshape(-1).astype(jnp.int32)


def block_scale(stream_key, extent, cuts, low, high):
    def one(dim, blocks):
        steps = jax.random.uniform(jax.random.fold_in(jax.random.fold_in(stream_key, 6), dim), (blocks,), jnp.float32, low / len(cuts), high / len(cuts))
        return jnp.repeat(jnp.exp(steps), extent[dim] // blocks).reshape((-1,) + (1,) * (len(extent) - dim - 1))

    factor_of = one(*cuts[0])
    for cut in cuts[1:]:
        factor_of = factor_of * one(*cut)
    return factor_of


def deal_out(rng, own, number, rows, number_of, top, bound, lean):
    order = jax.random.permutation(rng, number_of)
    crowded, common = load_shares(number_of, rows * top, bound, lean, True), load_shares(number_of, rows * top, bound, lean, False)
    places = jnp.arange(number_of)

    def named(lengths, turn):
        used = int((lengths > 0).sum())
        fixed = max(1, used // 4)
        passed = fixed + (places - fixed + turn * (used - fixed)) % max(1, number_of - fixed)
        return jnp.zeros((number_of,), jnp.int32).at[order[jnp.where(places < fixed, places, passed)]].set(jnp.asarray(lengths, jnp.int32))

    lengths = jnp.where(number % 4 == 0, named(crowded, number // 4), named(common, number - number // 4 - 1))
    mixed = jax.random.permutation(jax.random.fold_in(own, 3), number_of)
    donor, sink = mixed[0:number_of // 2 * 2:2], mixed[1:number_of // 2 * 2:2]
    margin = jnp.minimum(lengths[donor] - 1, bound - lengths[sink]) // 2
    margin = jnp.where((donor == order[0]) | (sink == order[0]) | (lengths[sink] == 0), 0, jnp.maximum(margin, 0))
    passed = jax.random.randint(jax.random.fold_in(own, 4), (number_of // 2,), 0, 1 << 20) % (margin + 1)
    lengths = lengths.at[donor].add(-passed).at[sink].add(passed)
    labels = jnp.searchsorted(jnp.cumsum(lengths), jnp.arange(rows * top), side="right").astype(jnp.int32)
    table = labels.reshape(top, rows).T
    table = table[jax.random.permutation(jax.random.fold_in(own, 1), rows)]
    turn = jax.random.randint(jax.random.fold_in(own, 2), (rows, 1), 0, top)
    return jnp.take_along_axis(table, (jnp.arange(top)[None, :] + turn) % top, axis=1)


def load_shares(amount, total, most, lean, full):
    weights = [(1 << 20) // math.isqrt(grade ** lean) + 1 for grade in range(1, amount + 1)]
    largest = most if full else min(most, max(-(-total // amount), total * weights[0] // sum(weights)))
    least = 1 if total - largest >= amount - 1 else 0
    holding, surplus = [largest] + [least] * (amount - 1), total - largest - least * (amount - 1)
    while surplus > 0:
        candidates = [i for i in range(1, amount) if holding[i] < largest] or [i for i in range(1, amount) if holding[i] < most]
        whole, left = sum([weights[i] for i in candidates]), surplus
        for i in candidates:
            addition = min(most - holding[i], max(1, left * weights[i] // whole), surplus)
            holding[i] = holding[i] + addition
            surplus = surplus - addition
    return np.array(holding)


def centred(key, dims, scale, most, shards=(), held_as=jnp.bfloat16):
    level = block_scale(key, dims, shards, -0.22, 0.18) if shards else 1.0
    drawn = jax.random.normal(key, dims, jnp.float32) * scale * level
    return jnp.minimum(jnp.maximum(drawn, -most), most).astype(held_as)


def setup_inputs(seed: int = 0, part: int = 0) -> dict:
    seeds = jax.random.split(jax.random.key(seed), 8)
    own_keys = jax.random.split(jax.random.fold_in(seeds[7], part), 8)
    text_tokens = centred(own_keys[0], (TEXT_ROWS, D), 1.0, 6.0, ((0, 16),))
    panels = centred(own_keys[1], (NPANELS, PANEL_ROWS, D), 1.0, 6.0, ((0, 16),))
    panel_target = draw_panel_target(jax.random.fold_in(jax.random.fold_in(seeds[7], part), 71), part)
    expert_ids_keys = jax.random.split(jax.random.fold_in(own_keys[3], 1), TOKENS // TOK_DEV)
    expert_ids_turns = jax.random.permutation(jax.random.fold_in(own_keys[3], 3), TOKENS // TOK_DEV)
    expert_ids = jax.vmap(lambda own, number: deal_out(jax.random.fold_in(own_keys[3], 2), own, number, TOK_DEV, EXPERTS, TOPK, CAP_E, 2))(expert_ids_keys, expert_ids_turns).reshape((TOKENS, TOPK))
    gate_weights = jnp.clip(jnp.exp(math.log(0.5) - 2.3025851 * jax.random.uniform(own_keys[4], (TOKENS, TOPK), jnp.float32) ** block_scale(own_keys[4], (TOKENS, TOPK), ((0, 16),), -0.2, 0.2)), 0.05, 0.5)
    gate_up_weight = centred(seeds[5], (EXPERTS, 2, FF, D), D ** -0.5, 0.125, ((0, 16),))
    down_weight = centred(seeds[6], (EXPERTS, FF, D), FF ** -0.5, 0.15625, ((0, 16),))
    return dict(text_tokens=text_tokens, panels=panels, panel_target=panel_target, expert_ids=expert_ids, gate_weights=gate_weights, gate_up_weight=gate_up_weight, down_weight=down_weight)


def reference(text_tokens, panels, panel_target, expert_ids, gate_weights, gate_up_weight, down_weight):
    owners = N_SEQ * N_EXPERT
    panel_count = panels.shape[0]
    inverse = jnp.zeros((panel_count,), jnp.int32).at[panel_target].set(jnp.arange(panel_count, dtype=jnp.int32))
    image_rows = panels[inverse].reshape(owners, PAN_DEV * PANEL_ROWS, D)
    text_rows = text_tokens.reshape(owners, TXT_DEV, D)
    tokens = jnp.concatenate([text_rows, image_rows], axis=1).reshape(TOKENS, D)
    flat_ids = expert_ids.reshape(-1)
    assign_count = flat_ids.shape[0]
    onehot = (flat_ids[:, None] == jnp.arange(EXPERTS, dtype=jnp.int32)[None, :]).astype(jnp.int32)
    before = jnp.cumsum(onehot, axis=0) - onehot
    slot_rank = jnp.sum(before * onehot, axis=1).astype(jnp.int32)
    slot_width = owners * CAP_E
    slot_table = jnp.full((EXPERTS, slot_width), -1, jnp.int32).at[flat_ids, slot_rank].set(
        jnp.arange(assign_count, dtype=jnp.int32))
    gates_flat = gate_weights.reshape(-1)

    def expert_step(running, packed):
        slot_list, pair_weight, out_weight = packed
        is_live = slot_list >= 0
        safe_slot = jnp.where(is_live, slot_list, 0).astype(jnp.int32)
        token_row = (safe_slot // TOPK).astype(jnp.int32)
        gathered = tokens[token_row]
        gate_act = jnp.dot(gathered, pair_weight[0].T, preferred_element_type=jnp.float32)
        up_act = jnp.dot(gathered, pair_weight[1].T, preferred_element_type=jnp.float32)
        hidden = (jax.nn.silu(gate_act) * up_act).astype(jnp.bfloat16)
        expert_out = jnp.dot(hidden, out_weight, preferred_element_type=jnp.float32).astype(jnp.bfloat16)
        weight = jnp.where(is_live, gates_flat[safe_slot], jnp.zeros((), gates_flat.dtype))
        running = running.at[token_row].add(weight[:, None] * expert_out.astype(jnp.float32))
        return running, None

    running, _ = lax.scan(expert_step, jnp.zeros((TOKENS, D), jnp.float32), (slot_table, gate_up_weight, down_weight))
    return running.astype(jnp.bfloat16)
```

```python
import functools

import jax
import jax.numpy as jnp
import numpy as np
from jax import lax
from jax.experimental import pallas as pl
from jax.experimental.pallas import tpu as pltpu
from jax.sharding import PartitionSpec as P

AXES = ("seq", "expert")


def slot_shards(
    text_tokens, panels, panel_target, expert_ids, gate_weights, gate_up_weight, down_weight
):
    seq_count = lax.axis_size("seq")
    expert_count = lax.axis_size("expert")
    owner_count = seq_count * expert_count
    pan_count = panels.shape[0]
    cap_panel = max(2, (3 * pan_count + 2 * seq_count - 1) // (2 * seq_count))
    slot_range = jnp.arange(pan_count, dtype=jnp.int32)
    owner_dev = panel_target // pan_count
    dest_seq = owner_dev // expert_count
    dest_slot = panel_target % pan_count
    onehot = (dest_seq[:, None] == jnp.arange(seq_count, dtype=jnp.int32)[None, :]).astype(
        jnp.int32
    )
    earlier = jnp.cumsum(onehot, axis=0) - onehot
    placing = dest_seq * cap_panel + jnp.sum(earlier * onehot, axis=1)
    outgoing = (
        jnp.zeros((seq_count * cap_panel,) + panels.shape[1:], panels.dtype).at[placing].set(panels)
    )
    labels = jnp.full((seq_count * cap_panel,), -1, jnp.int32).at[placing].set(dest_slot)
    arrived, arrived_labels = (
        lax.all_to_all(outgoing, "seq", split_axis=0, concat_axis=0, tiled=True),
        lax.all_to_all(labels, "seq", split_axis=0, concat_axis=0, tiled=True),
    )
    matches = (arrived_labels[None, :] == slot_range[:, None]).astype(jnp.bfloat16)
    image_rows = jnp.einsum(
        "qn,nrd->qrd", matches, arrived, preferred_element_type=jnp.float32
    ).astype(jnp.bfloat16)
    half_rows = jnp.concatenate([text_tokens, image_rows.reshape(-1, image_rows.shape[-1])], axis=0)
    tokens = lax.all_gather(half_rows, "tensor", axis=1, tiled=True)
    feature_width = tokens.shape[1]
    tok_count, top_count = expert_ids.shape
    experts_all = owner_count * gate_up_weight.shape[0]
    capacity = slot_capacity(tok_count, top_count, experts_all)
    flat_ids = expert_ids.reshape(-1)
    onehot_ids = (flat_ids[:, None] == jnp.arange(experts_all, dtype=jnp.int32)[None, :]).astype(
        jnp.int32
    )
    before = jnp.cumsum(onehot_ids, axis=0) - onehot_ids
    placing_ids = flat_ids * capacity + jnp.sum(before * onehot_ids, axis=1)
    source_rows = jnp.arange(tok_count * top_count, dtype=jnp.int32) // top_count
    outgoing_rows = (
        jnp.zeros((experts_all * capacity, feature_width), tokens.dtype)
        .at[placing_ids]
        .set(tokens[source_rows])
    )
    load_counts = jnp.sum(onehot_ids, axis=0).reshape(experts_all, 1)
    outgoing_rows = outgoing_rows.reshape(experts_all, capacity, feature_width)
    pair_weight = gate_up_weight[0]
    out_weight = down_weight[0]
    arrived_rows, arrived_loads = (
        lax.all_to_all(outgoing_rows, AXES, split_axis=0, concat_axis=0, tiled=True),
        lax.all_to_all(load_counts, AXES, split_axis=0, concat_axis=0, tiled=True),
    )
    arrived_rows = arrived_rows.reshape(-1, feature_width)
    slot_total = arrived_rows.shape[0]
    slot_index = jnp.arange(capacity, dtype=jnp.int32)
    is_live = (slot_index[None, :] < arrived_loads).reshape(-1)
    live_int = is_live.astype(jnp.int32)
    compact_at = jnp.cumsum(live_int) - live_int
    live_total = jnp.sum(live_int)
    compact_src = (
        jnp.zeros((slot_total,), jnp.int32)
        .at[jnp.where(is_live, compact_at, slot_total)]
        .set(jnp.arange(slot_total, dtype=jnp.int32), mode="drop")
    )

    def expert_block(block_no, partial_out):
        chosen = lax.dynamic_slice_in_dim(compact_src, block_no * 128, 128)
        block_rows = arrived_rows[chosen]
        gate_up = jnp.einsum(
            "rd,gfd->grf", block_rows, pair_weight, preferred_element_type=jnp.float32
        )
        hidden = (jax.nn.silu(gate_up[0]) * gate_up[1]).astype(jnp.bfloat16)
        result = jnp.dot(hidden, out_weight, preferred_element_type=jnp.float32)
        return lax.dynamic_update_slice_in_dim(partial_out, result, block_no * 128, 0)

    block_total = (live_total + 127) // 128
    padded_total = (slot_total + 127) // 128 * 128
    partial_out = lax.fori_loop(
        0, block_total, expert_block, jnp.zeros((padded_total, feature_width), jnp.float32)
    )
    summed = lax.psum_scatter(partial_out, "tensor", scatter_dimension=1, tiled=True).astype(
        jnp.bfloat16
    )
    out_width = summed.shape[1]
    returned = jnp.where(
        is_live[:, None], summed[jnp.where(is_live, compact_at, 0)], jnp.zeros((), jnp.bfloat16)
    )
    came_back = lax.all_to_all(
        returned.reshape(experts_all, capacity, out_width),
        AXES,
        split_axis=0,
        concat_axis=0,
        tiled=True,
    )
    half_width = came_back.shape[2]
    picked = came_back.reshape(-1, half_width)[placing_ids].reshape(
        tok_count, top_count, half_width
    )
    mixed_out = jnp.sum(gate_weights[:, :, None] * picked.astype(jnp.float32), axis=1)
    return mixed_out.astype(jnp.bfloat16)


def slot_capacity(tok_count, top_count, experts_all):
    return min(tok_count, (2 * tok_count * top_count // experts_all + 7) // 8 * 8)


class Ring:
    def __init__(self, seq_count, expert_count):
        self.seq, self.expert = seq_count, expert_count
        self.chips = 2 * seq_count
        self.half = seq_count
        self.devices = seq_count * expert_count
        self.slots = [(0, 0), (0, 1), (self.half, 0), (self.half, 1)]
        for s in range(1, self.half):
            self.slots += [(s, 0), (-s, 0), (s, 1), (-s, 1)]
        slot_of = {(r % self.chips, k): i for i, (r, k) in enumerate(self.slots)}
        self.owner_of = np.zeros((self.devices, len(self.slots)), np.int32)
        self.sources_of = np.zeros((self.devices, len(self.slots), seq_count), np.int32)
        for d in range(self.devices):
            p, c = self.place(d)
            for i, (r, k) in enumerate(self.slots):
                q = (p + r) % self.chips
                self.owner_of[d, i] = self.device(q, c ^ k)
                x = q // seq_count
                for z in range(seq_count):
                    pos = z if x == 0 else self.chips - 1 - z
                    self.sources_of[d, i, z] = slot_of[((pos - p) % self.chips, k)]

    def place(self, d):
        z, e = divmod(d, self.expert)
        x, c = divmod(e, 2)
        return (z if x == 0 else self.chips - 1 - z), c

    def device(self, pos, c):
        x, z = (0, pos) if pos < self.seq else (1, self.chips - 1 - pos)
        return z * self.expert + x * 2 + c

    def step(self, by):
        pairs = []
        for d in range(self.devices):
            p, c = self.place(d)
            pairs.append((d, self.device((p + by) % self.chips, c)))
        return pairs

    def swap(self):
        return [(d, d ^ 1) for d in range(self.devices)]


def hidden_kernel(count, rows, *refs):
    x_refs = refs[:count]
    w_ref = refs[count]
    out_ref, x_all = refs[-2:]

    @pl.when(pl.program_id(0) == 0)
    def _():
        for i in range(count):
            x_all[i * rows : (i + 1) * rows, :] = x_refs[i][...]

    width = w_ref.shape[2]
    weight = w_ref[0].reshape(2 * width, w_ref.shape[3])
    both = lax.dot_general(
        x_all[...], weight, (((1,), (1,)), ((), ())), preferred_element_type=jnp.float32
    )
    gate, up = both[:, :width], both[:, width:]
    out_ref[...] = (gate / (1.0 + jnp.exp(-gate)) * up).astype(out_ref.dtype)


def hidden_call(blocks, gate_up_weight, hidden, first_slot, slot_count):
    rows, wide = blocks[0].shape
    _, _, ff, _ = gate_up_weight.shape
    count = len(blocks)
    chunk = 128
    place = first_slot // count
    whole = pl.BlockSpec((rows, wide), lambda i: (0, 0))
    in_specs = [whole] * count + [pl.BlockSpec((1, 2, chunk, wide), lambda i: (0, 0, i, 0))]
    args = list(blocks) + [gate_up_weight]
    aliases = {}
    if hidden is not None:
        in_specs.append(pl.BlockSpec(memory_space=pl.ANY))
        args.append(hidden)
        aliases = {len(args) - 1: 0}
    return pl.pallas_call(
        functools.partial(hidden_kernel, count, rows),
        grid=(ff // chunk,),
        in_specs=in_specs,
        out_specs=pl.BlockSpec((count * rows, chunk), lambda i: (place, i)),
        out_shape=jax.ShapeDtypeStruct((slot_count * rows, ff), jnp.bfloat16),
        scratch_shapes=[pltpu.VMEM((count * rows, wide), jnp.bfloat16)],
        input_output_aliases=aliases,
        compiler_params=pltpu.CompilerParams(vmem_limit_bytes=32 * 1024 * 1024),
        cost_estimate=pl.CostEstimate(
            flops=4 * count * rows * wide * ff,
            bytes_accessed=4 * ff * wide + 2 * count * rows * (wide + ff),
            transcendentals=count * rows * ff,
        ),
    )(*args)


def down_kernel(
    slots, first_slot, rows, text_rows, sources_ref, hidden_ref, order_ref, scale_ref, w_ref,
    own_ref, other_ref, picked,
):
    image_rows = rows - text_rows
    seq_count = order_ref.shape[2] // image_rows

    @pl.when(pl.program_id(0) == 0)
    def _():
        for j in range(slots):
            at = (first_slot + j) * rows
            picked[j * rows : j * rows + text_rows, :] = hidden_ref[at : at + text_rows, :]
            wanted = lax.broadcasted_iota(jnp.int32, (image_rows, order_ref.shape[2]), 0)
            match = jnp.where(order_ref[j] == wanted, 1.0, 0.0).astype(jnp.bfloat16)
            total = jnp.zeros((image_rows, hidden_ref.shape[1]), jnp.float32)
            for z in range(seq_count):
                source = sources_ref[(first_slot + j) * seq_count + z]
                start = pl.multiple_of(source * rows + text_rows, 16)
                total += jnp.dot(
                    match[:, z * image_rows : (z + 1) * image_rows],
                    hidden_ref[pl.ds(start, image_rows), :],
                    preferred_element_type=jnp.float32,
                )
            picked[j * rows + text_rows : (j + 1) * rows, :] = total.astype(jnp.bfloat16)

    result = jnp.dot(picked[...], w_ref[0], preferred_element_type=jnp.float32)
    scaled = (result.astype(jnp.bfloat16).astype(jnp.float32) * scale_ref[...]).astype(jnp.bfloat16)
    half = slots * rows // 2
    own_ref[...] = scaled[:half]
    other_ref[...] = scaled[half:]


def down_call(hidden, order, scale, sources, down_weight, first_slot, slots, rows, text_rows):
    _, ff, wide = down_weight.shape
    chunk = 512
    half = slots * rows // 2
    slot_total = order.shape[0]
    grid_spec = pltpu.PrefetchScalarGridSpec(
        num_scalar_prefetch=1,
        grid=(wide // chunk,),
        in_specs=[
            pl.BlockSpec(hidden.shape, lambda i, s: (0, 0), pipeline_mode=pl.Buffered(1)),
            pl.BlockSpec((slots, 1, order.shape[2]), lambda i, s: (first_slot // slots, 0, 0)),
            pl.BlockSpec((slots * rows, 1), lambda i, s: (first_slot // slots, 0)),
            pl.BlockSpec((1, ff, chunk), lambda i, s: (0, 0, i)),
        ],
        out_specs=[pl.BlockSpec((half, chunk), lambda i, s: (0, i))] * 2,
        scratch_shapes=[pltpu.VMEM((slots * rows, ff), jnp.bfloat16)],
    )
    del slot_total
    return pl.pallas_call(
        functools.partial(down_kernel, slots, first_slot, rows, text_rows),
        grid_spec=grid_spec,
        out_shape=[jax.ShapeDtypeStruct((half, wide), jnp.bfloat16)] * 2,
        compiler_params=pltpu.CompilerParams(vmem_limit_bytes=40 * 1024 * 1024),
        cost_estimate=pl.CostEstimate(
            flops=2 * slots * rows * wide * ff,
            bytes_accessed=2 * ff * wide + 2 * hidden.size + 2 * slots * rows * wide,
            transcendentals=0,
        ),
    )(sources, hidden, order, scale, down_weight)


def add_up(*parts):
    total = parts[0].astype(jnp.float32)
    for part in parts[1:]:
        total = total + part.astype(jnp.float32)
    return total.astype(jnp.bfloat16)


def ring_shards(
    text_tokens, panels, panel_target, expert_ids, gate_weights, gate_up_weight, down_weight
):
    seq_count, expert_count = lax.axis_size("seq"), lax.axis_size("expert")
    ring = Ring(seq_count, expert_count)
    pan_count, panel_rows, wide = panels.shape
    text_rows = text_tokens.shape[0]
    tok_count, top_count = expert_ids.shape
    image_rows = pan_count * panel_rows
    slot_count = len(ring.slots)
    me = lax.axis_index(AXES)

    def onward(array):
        return lax.ppermute(array, AXES, ring.step(1))

    def back(array):
        return lax.ppermute(array, AXES, ring.step(-1))

    def across(array):
        return lax.ppermute(array, AXES, ring.swap())

    own = jnp.concatenate([text_tokens, panels.reshape(image_rows, wide)], axis=0)
    before, after = onward(own), back(own)
    other = across(own)

    table = jnp.concatenate(
        [
            expert_ids.astype(jnp.float32).reshape(-1),
            gate_weights.reshape(-1),
            panel_target.astype(jnp.float32),
        ]
    )
    tables = lax.all_gather(table, AXES)
    pairs = tok_count * top_count
    all_ids = tables[:, :pairs].reshape(-1, tok_count, top_count)
    all_gates = tables[:, pairs : 2 * pairs].reshape(-1, tok_count, top_count)
    weights = jnp.sum(jnp.where(all_ids == me.astype(jnp.float32), all_gates, 0.0), axis=-1)
    target = tables[:, 2 * pairs :].astype(jnp.int32)
    target_seq = target // pan_count // expert_count
    first_row = target_seq * image_rows + target % pan_count * panel_rows
    target_row = first_row[:, :, None] + jnp.arange(panel_rows, dtype=jnp.int32)
    by_column = target_row.reshape(seq_count, expert_count, image_rows).transpose(1, 0, 2)
    by_column = by_column.reshape(expert_count, seq_count * image_rows)
    owners = jnp.asarray(ring.owner_of)[me]
    sources = jnp.asarray(ring.sources_of.reshape(ring.devices, -1))[me]
    order = by_column[owners % expert_count] - (owners // expert_count * image_rows)[:, None]
    order = order[:, None, :]
    scale = weights[owners].reshape(slot_count * tok_count, 1)

    hidden = hidden_call([own, other], gate_up_weight, None, 0, slot_count)
    for s in range(1, ring.half):
        here = [after, before]
        there = [across(after), across(before)]
        if s + 1 < ring.half:
            before, after = onward(before), back(after)
        else:
            cut = tok_count // 2
            far_before, far_after = onward(before[:cut]), back(after[cut:])
        hidden = hidden_call(here + there, gate_up_weight, hidden, 4 * s, slot_count)
    far = jnp.concatenate([far_before, far_after], axis=0)
    hidden = hidden_call([far, across(far)], gate_up_weight, hidden, 2, slot_count)

    def outputs(first_slot, slots):
        mine, others = down_call(
            hidden, order, scale, sources, down_weight, first_slot, slots, tok_count, text_rows
        )
        return mine, across(others)

    mine, swapped = outputs(2, 2)
    cut = tok_count // 2
    ahead = onward(add_up(mine[:cut], swapped[:cut]))
    behind = back(add_up(mine[cut:], swapped[cut:]))
    ahead = jnp.pad(ahead, ((0, tok_count - cut), (0, 0)))
    behind = jnp.pad(behind, ((cut, 0), (0, 0)))
    for s in range(ring.half - 1, 0, -1):
        mine, swapped = outputs(4 * s, 4)
        ahead = onward(add_up(ahead, mine[:tok_count], swapped[:tok_count]))
        behind = back(add_up(behind, mine[tok_count:], swapped[tok_count:]))
    mine, swapped = outputs(0, 2)
    return add_up(mine, swapped, ahead, behind)


def solution(mesh):
    placed = (
        P(("groups", "seq", "expert"), "tensor"),
        P(("groups", "seq", "expert"), None, "tensor"),
        P(("groups", "seq", "expert")),
        P(("groups", "seq", "expert"), None),
        P(("groups", "seq", "expert"), None),
        P(("seq", "expert"), None, "tensor", None),
        P(("seq", "expert"), "tensor", None),
    )

    def chosen(*args):
        seq_count, expert_count = mesh.shape["seq"], mesh.shape["expert"]
        owners = seq_count * expert_count
        tok_count, top_count = args[3].shape[0] // (mesh.shape["groups"] * owners), args[3].shape[1]
        experts_all = args[5].shape[0]
        slot_rows = experts_all * slot_capacity(tok_count, top_count, experts_all)
        dense = owners * tok_count <= 2 * slot_rows
        ring = dense and mesh.shape["tensor"] == 1 and expert_count == 4 and experts_all == owners
        body = ring_shards if ring else slot_shards
        return jax.shard_map(
            body,
            mesh=mesh,
            in_specs=placed,
            out_specs=P(("groups", "seq", "expert"), "tensor"),
            check_vma=False,
        )(*args)

    return chosen
```

```python
import functools

import jax
import jax.numpy as jnp
import numpy as np
from jax import lax
from jax.experimental import pallas as pl
from jax.experimental.pallas import tpu as pltpu
from jax.sharding import PartitionSpec as P

AXES = ("seq", "expert")


def slot_shards(
    text_tokens, panels, panel_target, expert_ids, gate_weights, gate_up_weight, down_weight
):
    seq_count = lax.axis_size("seq")
    expert_count = lax.axis_size("expert")
    owner_count = seq_count * expert_count
    pan_count = panels.shape[0]
    cap_panel = max(2, (3 * pan_count + 2 * seq_count - 1) // (2 * seq_count))
    slot_range = jnp.arange(pan_count, dtype=jnp.int32)
    owner_dev = panel_target // pan_count
    dest_seq = owner_dev // expert_count
    dest_slot = panel_target % pan_count
    onehot = (dest_seq[:, None] == jnp.arange(seq_count, dtype=jnp.int32)[None, :]).astype(
        jnp.int32
    )
    earlier = jnp.cumsum(onehot, axis=0) - onehot
    placing = dest_seq * cap_panel + jnp.sum(earlier * onehot, axis=1)
    outgoing = (
        jnp.zeros((seq_count * cap_panel,) + panels.shape[1:], panels.dtype).at[placing].set(panels)
    )
    labels = jnp.full((seq_count * cap_panel,), -1, jnp.int32).at[placing].set(dest_slot)
    arrived, arrived_labels = (
        lax.all_to_all(outgoing, "seq", split_axis=0, concat_axis=0, tiled=True),
        lax.all_to_all(labels, "seq", split_axis=0, concat_axis=0, tiled=True),
    )
    matches = (arrived_labels[None, :] == slot_range[:, None]).astype(jnp.bfloat16)
    image_rows = jnp.einsum(
        "qn,nrd->qrd", matches, arrived, preferred_element_type=jnp.float32
    ).astype(jnp.bfloat16)
    half_rows = jnp.concatenate([text_tokens, image_rows.reshape(-1, image_rows.shape[-1])], axis=0)
    tokens = lax.all_gather(half_rows, "tensor", axis=1, tiled=True)
    feature_width = tokens.shape[1]
    tok_count, top_count = expert_ids.shape
    experts_all = owner_count * gate_up_weight.shape[0]
    capacity = slot_capacity(tok_count, top_count, experts_all)
    flat_ids = expert_ids.reshape(-1)
    onehot_ids = (flat_ids[:, None] == jnp.arange(experts_all, dtype=jnp.int32)[None, :]).astype(
        jnp.int32
    )
    before = jnp.cumsum(onehot_ids, axis=0) - onehot_ids
    placing_ids = flat_ids * capacity + jnp.sum(before * onehot_ids, axis=1)
    source_rows = jnp.arange(tok_count * top_count, dtype=jnp.int32) // top_count
    outgoing_rows = (
        jnp.zeros((experts_all * capacity, feature_width), tokens.dtype)
        .at[placing_ids]
        .set(tokens[source_rows])
    )
    load_counts = jnp.sum(onehot_ids, axis=0).reshape(experts_all, 1)
    outgoing_rows = outgoing_rows.reshape(experts_all, capacity, feature_width)
    pair_weight = gate_up_weight[0]
    out_weight = down_weight[0]
    arrived_rows, arrived_loads = (
        lax.all_to_all(outgoing_rows, AXES, split_axis=0, concat_axis=0, tiled=True),
        lax.all_to_all(load_counts, AXES, split_axis=0, concat_axis=0, tiled=True),
    )
    arrived_rows = arrived_rows.reshape(-1, feature_width)
    slot_total = arrived_rows.shape[0]
    slot_index = jnp.arange(capacity, dtype=jnp.int32)
    is_live = (slot_index[None, :] < arrived_loads).reshape(-1)
    live_int = is_live.astype(jnp.int32)
    compact_at = jnp.cumsum(live_int) - live_int
    live_total = jnp.sum(live_int)
    compact_src = (
        jnp.zeros((slot_total,), jnp.int32)
        .at[jnp.where(is_live, compact_at, slot_total)]
        .set(jnp.arange(slot_total, dtype=jnp.int32), mode="drop")
    )

    def expert_block(block_no, partial_out):
        chosen = lax.dynamic_slice_in_dim(compact_src, block_no * 128, 128)
        block_rows = arrived_rows[chosen]
        gate_up = jnp.einsum(
            "rd,gfd->grf", block_rows, pair_weight, preferred_element_type=jnp.float32
        )
        hidden = (jax.nn.silu(gate_up[0]) * gate_up[1]).astype(jnp.bfloat16)
        result = jnp.dot(hidden, out_weight, preferred_element_type=jnp.float32)
        return lax.dynamic_update_slice_in_dim(partial_out, result, block_no * 128, 0)

    block_total = (live_total + 127) // 128
    padded_total = (slot_total + 127) // 128 * 128
    partial_out = lax.fori_loop(
        0, block_total, expert_block, jnp.zeros((padded_total, feature_width), jnp.float32)
    )
    summed = lax.psum_scatter(partial_out, "tensor", scatter_dimension=1, tiled=True).astype(
        jnp.bfloat16
    )
    out_width = summed.shape[1]
    returned = jnp.where(
        is_live[:, None], summed[jnp.where(is_live, compact_at, 0)], jnp.zeros((), jnp.bfloat16)
    )
    came_back = lax.all_to_all(
        returned.reshape(experts_all, capacity, out_width),
        AXES,
        split_axis=0,
        concat_axis=0,
        tiled=True,
    )
    half_width = came_back.shape[2]
    picked = came_back.reshape(-1, half_width)[placing_ids].reshape(
        tok_count, top_count, half_width
    )
    mixed_out = jnp.sum(gate_weights[:, :, None] * picked.astype(jnp.float32), axis=1)
    return mixed_out.astype(jnp.bfloat16)


def slot_capacity(tok_count, top_count, experts_all):
    return min(tok_count, (2 * tok_count * top_count // experts_all + 7) // 8 * 8)


class Ring:
    def __init__(self, seq_count, expert_count):
        self.seq, self.expert = seq_count, expert_count
        self.chips = 2 * seq_count
        self.half = seq_count
        self.devices = seq_count * expert_count
        self.slots = [(0, 0), (0, 1), (self.half, 0), (self.half, 1)]
        for s in range(1, self.half):
            self.slots += [(s, 0), (-s, 0), (s, 1), (-s, 1)]
        slot_of = {(r % self.chips, k): i for i, (r, k) in enumerate(self.slots)}
        self.owner_of = np.zeros((self.devices, len(self.slots)), np.int32)
        self.sources_of = np.zeros((self.devices, len(self.slots), seq_count), np.int32)
        for d in range(self.devices):
            p, c = self.place(d)
            for i, (r, k) in enumerate(self.slots):
                q = (p + r) % self.chips
                self.owner_of[d, i] = self.device(q, c ^ k)
                x = q // seq_count
                for z in range(seq_count):
                    pos = z if x == 0 else self.chips - 1 - z
                    self.sources_of[d, i, z] = slot_of[((pos - p) % self.chips, k)]

    def place(self, d):
        z, e = divmod(d, self.expert)
        x, c = divmod(e, 2)
        return (z if x == 0 else self.chips - 1 - z), c

    def device(self, pos, c):
        x, z = (0, pos) if pos < self.seq else (1, self.chips - 1 - pos)
        return z * self.expert + x * 2 + c

    def step(self, by):
        pairs = []
        for d in range(self.devices):
            p, c = self.place(d)
            pairs.append((d, self.device((p + by) % self.chips, c)))
        return pairs

    def swap(self):
        return [(d, d ^ 1) for d in range(self.devices)]


def hidden_kernel(count, rows, *refs):
    x_refs = refs[:count]
    w_ref = refs[count]
    out_ref, x_all = refs[-2:]

    @pl.when(pl.program_id(0) == 0)
    def _():
        for i in range(count):
            x_all[i * rows : (i + 1) * rows, :] = x_refs[i][...]

    width = w_ref.shape[2]
    weight = w_ref[0].reshape(2 * width, w_ref.shape[3])
    both = lax.dot_general(
        x_all[...], weight, (((1,), (1,)), ((), ())), preferred_element_type=jnp.float32
    )
    gate, up = both[:, :width], both[:, width:]
    out_ref[...] = (gate / (1.0 + jnp.exp(-gate)) * up).astype(out_ref.dtype)


def hidden_call(blocks, gate_up_weight, hidden, first_slot, slot_count):
    rows, wide = blocks[0].shape
    _, _, ff, _ = gate_up_weight.shape
    count = len(blocks)
    chunk = 256
    place = first_slot // count
    whole = pl.BlockSpec((rows, wide), lambda i: (0, 0))
    in_specs = [whole] * count + [pl.BlockSpec((1, 2, chunk, wide), lambda i: (0, 0, i, 0))]
    args = list(blocks) + [gate_up_weight]
    aliases = {}
    if hidden is not None:
        in_specs.append(pl.BlockSpec(memory_space=pl.ANY))
        args.append(hidden)
        aliases = {len(args) - 1: 0}
    return pl.pallas_call(
        functools.partial(hidden_kernel, count, rows),
        grid=(pl.cdiv(ff, chunk),),
        in_specs=in_specs,
        out_specs=pl.BlockSpec((count * rows, chunk), lambda i: (place, i)),
        out_shape=jax.ShapeDtypeStruct((slot_count * rows, ff), jnp.bfloat16),
        scratch_shapes=[pltpu.VMEM((count * rows, wide), jnp.bfloat16)],
        input_output_aliases=aliases,
        compiler_params=pltpu.CompilerParams(vmem_limit_bytes=32 * 1024 * 1024),
        cost_estimate=pl.CostEstimate(
            flops=4 * count * rows * wide * ff,
            bytes_accessed=4 * ff * wide + 2 * count * rows * (wide + ff),
            transcendentals=count * rows * ff,
        ),
    )(*args)


def down_kernel(
    slots, first_slot, rows, text_rows, sources_ref, hidden_ref, order_ref, scale_ref, w_ref,
    own_ref, other_ref, picked,
):
    image_rows = rows - text_rows
    seq_count = order_ref.shape[2] // image_rows

    @pl.when(pl.program_id(0) == 0)
    def _():
        for j in range(slots):
            at = (first_slot + j) * rows
            picked[j * rows : j * rows + text_rows, :] = hidden_ref[at : at + text_rows, :]
            wanted = lax.broadcasted_iota(jnp.int32, (image_rows, order_ref.shape[2]), 0)
            match = jnp.where(order_ref[j] == wanted, 1.0, 0.0).astype(jnp.bfloat16)
            total = jnp.zeros((image_rows, hidden_ref.shape[1]), jnp.float32)
            for z in range(seq_count):
                source = sources_ref[(first_slot + j) * seq_count + z]
                start = pl.multiple_of(source * rows + text_rows, 16)
                total += jnp.dot(
                    match[:, z * image_rows : (z + 1) * image_rows],
                    hidden_ref[pl.ds(start, image_rows), :],
                    preferred_element_type=jnp.float32,
                )
            picked[j * rows + text_rows : (j + 1) * rows, :] = total.astype(jnp.bfloat16)

    result = jnp.dot(picked[...], w_ref[0], preferred_element_type=jnp.float32)
    scaled = (result.astype(jnp.bfloat16).astype(jnp.float32) * scale_ref[...]).astype(jnp.bfloat16)
    half = slots * rows // 2
    own_ref[...] = scaled[:half]
    other_ref[...] = scaled[half:]


def down_call(hidden, order, scale, sources, down_weight, first_slot, slots, rows, text_rows):
    _, ff, wide = down_weight.shape
    chunk = 512
    half = slots * rows // 2
    grid_spec = pltpu.PrefetchScalarGridSpec(
        num_scalar_prefetch=1,
        grid=(wide // chunk,),
        in_specs=[
            pl.BlockSpec(hidden.shape, lambda i, s: (0, 0), pipeline_mode=pl.Buffered(1)),
            pl.BlockSpec((slots, 1, order.shape[2]), lambda i, s: (first_slot // slots, 0, 0)),
            pl.BlockSpec((slots * rows, 1), lambda i, s: (first_slot // slots, 0)),
            pl.BlockSpec((1, ff, chunk), lambda i, s: (0, 0, i)),
        ],
        out_specs=[pl.BlockSpec((half, chunk), lambda i, s: (0, i))] * 2,
        scratch_shapes=[pltpu.VMEM((slots * rows, ff), jnp.bfloat16)],
    )
    return pl.pallas_call(
        functools.partial(down_kernel, slots, first_slot, rows, text_rows),
        grid_spec=grid_spec,
        out_shape=[jax.ShapeDtypeStruct((half, wide), jnp.bfloat16)] * 2,
        compiler_params=pltpu.CompilerParams(vmem_limit_bytes=40 * 1024 * 1024),
        cost_estimate=pl.CostEstimate(
            flops=2 * slots * rows * wide * ff,
            bytes_accessed=2 * ff * wide + 2 * hidden.size + 2 * slots * rows * wide,
            transcendentals=0,
        ),
    )(sources, hidden, order, scale, down_weight)


def add_up(*parts):
    total = parts[0].astype(jnp.float32)
    for part in parts[1:]:
        total = total + part.astype(jnp.float32)
    return total.astype(jnp.bfloat16)


def ring_shards(
    text_tokens, panels, panel_target, expert_ids, gate_weights, gate_up_weight, down_weight
):
    seq_count, expert_count = lax.axis_size("seq"), lax.axis_size("expert")
    ring = Ring(seq_count, expert_count)
    pan_count, panel_rows, wide = panels.shape
    text_rows = text_tokens.shape[0]
    tok_count = expert_ids.shape[0]
    image_rows = pan_count * panel_rows
    slot_count = len(ring.slots)
    me = lax.axis_index(AXES)

    def onward(array):
        return lax.ppermute(array, AXES, ring.step(1))

    def back(array):
        return lax.ppermute(array, AXES, ring.step(-1))

    def across(array):
        return lax.ppermute(array, AXES, ring.swap())

    own = jnp.concatenate([text_tokens, panels.reshape(image_rows, wide)], axis=0)
    before, after = onward(own), back(own)
    other = across(own)

    experts = jnp.arange(ring.devices, dtype=jnp.int32)[:, None, None]
    routed = jnp.where(expert_ids[None] == experts, gate_weights[None], 0.0).sum(axis=-1)
    targets = jnp.broadcast_to(panel_target.astype(jnp.float32), (ring.devices, pan_count))
    tables = lax.all_to_all(
        jnp.concatenate([routed, targets], axis=1), AXES, split_axis=0, concat_axis=0, tiled=True
    )
    weights = tables[:, :tok_count]
    target = tables[:, tok_count:].astype(jnp.int32)
    target_seq = target // pan_count // expert_count
    first_row = target_seq * image_rows + target % pan_count * panel_rows
    target_row = first_row[:, :, None] + jnp.arange(panel_rows, dtype=jnp.int32)
    by_column = target_row.reshape(seq_count, expert_count, image_rows).transpose(1, 0, 2)
    by_column = by_column.reshape(expert_count, seq_count * image_rows)
    owners = jnp.asarray(ring.owner_of)[me]
    sources = jnp.asarray(ring.sources_of.reshape(ring.devices, -1))[me]
    order = by_column[owners % expert_count] - (owners // expert_count * image_rows)[:, None]
    order = order[:, None, :]
    scale = weights[owners].reshape(slot_count * tok_count, 1)

    hidden = hidden_call([own, other], gate_up_weight, None, 0, slot_count)
    for s in range(1, ring.half):
        here = [after, before]
        there = [across(after), across(before)]
        if s + 1 < ring.half:
            before, after = onward(before), back(after)
        else:
            cut = tok_count // 2
            far_before, far_after = onward(before[:cut]), back(after[cut:])
        hidden = hidden_call(here + there, gate_up_weight, hidden, 4 * s, slot_count)
    far = jnp.concatenate([far_before, far_after], axis=0)
    hidden = hidden_call([far, across(far)], gate_up_weight, hidden, 2, slot_count)

    def outputs(first_slot, slots):
        mine, others = down_call(
            hidden, order, scale, sources, down_weight, first_slot, slots, tok_count, text_rows
        )
        return mine, across(others)

    cut = tok_count // 2
    mine, swapped = outputs(2, 2)
    leaving = add_up(mine[:cut], swapped[:cut]), add_up(mine[cut:], swapped[cut:])
    for s in range(ring.half - 1, -1, -1):
        ahead, behind = onward(leaving[0]), back(leaving[1])
        if s == ring.half - 1:
            ahead = jnp.pad(ahead, ((0, tok_count - cut), (0, 0)))
            behind = jnp.pad(behind, ((cut, 0), (0, 0)))
        if s:
            mine, swapped = outputs(4 * s, 4)
            leaving = (
                add_up(ahead, mine[:tok_count], swapped[:tok_count]),
                add_up(behind, mine[tok_count:], swapped[tok_count:]),
            )
    mine, swapped = outputs(0, 2)
    return add_up(mine, swapped, ahead, behind)


def solution(mesh):
    placed = (
        P(("groups", "seq", "expert"), "tensor"),
        P(("groups", "seq", "expert"), None, "tensor"),
        P(("groups", "seq", "expert")),
        P(("groups", "seq", "expert"), None),
        P(("groups", "seq", "expert"), None),
        P(("seq", "expert"), None, "tensor", None),
        P(("seq", "expert"), "tensor", None),
    )

    def chosen(*args):
        seq_count, expert_count = mesh.shape["seq"], mesh.shape["expert"]
        owners = seq_count * expert_count
        tok_count, top_count = args[3].shape[0] // (mesh.shape["groups"] * owners), args[3].shape[1]
        experts_all = args[5].shape[0]
        slot_rows = experts_all * slot_capacity(tok_count, top_count, experts_all)
        dense = owners * tok_count <= 2 * slot_rows
        ring = dense and mesh.shape["tensor"] == 1 and expert_count == 4 and experts_all == owners
        body = ring_shards if ring else slot_shards
        return jax.shard_map(
            body,
            mesh=mesh,
            in_specs=placed,
            out_specs=P(("groups", "seq", "expert"), "tensor"),
            check_vma=False,
        )(*args)

    return chosen
```

```python
import functools

import jax
import jax.numpy as jnp
import numpy as np
from jax import lax
from jax.experimental import pallas as pl
from jax.experimental.pallas import tpu as pltpu
from jax.sharding import PartitionSpec as P

AXES = ("seq", "expert")


def slot_shards(
    text_tokens, panels, panel_target, expert_ids, gate_weights, gate_up_weight, down_weight
):
    seq_count = lax.axis_size("seq")
    expert_count = lax.axis_size("expert")
    owner_count = seq_count * expert_count
    pan_count = panels.shape[0]
    cap_panel = max(2, (3 * pan_count + 2 * seq_count - 1) // (2 * seq_count))
    slot_range = jnp.arange(pan_count, dtype=jnp.int32)
    owner_dev = panel_target // pan_count
    dest_seq = owner_dev // expert_count
    dest_slot = panel_target % pan_count
    onehot = (dest_seq[:, None] == jnp.arange(seq_count, dtype=jnp.int32)[None, :]).astype(
        jnp.int32
    )
    earlier = jnp.cumsum(onehot, axis=0) - onehot
    placing = dest_seq * cap_panel + jnp.sum(earlier * onehot, axis=1)
    outgoing = (
        jnp.zeros((seq_count * cap_panel,) + panels.shape[1:], panels.dtype).at[placing].set(panels)
    )
    labels = jnp.full((seq_count * cap_panel,), -1, jnp.int32).at[placing].set(dest_slot)
    arrived, arrived_labels = (
        lax.all_to_all(outgoing, "seq", split_axis=0, concat_axis=0, tiled=True),
        lax.all_to_all(labels, "seq", split_axis=0, concat_axis=0, tiled=True),
    )
    matches = (arrived_labels[None, :] == slot_range[:, None]).astype(jnp.bfloat16)
    image_rows = jnp.einsum(
        "qn,nrd->qrd", matches, arrived, preferred_element_type=jnp.float32
    ).astype(jnp.bfloat16)
    half_rows = jnp.concatenate([text_tokens, image_rows.reshape(-1, image_rows.shape[-1])], axis=0)
    tokens = lax.all_gather(half_rows, "tensor", axis=1, tiled=True)
    feature_width = tokens.shape[1]
    tok_count, top_count = expert_ids.shape
    experts_all = owner_count * gate_up_weight.shape[0]
    capacity = slot_capacity(tok_count, top_count, experts_all)
    flat_ids = expert_ids.reshape(-1)
    onehot_ids = (flat_ids[:, None] == jnp.arange(experts_all, dtype=jnp.int32)[None, :]).astype(
        jnp.int32
    )
    before = jnp.cumsum(onehot_ids, axis=0) - onehot_ids
    placing_ids = flat_ids * capacity + jnp.sum(before * onehot_ids, axis=1)
    source_rows = jnp.arange(tok_count * top_count, dtype=jnp.int32) // top_count
    outgoing_rows = (
        jnp.zeros((experts_all * capacity, feature_width), tokens.dtype)
        .at[placing_ids]
        .set(tokens[source_rows])
    )
    load_counts = jnp.sum(onehot_ids, axis=0).reshape(experts_all, 1)
    outgoing_rows = outgoing_rows.reshape(experts_all, capacity, feature_width)
    pair_weight = gate_up_weight[0]
    out_weight = down_weight[0]
    arrived_rows, arrived_loads = (
        lax.all_to_all(outgoing_rows, AXES, split_axis=0, concat_axis=0, tiled=True),
        lax.all_to_all(load_counts, AXES, split_axis=0, concat_axis=0, tiled=True),
    )
    arrived_rows = arrived_rows.reshape(-1, feature_width)
    slot_total = arrived_rows.shape[0]
    slot_index = jnp.arange(capacity, dtype=jnp.int32)
    is_live = (slot_index[None, :] < arrived_loads).reshape(-1)
    live_int = is_live.astype(jnp.int32)
    compact_at = jnp.cumsum(live_int) - live_int
    live_total = jnp.sum(live_int)
    compact_src = (
        jnp.zeros((slot_total,), jnp.int32)
        .at[jnp.where(is_live, compact_at, slot_total)]
        .set(jnp.arange(slot_total, dtype=jnp.int32), mode="drop")
    )

    def expert_block(block_no, partial_out):
        chosen = lax.dynamic_slice_in_dim(compact_src, block_no * 128, 128)
        block_rows = arrived_rows[chosen]
        gate_up = jnp.einsum(
            "rd,gfd->grf", block_rows, pair_weight, preferred_element_type=jnp.float32
        )
        hidden = (jax.nn.silu(gate_up[0]) * gate_up[1]).astype(jnp.bfloat16)
        result = jnp.dot(hidden, out_weight, preferred_element_type=jnp.float32)
        return lax.dynamic_update_slice_in_dim(partial_out, result, block_no * 128, 0)

    block_total = (live_total + 127) // 128
    padded_total = (slot_total + 127) // 128 * 128
    partial_out = lax.fori_loop(
        0, block_total, expert_block, jnp.zeros((padded_total, feature_width), jnp.float32)
    )
    summed = lax.psum_scatter(partial_out, "tensor", scatter_dimension=1, tiled=True).astype(
        jnp.bfloat16
    )
    out_width = summed.shape[1]
    returned = jnp.where(
        is_live[:, None], summed[jnp.where(is_live, compact_at, 0)], jnp.zeros((), jnp.bfloat16)
    )
    came_back = lax.all_to_all(
        returned.reshape(experts_all, capacity, out_width),
        AXES,
        split_axis=0,
        concat_axis=0,
        tiled=True,
    )
    half_width = came_back.shape[2]
    picked = came_back.reshape(-1, half_width)[placing_ids].reshape(
        tok_count, top_count, half_width
    )
    mixed_out = jnp.sum(gate_weights[:, :, None] * picked.astype(jnp.float32), axis=1)
    return mixed_out.astype(jnp.bfloat16)


def slot_capacity(tok_count, top_count, experts_all):
    return min(tok_count, (2 * tok_count * top_count // experts_all + 7) // 8 * 8)


class Ring:
    def __init__(self, seq_count, expert_count):
        self.seq, self.expert = seq_count, expert_count
        self.chips = 2 * seq_count
        self.half = seq_count
        self.devices = seq_count * expert_count
        self.slots = [(0, 0), (0, 1), (self.half, 0), (self.half, 1)]
        for s in range(1, self.half):
            self.slots += [(s, 0), (-s, 0), (s, 1), (-s, 1)]
        slot_of = {(r % self.chips, k): i for i, (r, k) in enumerate(self.slots)}
        self.owner_of = np.zeros((self.devices, len(self.slots)), np.int32)
        self.sources_of = np.zeros((self.devices, len(self.slots), seq_count), np.int32)
        for d in range(self.devices):
            p, c = self.place(d)
            for i, (r, k) in enumerate(self.slots):
                q = (p + r) % self.chips
                self.owner_of[d, i] = self.device(q, c ^ k)
                x = q // seq_count
                for z in range(seq_count):
                    pos = z if x == 0 else self.chips - 1 - z
                    self.sources_of[d, i, z] = slot_of[((pos - p) % self.chips, k)]

    def place(self, d):
        z, e = divmod(d, self.expert)
        x, c = divmod(e, 2)
        return (z if x == 0 else self.chips - 1 - z), c

    def device(self, pos, c):
        x, z = (0, pos) if pos < self.seq else (1, self.chips - 1 - pos)
        return z * self.expert + x * 2 + c

    def step(self, by):
        pairs = []
        for d in range(self.devices):
            p, c = self.place(d)
            pairs.append((d, self.device((p + by) % self.chips, c)))
        return pairs

    def swap(self):
        return [(d, d ^ 1) for d in range(self.devices)]


def hidden_kernel(count, rows, first_row, chunk, *refs):
    x_refs = refs[:count]
    w_ref = refs[count]
    out_ref, x_all, w_all, h_all, x_sems, w_sems, h_sems = refs[-7:]
    ff = w_ref.shape[2]
    whole, rest = divmod(ff, chunk)
    total = count * rows

    def row_copy(i):
        return pltpu.make_async_copy(
            x_refs[i], x_all.at[i * rows : (i + 1) * rows], x_sems.at[i]
        )

    def weight_copy(i, width):
        part = pl.ds(pl.multiple_of(i * chunk, chunk), width)
        return pltpu.make_async_copy(w_ref.at[0, :, part], w_all.at[:, part], w_sems.at[i])

    def out_copy(i, width):
        part = pl.ds(pl.multiple_of(i * chunk, chunk), width)
        return pltpu.make_async_copy(
            h_all.at[i, :, :width],
            out_ref.at[first_row : first_row + total, part],
            h_sems.at[i],
        )

    widths = [chunk] * whole + [rest] * (rest > 0)
    for i in range(count):
        row_copy(i).start()
    for i, width in enumerate(widths):
        weight_copy(i, width).start()
    for i in range(count):
        row_copy(i).wait()

    def step(i, width):
        weight_copy(i, width).wait()
        part = pl.ds(pl.multiple_of(i * chunk, chunk), width)
        weight = w_all[:, part, :].reshape(2 * width, w_ref.shape[3])
        both = lax.dot_general(
            x_all[...], weight, (((1,), (1,)), ((), ())), preferred_element_type=jnp.float32
        )
        gate, up = both[:, :width], both[:, width:]
        h_all[i, :, :width] = (gate / (1.0 + jnp.exp(-gate)) * up).astype(h_all.dtype)
        out_copy(i, width).start()

    @pl.loop(0, whole)
    def _(i):
        step(i, chunk)

    if rest:
        step(whole, rest)
    for i, width in enumerate(widths):
        out_copy(i, width).wait()


def hidden_call(blocks, gate_up_weight, hidden, first_row, all_rows):
    rows, wide = blocks[0].shape
    _, _, ff, _ = gate_up_weight.shape
    count = len(blocks)
    chunk = 256
    chunks = pl.cdiv(ff, chunk)
    args = list(blocks) + [gate_up_weight]
    aliases = {}
    if hidden is not None:
        args.append(hidden)
        aliases = {len(args) - 1: 0}
    return pl.pallas_call(
        functools.partial(hidden_kernel, count, rows, first_row, chunk),
        in_specs=[pl.BlockSpec(memory_space=pl.ANY)] * len(args),
        out_specs=pl.BlockSpec(memory_space=pl.ANY),
        out_shape=jax.ShapeDtypeStruct((all_rows, ff), jnp.bfloat16),
        scratch_shapes=[
            pltpu.VMEM((count * rows, wide), jnp.bfloat16),
            pltpu.VMEM((2, ff, wide), jnp.bfloat16),
            pltpu.VMEM((chunks, count * rows, chunk), jnp.bfloat16),
            pltpu.SemaphoreType.DMA((count,)),
            pltpu.SemaphoreType.DMA((chunks,)),
            pltpu.SemaphoreType.DMA((chunks,)),
        ],
        input_output_aliases=aliases,
        compiler_params=pltpu.CompilerParams(vmem_limit_bytes=32 * 1024 * 1024),
        cost_estimate=pl.CostEstimate(
            flops=4 * count * rows * wide * ff,
            bytes_accessed=4 * ff * wide + 2 * count * rows * (wide + ff),
            transcendentals=count * rows * ff,
        ),
    )(*args)


def down_kernel(
    slots, first_slot, rows, text_rows, seq_count, sources_ref, hidden_ref, order_ref, scale_ref,
    w_ref, own_ref, other_ref, column, picked, w_all, y_all, text_sems, image_sems, w_sems, y_sems,
):
    image_rows = rows - text_rows
    chunks, _, chunk = w_all.shape
    half = slots * rows // 2

    def text_copy(j):
        at = (first_slot + j) * rows
        return pltpu.make_async_copy(
            hidden_ref.at[at : at + text_rows],
            picked.at[j * rows : j * rows + text_rows],
            text_sems.at[j],
        )

    def image_copy(j, z):
        source = sources_ref[(first_slot + j) * seq_count + z]
        start = pl.multiple_of(source * rows + text_rows, 16)
        return pltpu.make_async_copy(
            hidden_ref.at[pl.ds(start, image_rows)],
            column.at[j, z * image_rows : (z + 1) * image_rows],
            image_sems.at[j, z],
        )

    def weight_copy(i):
        part = pl.ds(pl.multiple_of(i * chunk, chunk), chunk)
        return pltpu.make_async_copy(w_ref.at[0, :, part], w_all.at[i], w_sems.at[i])

    def out_copies(i):
        part = pl.ds(pl.multiple_of(i * chunk, chunk), chunk)
        return (
            pltpu.make_async_copy(y_all.at[i, :half], own_ref.at[:, part], y_sems.at[0, i]),
            pltpu.make_async_copy(y_all.at[i, half:], other_ref.at[:, part], y_sems.at[1, i]),
        )

    for j in range(slots):
        text_copy(j).start()
        for z in range(seq_count):
            image_copy(j, z).start()
    for i in range(chunks):
        weight_copy(i).start()
    wanted = lax.broadcasted_iota(jnp.int32, (image_rows, seq_count * image_rows), 0)
    for j in range(slots):
        text_copy(j).wait()
        for z in range(seq_count):
            image_copy(j, z).wait()
        match = jnp.where(order_ref[j] == wanted, 1.0, 0.0).astype(jnp.bfloat16)
        rows_here = jnp.dot(match, column[j], preferred_element_type=jnp.float32)
        picked[j * rows + text_rows : (j + 1) * rows, :] = rows_here.astype(jnp.bfloat16)

    @pl.loop(0, chunks)
    def _(i):
        weight_copy(i).wait()
        result = jnp.dot(picked[...], w_all[i], preferred_element_type=jnp.float32)
        scaled = result.astype(jnp.bfloat16).astype(jnp.float32) * scale_ref[...]
        y_all[i] = scaled.astype(jnp.bfloat16)
        for copy in out_copies(i):
            copy.start()

    for i in range(chunks):
        for copy in out_copies(i):
            copy.wait()


def down_call(hidden, order, scale, sources, down_weight, first_slot, slots, rows, text_rows):
    _, ff, wide = down_weight.shape
    chunk = 512
    chunks = wide // chunk
    half = slots * rows // 2
    source_rows = order.shape[2]
    seq_count = source_rows // (rows - text_rows)
    grid_spec = pltpu.PrefetchScalarGridSpec(
        num_scalar_prefetch=1,
        grid=(1,),
        in_specs=[
            pl.BlockSpec(memory_space=pl.ANY),
            pl.BlockSpec((slots, 1, source_rows), lambda i, s: (first_slot // slots, 0, 0)),
            pl.BlockSpec((slots * rows, 1), lambda i, s: (first_slot // slots, 0)),
            pl.BlockSpec(memory_space=pl.ANY),
        ],
        out_specs=[pl.BlockSpec(memory_space=pl.ANY)] * 2,
        scratch_shapes=[
            pltpu.VMEM((slots, source_rows, ff), jnp.bfloat16),
            pltpu.VMEM((slots * rows, ff), jnp.bfloat16),
            pltpu.VMEM((chunks, ff, chunk), jnp.bfloat16),
            pltpu.VMEM((chunks, slots * rows, chunk), jnp.bfloat16),
            pltpu.SemaphoreType.DMA((slots,)),
            pltpu.SemaphoreType.DMA((slots, seq_count)),
            pltpu.SemaphoreType.DMA((chunks,)),
            pltpu.SemaphoreType.DMA((2, chunks)),
        ],
    )
    return pl.pallas_call(
        functools.partial(down_kernel, slots, first_slot, rows, text_rows, seq_count),
        grid_spec=grid_spec,
        out_shape=[jax.ShapeDtypeStruct((half, wide), jnp.bfloat16)] * 2,
        compiler_params=pltpu.CompilerParams(vmem_limit_bytes=32 * 1024 * 1024),
        cost_estimate=pl.CostEstimate(
            flops=2 * slots * rows * wide * ff,
            bytes_accessed=2 * ff * wide + 2 * slots * rows * wide,
            transcendentals=0,
        ),
    )(sources, hidden, order, scale, down_weight)


def add_up(*parts):
    total = parts[0].astype(jnp.float32)
    for part in parts[1:]:
        total = total + part.astype(jnp.float32)
    return total.astype(jnp.bfloat16)


def ring_shards(
    text_tokens, panels, panel_target, expert_ids, gate_weights, gate_up_weight, down_weight
):
    seq_count, expert_count = lax.axis_size("seq"), lax.axis_size("expert")
    ring = Ring(seq_count, expert_count)
    pan_count, panel_rows, wide = panels.shape
    text_rows = text_tokens.shape[0]
    tok_count = expert_ids.shape[0]
    image_rows = pan_count * panel_rows
    slot_count = len(ring.slots)
    me = lax.axis_index(AXES)

    def onward(array):
        return lax.ppermute(array, AXES, ring.step(1))

    def back(array):
        return lax.ppermute(array, AXES, ring.step(-1))

    def across(array):
        return lax.ppermute(array, AXES, ring.swap())

    own = jnp.concatenate([text_tokens, panels.reshape(image_rows, wide)], axis=0)
    before, after = onward(own), back(own)
    other = across(own)

    experts = jnp.arange(ring.devices, dtype=jnp.int32)[:, None, None]
    routed = jnp.where(expert_ids[None] == experts, gate_weights[None], 0.0).sum(axis=-1)
    targets = jnp.broadcast_to(panel_target.astype(jnp.float32), (ring.devices, pan_count))
    outgoing = jnp.concatenate([routed, targets], axis=1)
    tables = (lax.all_to_all(outgoing, AXES, split_axis=0, concat_axis=0, tiled=True),)

    def read_tables(tables):
        weights = tables[:, :tok_count]
        target = tables[:, tok_count:].astype(jnp.int32)
        target_seq = target // pan_count // expert_count
        first_row = target_seq * image_rows + target % pan_count * panel_rows
        target_row = first_row[:, :, None] + jnp.arange(panel_rows, dtype=jnp.int32)
        by_column = target_row.reshape(seq_count, expert_count, image_rows).transpose(1, 0, 2)
        by_column = by_column.reshape(expert_count, seq_count * image_rows)
        owners = jnp.asarray(ring.owner_of)[me]
        sources = jnp.asarray(ring.sources_of.reshape(ring.devices, -1))[me]
        order = by_column[owners % expert_count] - (owners // expert_count * image_rows)[:, None]
        order = order[:, None, :]
        scale = weights[owners].reshape(slot_count * tok_count, 1)
        return order, scale, sources

    all_rows = slot_count * tok_count
    hidden = hidden_call([own, other], gate_up_weight, None, 0, all_rows)
    hidden, before, after = lax.optimization_barrier((hidden, before, after))
    cut = tok_count // 2
    for s in range(1, ring.half):
        here = [after, before]
        there = [across(after), across(before)]
        if s + 1 == ring.half:
            before, after = before[:cut], after[cut:]
        before, after = onward(before), back(after)
        first_row = 4 * s * tok_count
        hidden = hidden_call(here + there, gate_up_weight, hidden, first_row, all_rows)
        hidden, before, after, *tables = lax.optimization_barrier((hidden, before, after, *tables))
        if s == 1:
            tables = read_tables(*tables)
    order, scale, sources = tables
    far = [before, after, across(before), across(after)]
    hidden = hidden_call(far, gate_up_weight, hidden, 2 * tok_count, all_rows)

    def outputs(first_slot, slots):
        mine, others = down_call(
            hidden, order, scale, sources, down_weight, first_slot, slots, tok_count, text_rows
        )
        return mine, across(others)

    mine, swapped = outputs(2, 2)
    leaving = add_up(mine[:cut], swapped[:cut]), add_up(mine[cut:], swapped[cut:])
    for s in range(ring.half - 1, -1, -1):
        ahead, behind = onward(leaving[0]), back(leaving[1])
        if s == ring.half - 1:
            ahead = jnp.pad(ahead, ((0, tok_count - cut), (0, 0)))
            behind = jnp.pad(behind, ((cut, 0), (0, 0)))
        if s:
            mine, swapped = outputs(4 * s, 4)
            leaving = (
                add_up(ahead, mine[:tok_count], swapped[:tok_count]),
                add_up(behind, mine[tok_count:], swapped[tok_count:]),
            )
    mine, swapped = outputs(0, 2)
    return add_up(mine, swapped, ahead, behind)


def solution(mesh):
    placed = (
        P(("groups", "seq", "expert"), "tensor"),
        P(("groups", "seq", "expert"), None, "tensor"),
        P(("groups", "seq", "expert")),
        P(("groups", "seq", "expert"), None),
        P(("groups", "seq", "expert"), None),
        P(("seq", "expert"), None, "tensor", None),
        P(("seq", "expert"), "tensor", None),
    )

    def chosen(*args):
        seq_count, expert_count = mesh.shape["seq"], mesh.shape["expert"]
        owners = seq_count * expert_count
        tok_count, top_count = args[3].shape[0] // (mesh.shape["groups"] * owners), args[3].shape[1]
        experts_all = args[5].shape[0]
        slot_rows = experts_all * slot_capacity(tok_count, top_count, experts_all)
        dense = owners * tok_count <= 2 * slot_rows
        ring = dense and mesh.shape["tensor"] == 1 and expert_count == 4 and experts_all == owners
        body = ring_shards if ring else slot_shards
        return jax.shard_map(
            body,
            mesh=mesh,
            in_specs=placed,
            out_specs=P(("groups", "seq", "expert"), "tensor"),
            check_vma=False,
        )(*args)

    return chosen
```

```python
import functools

import jax
import jax.numpy as jnp
import numpy as np
from jax import lax
from jax.experimental import pallas as pl
from jax.experimental.pallas import tpu as pltpu
from jax.sharding import PartitionSpec as P

AXES = ("seq", "expert")


def slot_shards(
    text_tokens, panels, panel_target, expert_ids, gate_weights, gate_up_weight, down_weight
):
    seq_count = lax.axis_size("seq")
    expert_count = lax.axis_size("expert")
    owner_count = seq_count * expert_count
    pan_count = panels.shape[0]
    cap_panel = max(2, (3 * pan_count + 2 * seq_count - 1) // (2 * seq_count))
    slot_range = jnp.arange(pan_count, dtype=jnp.int32)
    owner_dev = panel_target // pan_count
    dest_seq = owner_dev // expert_count
    dest_slot = panel_target % pan_count
    onehot = (dest_seq[:, None] == jnp.arange(seq_count, dtype=jnp.int32)[None, :]).astype(
        jnp.int32
    )
    earlier = jnp.cumsum(onehot, axis=0) - onehot
    placing = dest_seq * cap_panel + jnp.sum(earlier * onehot, axis=1)
    outgoing = (
        jnp.zeros((seq_count * cap_panel,) + panels.shape[1:], panels.dtype).at[placing].set(panels)
    )
    labels = jnp.full((seq_count * cap_panel,), -1, jnp.int32).at[placing].set(dest_slot)
    arrived, arrived_labels = (
        lax.all_to_all(outgoing, "seq", split_axis=0, concat_axis=0, tiled=True),
        lax.all_to_all(labels, "seq", split_axis=0, concat_axis=0, tiled=True),
    )
    matches = (arrived_labels[None, :] == slot_range[:, None]).astype(jnp.bfloat16)
    image_rows = jnp.einsum(
        "qn,nrd->qrd", matches, arrived, preferred_element_type=jnp.float32
    ).astype(jnp.bfloat16)
    half_rows = jnp.concatenate([text_tokens, image_rows.reshape(-1, image_rows.shape[-1])], axis=0)
    tokens = lax.all_gather(half_rows, "tensor", axis=1, tiled=True)
    feature_width = tokens.shape[1]
    tok_count, top_count = expert_ids.shape
    experts_all = owner_count * gate_up_weight.shape[0]
    capacity = slot_capacity(tok_count, top_count, experts_all)
    flat_ids = expert_ids.reshape(-1)
    onehot_ids = (flat_ids[:, None] == jnp.arange(experts_all, dtype=jnp.int32)[None, :]).astype(
        jnp.int32
    )
    before = jnp.cumsum(onehot_ids, axis=0) - onehot_ids
    placing_ids = flat_ids * capacity + jnp.sum(before * onehot_ids, axis=1)
    source_rows = jnp.arange(tok_count * top_count, dtype=jnp.int32) // top_count
    outgoing_rows = (
        jnp.zeros((experts_all * capacity, feature_width), tokens.dtype)
        .at[placing_ids]
        .set(tokens[source_rows])
    )
    load_counts = jnp.sum(onehot_ids, axis=0).reshape(experts_all, 1)
    outgoing_rows = outgoing_rows.reshape(experts_all, capacity, feature_width)
    pair_weight = gate_up_weight[0]
    out_weight = down_weight[0]
    arrived_rows, arrived_loads = (
        lax.all_to_all(outgoing_rows, AXES, split_axis=0, concat_axis=0, tiled=True),
        lax.all_to_all(load_counts, AXES, split_axis=0, concat_axis=0, tiled=True),
    )
    arrived_rows = arrived_rows.reshape(-1, feature_width)
    slot_total = arrived_rows.shape[0]
    slot_index = jnp.arange(capacity, dtype=jnp.int32)
    is_live = (slot_index[None, :] < arrived_loads).reshape(-1)
    live_int = is_live.astype(jnp.int32)
    compact_at = jnp.cumsum(live_int) - live_int
    live_total = jnp.sum(live_int)
    compact_src = (
        jnp.zeros((slot_total,), jnp.int32)
        .at[jnp.where(is_live, compact_at, slot_total)]
        .set(jnp.arange(slot_total, dtype=jnp.int32), mode="drop")
    )

    def expert_block(block_no, partial_out):
        chosen = lax.dynamic_slice_in_dim(compact_src, block_no * 128, 128)
        block_rows = arrived_rows[chosen]
        gate_up = jnp.einsum(
            "rd,gfd->grf", block_rows, pair_weight, preferred_element_type=jnp.float32
        )
        hidden = (jax.nn.silu(gate_up[0]) * gate_up[1]).astype(jnp.bfloat16)
        result = jnp.dot(hidden, out_weight, preferred_element_type=jnp.float32)
        return lax.dynamic_update_slice_in_dim(partial_out, result, block_no * 128, 0)

    block_total = (live_total + 127) // 128
    padded_total = (slot_total + 127) // 128 * 128
    partial_out = lax.fori_loop(
        0, block_total, expert_block, jnp.zeros((padded_total, feature_width), jnp.float32)
    )
    summed = lax.psum_scatter(partial_out, "tensor", scatter_dimension=1, tiled=True).astype(
        jnp.bfloat16
    )
    out_width = summed.shape[1]
    returned = jnp.where(
        is_live[:, None], summed[jnp.where(is_live, compact_at, 0)], jnp.zeros((), jnp.bfloat16)
    )
    came_back = lax.all_to_all(
        returned.reshape(experts_all, capacity, out_width),
        AXES,
        split_axis=0,
        concat_axis=0,
        tiled=True,
    )
    half_width = came_back.shape[2]
    picked = came_back.reshape(-1, half_width)[placing_ids].reshape(
        tok_count, top_count, half_width
    )
    mixed_out = jnp.sum(gate_weights[:, :, None] * picked.astype(jnp.float32), axis=1)
    return mixed_out.astype(jnp.bfloat16)


def slot_capacity(tok_count, top_count, experts_all):
    return min(tok_count, (2 * tok_count * top_count // experts_all + 7) // 8 * 8)


class Ring:
    def __init__(self, seq_count, expert_count):
        self.seq, self.expert = seq_count, expert_count
        self.chips = 2 * seq_count
        self.half = seq_count
        self.devices = seq_count * expert_count
        self.slots = [(0, 0), (0, 1), (self.half, 0), (self.half, 1)]
        for s in range(1, self.half):
            self.slots += [(s, 0), (-s, 0), (s, 1), (-s, 1)]
        slot_of = {(r % self.chips, k): i for i, (r, k) in enumerate(self.slots)}
        self.owner_of = np.zeros((self.devices, len(self.slots)), np.int32)
        self.sources_of = np.zeros((self.devices, len(self.slots), seq_count), np.int32)
        for d in range(self.devices):
            p, c = self.place(d)
            for i, (r, k) in enumerate(self.slots):
                q = (p + r) % self.chips
                self.owner_of[d, i] = self.device(q, c ^ k)
                x = q // seq_count
                for z in range(seq_count):
                    pos = z if x == 0 else self.chips - 1 - z
                    self.sources_of[d, i, z] = slot_of[((pos - p) % self.chips, k)]

    def place(self, d):
        z, e = divmod(d, self.expert)
        x, c = divmod(e, 2)
        return (z if x == 0 else self.chips - 1 - z), c

    def device(self, pos, c):
        x, z = (0, pos) if pos < self.seq else (1, self.chips - 1 - pos)
        return z * self.expert + x * 2 + c

    def step(self, by):
        pairs = []
        for d in range(self.devices):
            p, c = self.place(d)
            pairs.append((d, self.device((p + by) % self.chips, c)))
        return pairs

    def swap(self):
        return [(d, d ^ 1) for d in range(self.devices)]


def hidden_kernel(count, rows, first_row, chunk, fetch, *refs):
    x_refs, refs = refs[:count], refs[count:]
    if fetch == "gate_up":
        far_ref, out_ref, w_ref, x_all, sems = refs
    elif fetch == "down":
        w_ref, _, far_ref, out_ref, _, down_ref, x_all, sems = refs
    else:
        w_ref, _, out_ref, x_all = refs[0], refs[1], refs[2], refs[-1]
    ff, wide = w_ref.shape[2:]
    whole, rest = divmod(ff, chunk)
    total = count * rows

    def fetched(i, width):
        part = pl.ds(pl.multiple_of(i * chunk, chunk), width)
        return pltpu.make_async_copy(far_ref.at[0, :, part], w_ref.at[0, :, part], sems.at[i])

    if fetch == "gate_up":
        for i in range(whole):
            fetched(i, chunk).start()
        if rest:
            fetched(whole, rest).start()
    if fetch == "down":
        pltpu.make_async_copy(far_ref, down_ref, sems.at[0]).start()
    for i in range(count):
        x_all[i * rows : (i + 1) * rows, :] = x_refs[i][...]

    def step(i, width):
        if fetch == "gate_up":
            fetched(i, width).wait()
        part = pl.ds(pl.multiple_of(i * chunk, chunk), width)
        weight = w_ref[0, :, part, :].reshape(2 * width, wide)
        both = lax.dot_general(
            x_all[...], weight, (((1,), (1,)), ((), ())), preferred_element_type=jnp.float32
        )
        gate, up = both[:, :width], both[:, width:]
        hidden = (gate / (1.0 + jnp.exp(-gate)) * up).astype(out_ref.dtype)
        out_ref[first_row : first_row + total, part] = hidden

    @pl.loop(0, whole)
    def _(i):
        step(i, chunk)

    if rest:
        step(whole, rest)
    if fetch == "down":
        pltpu.make_async_copy(far_ref, down_ref, sems.at[0]).wait()


def kept(array):
    return pltpu.with_memory_space_constraint(array, pltpu.VMEM)


def distant(array):
    return pltpu.with_memory_space_constraint(array, pltpu.HBM)


def hidden_call(blocks, gate_up_weight, hidden, first_row, all_rows, down_weight=None, last=False):
    rows, wide = blocks[0].shape
    ff = gate_up_weight.shape[2]
    count = len(blocks)
    chunk = 256
    here, far = pl.BlockSpec(memory_space=pltpu.VMEM), pl.BlockSpec(memory_space=pltpu.HBM)
    args, in_specs = [kept(block) for block in blocks], [here] * count
    out_shape, aliases = [pltpu.VMEM((all_rows, ff), jnp.bfloat16)], {}
    scratch = [pltpu.VMEM((count * rows, wide), jnp.bfloat16)]
    fetch = None
    if hidden is None:
        fetch = "gate_up"
        args, in_specs = args + [distant(gate_up_weight)], in_specs + [far]
        out_shape.append(pltpu.VMEM(gate_up_weight.shape, gate_up_weight.dtype))
        scratch.append(pltpu.SemaphoreType.DMA((pl.cdiv(ff, chunk),)))
    else:
        args, in_specs = args + [kept(gate_up_weight), kept(hidden)], in_specs + [here, here]
        aliases = {count + 1: 0}
        if not last:
            out_shape.append(pltpu.VMEM(gate_up_weight.shape, gate_up_weight.dtype))
            aliases[count] = 1
        if down_weight is not None:
            fetch = "down"
            args, in_specs = args + [distant(down_weight)], in_specs + [far]
            out_shape.append(pltpu.VMEM(down_weight.shape, down_weight.dtype))
            scratch.append(pltpu.SemaphoreType.DMA((1,)))
    return pl.pallas_call(
        functools.partial(hidden_kernel, count, rows, first_row, chunk, fetch),
        in_specs=in_specs,
        out_specs=[here] * len(out_shape),
        out_shape=out_shape,
        scratch_shapes=scratch,
        input_output_aliases=aliases,
        compiler_params=pltpu.CompilerParams(vmem_limit_bytes=14 * 1024 * 1024),
        cost_estimate=pl.CostEstimate(
            flops=4 * count * rows * wide * ff,
            bytes_accessed=4 * ff * wide + 2 * count * rows * (wide + ff),
            transcendentals=count * rows * ff,
        ),
    )(*args)


def down_kernel(
    slots, first_slot, rows, text_rows, seq_count, expert_count, chunk, places_ref, hidden_ref,
    tables_ref, w_ref, own_ref, other_ref, column, picked, scale,
):
    image_rows = rows - text_rows
    half = slots * rows // 2
    slot_total = hidden_ref.shape[0] // rows
    targets_at = tables_ref.shape[2] - image_rows
    wanted = lax.broadcasted_iota(jnp.int32, (image_rows, image_rows), 0).astype(jnp.float32)
    diagonal = lax.broadcasted_iota(jnp.int32, (rows, rows), 0) == lax.broadcasted_iota(
        jnp.int32, (rows, rows), 1
    )
    for j in range(slots):
        at = (first_slot + j) * rows
        picked[j * rows : j * rows + text_rows, :] = hidden_ref[at : at + text_rows, :]
        owner = places_ref[first_slot + j]
        first_wanted = wanted + (owner // expert_count * image_rows).astype(jnp.float32)
        matches = []
        for z in range(seq_count):
            source = places_ref[slot_total + (first_slot + j) * seq_count + z]
            start = pl.multiple_of(source * rows + text_rows, 16)
            column[z * image_rows : (z + 1) * image_rows, :] = hidden_ref[
                pl.ds(start, image_rows), :
            ]
            targets = tables_ref[places_ref[source], :, targets_at:]
            matches.append(jnp.where(targets == first_wanted, 1.0, 0.0).astype(jnp.bfloat16))
        match = jnp.concatenate(matches, axis=1)
        rows_here = jnp.dot(match, column[...], preferred_element_type=jnp.float32)
        picked[j * rows + text_rows : (j + 1) * rows, :] = rows_here.astype(jnp.bfloat16)
        weights = jnp.where(diagonal, tables_ref[owner, :, :rows], 0.0)
        scale[j * rows : (j + 1) * rows, :] = jnp.sum(weights, axis=1, keepdims=True)

    @pl.loop(0, w_ref.shape[2] // chunk)
    def _(i):
        part = pl.ds(pl.multiple_of(i * chunk, chunk), chunk)
        result = jnp.dot(picked[...], w_ref[0, :, part], preferred_element_type=jnp.float32)
        scaled = result.astype(jnp.bfloat16).astype(jnp.float32) * scale[...]
        scaled = scaled.astype(jnp.bfloat16)
        own_ref[:, part] = scaled[:half]
        other_ref[:, part] = scaled[half:]


def down_call(
    hidden, tables, places, down_weight, first_slot, slots, rows, text_rows, seq_count, expert_count
):
    _, ff, wide = down_weight.shape
    half = slots * rows // 2
    here = pl.BlockSpec(memory_space=pltpu.VMEM)
    return pl.pallas_call(
        functools.partial(
            down_kernel, slots, first_slot, rows, text_rows, seq_count, expert_count, 512
        ),
        grid_spec=pltpu.PrefetchScalarGridSpec(
            num_scalar_prefetch=1,
            grid=(1,),
            in_specs=[here] * 3,
            out_specs=[here] * 2,
            scratch_shapes=[
                pltpu.VMEM((seq_count * (rows - text_rows), ff), jnp.bfloat16),
                pltpu.VMEM((slots * rows, ff), jnp.bfloat16),
                pltpu.VMEM((slots * rows, 1), jnp.float32),
            ],
        ),
        out_shape=[pltpu.VMEM((half, wide), jnp.bfloat16)] * 2,
        compiler_params=pltpu.CompilerParams(vmem_limit_bytes=14 * 1024 * 1024),
        cost_estimate=pl.CostEstimate(
            flops=2 * slots * rows * wide * ff,
            bytes_accessed=2 * ff * wide + 2 * slots * rows * wide,
            transcendentals=0,
        ),
    )(places, kept(hidden), tables, kept(down_weight))


def add_up(*parts):
    total = parts[0].astype(jnp.float32)
    for part in parts[1:]:
        total = total + part.astype(jnp.float32)
    return total.astype(jnp.bfloat16)


def ring_shards(
    text_tokens, panels, panel_target, expert_ids, gate_weights, gate_up_weight, down_weight
):
    seq_count, expert_count = lax.axis_size("seq"), lax.axis_size("expert")
    ring = Ring(seq_count, expert_count)
    pan_count, panel_rows, wide = panels.shape
    text_rows = text_tokens.shape[0]
    tok_count = expert_ids.shape[0]
    image_rows = pan_count * panel_rows
    slot_count = len(ring.slots)
    me = lax.axis_index(AXES)

    def onward(array):
        return lax.ppermute(array, AXES, ring.step(1))

    def back(array):
        return lax.ppermute(array, AXES, ring.step(-1))

    def across(array):
        return lax.ppermute(array, AXES, ring.swap())

    own = jnp.concatenate([text_tokens, panels.reshape(image_rows, wide)], axis=0)
    before, after = onward(own), back(own)
    other = across(own)

    experts = jnp.arange(ring.devices, dtype=jnp.int32)[:, None, None]
    routed = jnp.where(expert_ids[None] == experts, gate_weights[None], 0.0).sum(axis=-1)
    target_seq = panel_target // pan_count // expert_count
    targets = target_seq * image_rows + panel_target % pan_count * panel_rows
    targets = (targets[:, None] + jnp.arange(panel_rows, dtype=jnp.int32)).reshape(image_rows)
    targets = jnp.broadcast_to(targets.astype(jnp.float32), (ring.devices, image_rows))
    routed = jnp.pad(routed, ((0, 0), (0, -tok_count % 128)))
    outgoing = jnp.concatenate([routed, targets], axis=1)[:, None, :]
    tables = lax.all_to_all(outgoing, AXES, split_axis=0, concat_axis=0, tiled=True)
    places = np.concatenate([ring.owner_of, ring.sources_of.reshape(ring.devices, -1)], axis=1)
    places = jnp.asarray(places)[me]

    all_rows = slot_count * tok_count
    hidden, gate_up = hidden_call([own, other], gate_up_weight, None, 0, all_rows)
    hidden, before, after, tables = lax.optimization_barrier((hidden, before, after, tables))
    cut = tok_count // 2
    for s in range(1, ring.half):
        here = [after, before]
        there = [across(after), across(before)]
        if s + 1 == ring.half:
            before, after = before[:cut], after[cut:]
        before, after = onward(before), back(after)
        first_row = 4 * s * tok_count
        extra = down_weight if s == 1 else None
        hidden, gate_up, *down = hidden_call(
            here + there, gate_up, hidden, first_row, all_rows, extra
        )
        if down:
            (down_here,) = down
        hidden, before, after = lax.optimization_barrier((hidden, before, after))
    far = [before, after, across(before), across(after)]
    (hidden,) = hidden_call(far, gate_up, hidden, 2 * tok_count, all_rows, last=True)

    def outputs(first_slot, slots):
        mine, others = down_call(
            hidden, tables, places, down_here, first_slot, slots, tok_count, text_rows,
            seq_count, expert_count,
        )
        return mine, across(others)

    mine, swapped = outputs(2, 2)
    leaving = add_up(mine[:cut], swapped[:cut]), add_up(mine[cut:], swapped[cut:])
    for s in range(ring.half - 1, -1, -1):
        ahead, behind = onward(leaving[0]), back(leaving[1])
        if s == ring.half - 1:
            ahead = jnp.pad(ahead, ((0, tok_count - cut), (0, 0)))
            behind = jnp.pad(behind, ((cut, 0), (0, 0)))
        if s:
            mine, swapped = outputs(4 * s, 4)
            leaving = (
                add_up(ahead, mine[:tok_count], swapped[:tok_count]),
                add_up(behind, mine[tok_count:], swapped[tok_count:]),
            )
    mine, swapped = outputs(0, 2)
    return add_up(mine, swapped, ahead, behind)


def solution(mesh):
    placed = (
        P(("groups", "seq", "expert"), "tensor"),
        P(("groups", "seq", "expert"), None, "tensor"),
        P(("groups", "seq", "expert")),
        P(("groups", "seq", "expert"), None),
        P(("groups", "seq", "expert"), None),
        P(("seq", "expert"), None, "tensor", None),
        P(("seq", "expert"), "tensor", None),
    )

    def chosen(*args):
        seq_count, expert_count = mesh.shape["seq"], mesh.shape["expert"]
        owners = seq_count * expert_count
        tok_count, top_count = args[3].shape[0] // (mesh.shape["groups"] * owners), args[3].shape[1]
        experts_all = args[5].shape[0]
        slot_rows = experts_all * slot_capacity(tok_count, top_count, experts_all)
        dense = owners * tok_count <= 2 * slot_rows
        ring = dense and mesh.shape["tensor"] == 1 and expert_count == 4 and experts_all == owners
        body = ring_shards if ring else slot_shards
        return jax.shard_map(
            body,
            mesh=mesh,
            in_specs=placed,
            out_specs=P(("groups", "seq", "expert"), "tensor"),
            check_vma=False,
        )(*args)

    return chosen
```

```python
import functools

import jax
import jax.numpy as jnp
import numpy as np
from jax import lax
from jax.experimental import pallas as pl
from jax.experimental.pallas import tpu as pltpu
from jax.sharding import PartitionSpec as P

AXES = ("seq", "expert")


def slot_shards(
    text_tokens, panels, panel_target, expert_ids, gate_weights, gate_up_weight, down_weight
):
    seq_count = lax.axis_size("seq")
    expert_count = lax.axis_size("expert")
    owner_count = seq_count * expert_count
    pan_count = panels.shape[0]
    cap_panel = max(2, (3 * pan_count + 2 * seq_count - 1) // (2 * seq_count))
    slot_range = jnp.arange(pan_count, dtype=jnp.int32)
    owner_dev = panel_target // pan_count
    dest_seq = owner_dev // expert_count
    dest_slot = panel_target % pan_count
    onehot = (dest_seq[:, None] == jnp.arange(seq_count, dtype=jnp.int32)[None, :]).astype(
        jnp.int32
    )
    earlier = jnp.cumsum(onehot, axis=0) - onehot
    placing = dest_seq * cap_panel + jnp.sum(earlier * onehot, axis=1)
    outgoing = (
        jnp.zeros((seq_count * cap_panel,) + panels.shape[1:], panels.dtype).at[placing].set(panels)
    )
    labels = jnp.full((seq_count * cap_panel,), -1, jnp.int32).at[placing].set(dest_slot)
    arrived, arrived_labels = (
        lax.all_to_all(outgoing, "seq", split_axis=0, concat_axis=0, tiled=True),
        lax.all_to_all(labels, "seq", split_axis=0, concat_axis=0, tiled=True),
    )
    matches = (arrived_labels[None, :] == slot_range[:, None]).astype(jnp.bfloat16)
    image_rows = jnp.einsum(
        "qn,nrd->qrd", matches, arrived, preferred_element_type=jnp.float32
    ).astype(jnp.bfloat16)
    half_rows = jnp.concatenate([text_tokens, image_rows.reshape(-1, image_rows.shape[-1])], axis=0)
    tokens = lax.all_gather(half_rows, "tensor", axis=1, tiled=True)
    feature_width = tokens.shape[1]
    tok_count, top_count = expert_ids.shape
    experts_all = owner_count * gate_up_weight.shape[0]
    capacity = slot_capacity(tok_count, top_count, experts_all)
    flat_ids = expert_ids.reshape(-1)
    onehot_ids = (flat_ids[:, None] == jnp.arange(experts_all, dtype=jnp.int32)[None, :]).astype(
        jnp.int32
    )
    before = jnp.cumsum(onehot_ids, axis=0) - onehot_ids
    placing_ids = flat_ids * capacity + jnp.sum(before * onehot_ids, axis=1)
    source_rows = jnp.arange(tok_count * top_count, dtype=jnp.int32) // top_count
    outgoing_rows = (
        jnp.zeros((experts_all * capacity, feature_width), tokens.dtype)
        .at[placing_ids]
        .set(tokens[source_rows])
    )
    load_counts = jnp.sum(onehot_ids, axis=0).reshape(experts_all, 1)
    outgoing_rows = outgoing_rows.reshape(experts_all, capacity, feature_width)
    pair_weight = gate_up_weight[0]
    out_weight = down_weight[0]
    arrived_rows, arrived_loads = (
        lax.all_to_all(outgoing_rows, AXES, split_axis=0, concat_axis=0, tiled=True),
        lax.all_to_all(load_counts, AXES, split_axis=0, concat_axis=0, tiled=True),
    )
    arrived_rows = arrived_rows.reshape(-1, feature_width)
    slot_total = arrived_rows.shape[0]
    slot_index = jnp.arange(capacity, dtype=jnp.int32)
    is_live = (slot_index[None, :] < arrived_loads).reshape(-1)
    live_int = is_live.astype(jnp.int32)
    compact_at = jnp.cumsum(live_int) - live_int
    live_total = jnp.sum(live_int)
    compact_src = (
        jnp.zeros((slot_total,), jnp.int32)
        .at[jnp.where(is_live, compact_at, slot_total)]
        .set(jnp.arange(slot_total, dtype=jnp.int32), mode="drop")
    )

    def expert_block(block_no, partial_out):
        chosen = lax.dynamic_slice_in_dim(compact_src, block_no * 128, 128)
        block_rows = arrived_rows[chosen]
        gate_up = jnp.einsum(
            "rd,gfd->grf", block_rows, pair_weight, preferred_element_type=jnp.float32
        )
        hidden = (jax.nn.silu(gate_up[0]) * gate_up[1]).astype(jnp.bfloat16)
        result = jnp.dot(hidden, out_weight, preferred_element_type=jnp.float32)
        return lax.dynamic_update_slice_in_dim(partial_out, result, block_no * 128, 0)

    block_total = (live_total + 127) // 128
    padded_total = (slot_total + 127) // 128 * 128
    partial_out = lax.fori_loop(
        0, block_total, expert_block, jnp.zeros((padded_total, feature_width), jnp.float32)
    )
    summed = lax.psum_scatter(partial_out, "tensor", scatter_dimension=1, tiled=True).astype(
        jnp.bfloat16
    )
    out_width = summed.shape[1]
    returned = jnp.where(
        is_live[:, None], summed[jnp.where(is_live, compact_at, 0)], jnp.zeros((), jnp.bfloat16)
    )
    came_back = lax.all_to_all(
        returned.reshape(experts_all, capacity, out_width),
        AXES,
        split_axis=0,
        concat_axis=0,
        tiled=True,
    )
    half_width = came_back.shape[2]
    picked = came_back.reshape(-1, half_width)[placing_ids].reshape(
        tok_count, top_count, half_width
    )
    mixed_out = jnp.sum(gate_weights[:, :, None] * picked.astype(jnp.float32), axis=1)
    return mixed_out.astype(jnp.bfloat16)


def slot_capacity(tok_count, top_count, experts_all):
    return min(tok_count, (2 * tok_count * top_count // experts_all + 7) // 8 * 8)


class Ring:
    def __init__(self, seq_count, expert_count):
        self.seq, self.expert = seq_count, expert_count
        self.chips = 2 * seq_count
        self.half = seq_count
        self.devices = seq_count * expert_count
        self.slots = [(0, 0), (0, 1), (self.half, 0), (self.half, 1)]
        for s in range(1, self.half):
            self.slots += [(s, 0), (-s, 0), (s, 1), (-s, 1)]
        slot_of = {(r % self.chips, k): i for i, (r, k) in enumerate(self.slots)}
        self.owner_of = np.zeros((self.devices, len(self.slots)), np.int32)
        self.sources_of = np.zeros((self.devices, len(self.slots), seq_count), np.int32)
        for d in range(self.devices):
            p, c = self.place(d)
            for i, (r, k) in enumerate(self.slots):
                q = (p + r) % self.chips
                self.owner_of[d, i] = self.device(q, c ^ k)
                x = q // seq_count
                for z in range(seq_count):
                    pos = z if x == 0 else self.chips - 1 - z
                    self.sources_of[d, i, z] = slot_of[((pos - p) % self.chips, k)]

    def place(self, d):
        z, e = divmod(d, self.expert)
        x, c = divmod(e, 2)
        return (z if x == 0 else self.chips - 1 - z), c

    def device(self, pos, c):
        x, z = (0, pos) if pos < self.seq else (1, self.chips - 1 - pos)
        return z * self.expert + x * 2 + c

    def step(self, by):
        pairs = []
        for d in range(self.devices):
            p, c = self.place(d)
            pairs.append((d, self.device((p + by) % self.chips, c)))
        return pairs

    def swap(self):
        return [(d, d ^ 1) for d in range(self.devices)]


def pack_kernel(experts, expert_count, text_ref, panels_ref, target_ref, ids_ref, gates_ref, out_ref):
    text_rows, wide = text_ref.shape
    rows, width = out_ref.shape[0], out_ref.shape[1] - wide
    image_rows = rows - text_rows
    pan_count = target_ref.shape[1]
    panel_rows = image_rows // pan_count
    out_ref[:text_rows, :wide] = text_ref[...]
    out_ref[text_rows:, :wide] = panels_ref[...]
    lane = lax.broadcasted_iota(jnp.int32, (rows, width), 1)
    term = sum((lane >= i * experts).astype(jnp.int32) for i in range(1, 4))
    expert = lane - term * experts
    gate = jnp.zeros((rows, width), jnp.float32)
    for k in range(ids_ref.shape[1]):
        gate += jnp.where(ids_ref[:, k : k + 1] == expert, gates_ref[:, k : k + 1], 0.0)
    high = gate.astype(jnp.bfloat16).astype(jnp.float32)
    middle = (gate - high).astype(jnp.bfloat16).astype(jnp.float32)
    low = gate - high - middle
    panel = lax.broadcasted_iota(jnp.int32, (rows, pan_count), 1)
    row = lax.broadcasted_iota(jnp.int32, (rows, pan_count), 0) - text_rows
    past = row - panel * panel_rows
    mine = (past >= 0) & (past < panel_rows)
    target = jnp.sum(
        jnp.where(mine, target_ref[...].astype(jnp.float32), 0.0), axis=1, keepdims=True
    )
    within = jnp.sum(jnp.where(mine, past.astype(jnp.float32), 0.0), axis=1, keepdims=True)
    owner, seq = jnp.zeros_like(target), jnp.zeros_like(target)
    for i in range(1, experts):
        passed = jnp.where(target >= i * pan_count, 1.0, 0.0)
        owner += passed
        if i % expert_count == 0:
            seq += passed
    place = (target - owner * pan_count) * panel_rows + within
    tags = jnp.where(term == 0, high, jnp.where(term == 1, middle, jnp.where(term == 2, low, 0.0)))
    tags = jnp.where(lane == 3 * experts, seq, jnp.where(lane == 3 * experts + 1, place, tags))
    out_ref[:, wide:] = tags.astype(jnp.bfloat16)


def pack_call(text_tokens, panels, panel_target, expert_ids, gate_weights, experts, expert_count):
    rows, wide = expert_ids.shape[0], text_tokens.shape[1]
    width = (3 * experts + 2 + 127) // 128 * 128
    here = pl.BlockSpec(memory_space=pltpu.VMEM)
    return pl.pallas_call(
        functools.partial(pack_kernel, experts, expert_count),
        in_specs=[here] * 5,
        out_specs=here,
        out_shape=pltpu.VMEM((rows, wide + width), jnp.bfloat16),
        compiler_params=pltpu.CompilerParams(vmem_limit_bytes=14 * 1024 * 1024),
    )(text_tokens, panels.reshape(-1, wide), panel_target[None, :], expert_ids, gate_weights)


def hidden_kernel(count, rows, first_row, chunk, fetch, *refs):
    x_refs, refs = refs[:count], refs[count:]
    if fetch == "gate_up":
        far_ref, out_ref, w_ref, x_all, sems = refs
    elif fetch == "down":
        w_ref, _, far_ref, out_ref, _, down_ref, x_all, sems = refs
    else:
        w_ref, _, out_ref, x_all = refs[0], refs[1], refs[2], refs[-1]
    ff, wide = w_ref.shape[2:]
    whole, rest = divmod(ff, chunk)
    total = count * rows

    def fetched(i, width):
        part = pl.ds(pl.multiple_of(i * chunk, chunk), width)
        return pltpu.make_async_copy(far_ref.at[0, :, part], w_ref.at[0, :, part], sems.at[i])

    if fetch == "gate_up":
        for i in range(whole):
            fetched(i, chunk).start()
        if rest:
            fetched(whole, rest).start()
    if fetch == "down":
        pltpu.make_async_copy(far_ref, down_ref, sems.at[0]).start()
    for i in range(count):
        x_all[i * rows : (i + 1) * rows, :] = x_refs[i][:, :wide]
        at = first_row + i * rows
        out_ref[at : at + rows, ff:] = x_refs[i][:, wide:]

    def step(i, width):
        if fetch == "gate_up":
            fetched(i, width).wait()
        part = pl.ds(pl.multiple_of(i * chunk, chunk), width)
        weight = w_ref[0, :, part, :].reshape(2 * width, wide)
        both = lax.dot_general(
            x_all[...], weight, (((1,), (1,)), ((), ())), preferred_element_type=jnp.float32
        )
        gate, up = both[:, :width], both[:, width:]
        hidden = (gate / (1.0 + jnp.exp(-gate)) * up).astype(out_ref.dtype)
        out_ref[first_row : first_row + total, part] = hidden

    @pl.loop(0, whole)
    def _(i):
        step(i, chunk)

    if rest:
        step(whole, rest)
    if fetch == "down":
        pltpu.make_async_copy(far_ref, down_ref, sems.at[0]).wait()


def kept(array):
    return pltpu.with_memory_space_constraint(array, pltpu.VMEM)


def distant(array):
    return pltpu.with_memory_space_constraint(array, pltpu.HBM)


def hidden_call(blocks, gate_up_weight, hidden, first_row, all_rows, down_weight=None, last=False):
    rows, width = blocks[0].shape
    ff, wide = gate_up_weight.shape[2:]
    count = len(blocks)
    chunk = 256
    here, far = pl.BlockSpec(memory_space=pltpu.VMEM), pl.BlockSpec(memory_space=pltpu.HBM)
    args, in_specs = [kept(block) for block in blocks], [here] * count
    out_shape, aliases = [pltpu.VMEM((all_rows, ff + width - wide), jnp.bfloat16)], {}
    scratch = [pltpu.VMEM((count * rows, wide), jnp.bfloat16)]
    fetch = None
    if hidden is None:
        fetch = "gate_up"
        args, in_specs = args + [distant(gate_up_weight)], in_specs + [far]
        out_shape.append(pltpu.VMEM(gate_up_weight.shape, gate_up_weight.dtype))
        scratch.append(pltpu.SemaphoreType.DMA((pl.cdiv(ff, chunk),)))
    else:
        args, in_specs = args + [kept(gate_up_weight), kept(hidden)], in_specs + [here, here]
        aliases = {count + 1: 0}
        if not last:
            out_shape.append(pltpu.VMEM(gate_up_weight.shape, gate_up_weight.dtype))
            aliases[count] = 1
        if down_weight is not None:
            fetch = "down"
            args, in_specs = args + [distant(down_weight)], in_specs + [far]
            out_shape.append(pltpu.VMEM(down_weight.shape, down_weight.dtype))
            scratch.append(pltpu.SemaphoreType.DMA((1,)))
    return pl.pallas_call(
        functools.partial(hidden_kernel, count, rows, first_row, chunk, fetch),
        in_specs=in_specs,
        out_specs=[here] * len(out_shape),
        out_shape=out_shape,
        scratch_shapes=scratch,
        input_output_aliases=aliases,
        compiler_params=pltpu.CompilerParams(vmem_limit_bytes=14 * 1024 * 1024),
        cost_estimate=pl.CostEstimate(
            flops=4 * count * rows * wide * ff,
            bytes_accessed=4 * ff * wide + 2 * count * rows * (wide + ff),
            transcendentals=count * rows * ff,
        ),
    )(*args)


def down_kernel(
    slots, first_slot, rows, text_rows, seq_count, experts, chunk, places_ref, hidden_ref, w_ref,
    own_ref, other_ref, column, picked, scale,
):
    image_rows = rows - text_rows
    half = slots * rows // 2
    slot_total = hidden_ref.shape[0] // rows
    ff = w_ref.shape[1]
    width = hidden_ref.shape[1] - ff
    expert = places_ref[0]
    lane = lax.broadcasted_iota(jnp.int32, (1, width), 1)
    is_gate = (lane == expert) | (lane == expert + experts) | (lane == expert + 2 * experts)
    place_of = jnp.where(lane == 3 * experts, float(image_rows), 0.0)
    place_of = jnp.where(lane == 3 * experts + 1, 1.0, place_of)
    wanted = lax.broadcasted_iota(jnp.int32, (1, image_rows), 1)
    for j in range(slots):
        at = (first_slot + j) * rows
        picked[j * rows : j * rows + text_rows, :] = hidden_ref[at : at + text_rows, :ff]
        for z in range(seq_count):
            source = places_ref[1 + slot_total + (first_slot + j) * seq_count + z]
            start = pl.multiple_of(source * rows + text_rows, 16)
            column[z * image_rows : (z + 1) * image_rows, :] = hidden_ref[
                pl.ds(start, image_rows), :
            ]
        place = column[:, ff:].astype(jnp.float32) * place_of
        place = jnp.sum(place, axis=1, keepdims=True)
        first = places_ref[1 + first_slot + j] * image_rows
        match = jnp.where(place == (wanted + first).astype(jnp.float32), 1.0, 0.0)
        rows_here = lax.dot_general(
            match.astype(jnp.bfloat16),
            column[:, :ff],
            (((0,), (0,)), ((), ())),
            preferred_element_type=jnp.float32,
        )
        picked[j * rows + text_rows : (j + 1) * rows, :] = rows_here.astype(jnp.bfloat16)
        gates = jnp.where(is_gate, hidden_ref[at : at + rows, ff:].astype(jnp.float32), 0.0)
        scale[j * rows : (j + 1) * rows, :] = jnp.sum(gates, axis=1, keepdims=True)

    @pl.loop(0, w_ref.shape[2] // chunk)
    def _(i):
        part = pl.ds(pl.multiple_of(i * chunk, chunk), chunk)
        result = jnp.dot(picked[...], w_ref[0, :, part], preferred_element_type=jnp.float32)
        scaled = result.astype(jnp.bfloat16).astype(jnp.float32) * scale[...]
        scaled = scaled.astype(jnp.bfloat16)
        own_ref[:, part] = scaled[:half]
        other_ref[:, part] = scaled[half:]


def down_call(
    hidden, places, down_weight, first_slot, slots, rows, text_rows, seq_count, experts
):
    _, ff, wide = down_weight.shape
    half = slots * rows // 2
    here = pl.BlockSpec(memory_space=pltpu.VMEM)
    return pl.pallas_call(
        functools.partial(
            down_kernel, slots, first_slot, rows, text_rows, seq_count, experts, 512
        ),
        grid_spec=pltpu.PrefetchScalarGridSpec(
            num_scalar_prefetch=1,
            grid=(1,),
            in_specs=[here] * 2,
            out_specs=[here] * 2,
            scratch_shapes=[
                pltpu.VMEM((seq_count * (rows - text_rows), hidden.shape[1]), jnp.bfloat16),
                pltpu.VMEM((slots * rows, ff), jnp.bfloat16),
                pltpu.VMEM((slots * rows, 1), jnp.float32),
            ],
        ),
        out_shape=[pltpu.VMEM((half, wide), jnp.bfloat16)] * 2,
        compiler_params=pltpu.CompilerParams(vmem_limit_bytes=14 * 1024 * 1024),
        cost_estimate=pl.CostEstimate(
            flops=2 * slots * rows * wide * ff,
            bytes_accessed=2 * ff * wide + 2 * slots * rows * wide,
            transcendentals=0,
        ),
    )(places, kept(hidden), kept(down_weight))


def add_up(*parts):
    total = parts[0].astype(jnp.float32)
    for part in parts[1:]:
        total = total + part.astype(jnp.float32)
    return total.astype(jnp.bfloat16)


def ring_shards(
    text_tokens, panels, panel_target, expert_ids, gate_weights, gate_up_weight, down_weight
):
    seq_count, expert_count = lax.axis_size("seq"), lax.axis_size("expert")
    ring = Ring(seq_count, expert_count)
    pan_count, panel_rows, wide = panels.shape
    text_rows = text_tokens.shape[0]
    tok_count = expert_ids.shape[0]
    image_rows = pan_count * panel_rows
    slot_count = len(ring.slots)
    me = lax.axis_index(AXES)

    def onward(array):
        return lax.ppermute(array, AXES, ring.step(1))

    def back(array):
        return lax.ppermute(array, AXES, ring.step(-1))

    def across(array):
        return lax.ppermute(array, AXES, ring.swap())

    own = pack_call(
        text_tokens, panels, panel_target, expert_ids, gate_weights, ring.devices, expert_count
    )
    seq_of = ring.owner_of // expert_count
    numbers = np.arange(ring.devices, dtype=np.int32)[:, None]
    places = np.concatenate([numbers, seq_of, ring.sources_of.reshape(ring.devices, -1)], axis=1)
    places = jnp.asarray(places)[me]

    before, after = onward(own), back(own)
    other = across(own)
    own, places = lax.optimization_barrier((own, places))

    all_rows = slot_count * tok_count
    hidden, gate_up = hidden_call([own, other], gate_up_weight, None, 0, all_rows)
    hidden, before, after = lax.optimization_barrier((hidden, before, after))
    cut = tok_count // 2
    for s in range(1, ring.half):
        here = [after, before]
        there = [across(after), across(before)]
        if s + 1 == ring.half:
            before, after = before[:cut], after[cut:]
        before, after = onward(before), back(after)
        first_row = 4 * s * tok_count
        extra = down_weight if s == 1 else None
        hidden, gate_up, *down = hidden_call(
            here + there, gate_up, hidden, first_row, all_rows, extra
        )
        if down:
            (down_here,) = down
        hidden, before, after = lax.optimization_barrier((hidden, before, after))
    far = [before, after, across(before), across(after)]
    (hidden,) = hidden_call(far, gate_up, hidden, 2 * tok_count, all_rows, last=True)

    def outputs(first_slot, slots):
        mine, others = down_call(
            hidden, places, down_here, first_slot, slots, tok_count, text_rows, seq_count,
            ring.devices,
        )
        return mine, across(others)

    mine, swapped = outputs(2, 2)
    leaving = add_up(mine[:cut], swapped[:cut]), add_up(mine[cut:], swapped[cut:])
    for s in range(ring.half - 1, -1, -1):
        ahead, behind = onward(leaving[0]), back(leaving[1])
        if s == ring.half - 1:
            ahead = jnp.pad(ahead, ((0, tok_count - cut), (0, 0)))
            behind = jnp.pad(behind, ((cut, 0), (0, 0)))
        if s:
            mine, swapped = outputs(4 * s, 4)
            leaving = (
                add_up(ahead, mine[:tok_count], swapped[:tok_count]),
                add_up(behind, mine[tok_count:], swapped[tok_count:]),
            )
    mine, swapped = outputs(0, 2)
    return add_up(mine, swapped, ahead, behind)


def solution(mesh):
    placed = (
        P(("groups", "seq", "expert"), "tensor"),
        P(("groups", "seq", "expert"), None, "tensor"),
        P(("groups", "seq", "expert")),
        P(("groups", "seq", "expert"), None),
        P(("groups", "seq", "expert"), None),
        P(("seq", "expert"), None, "tensor", None),
        P(("seq", "expert"), "tensor", None),
    )

    def chosen(*args):
        seq_count, expert_count = mesh.shape["seq"], mesh.shape["expert"]
        owners = seq_count * expert_count
        tok_count, top_count = args[3].shape[0] // (mesh.shape["groups"] * owners), args[3].shape[1]
        experts_all = args[5].shape[0]
        slot_rows = experts_all * slot_capacity(tok_count, top_count, experts_all)
        dense = owners * tok_count <= 2 * slot_rows
        ring = dense and mesh.shape["tensor"] == 1 and expert_count == 4 and experts_all == owners
        body = ring_shards if ring else slot_shards
        return jax.shard_map(
            body,
            mesh=mesh,
            in_specs=placed,
            out_specs=P(("groups", "seq", "expert"), "tensor"),
            check_vma=False,
        )(*args)

    return chosen
```

```python
import functools

import jax
import jax.numpy as jnp
import numpy as np
from jax import lax
from jax.experimental import pallas as pl
from jax.experimental.pallas import tpu as pltpu
from jax.sharding import PartitionSpec as P

AXES = ("seq", "expert")


def slot_shards(
    text_tokens, panels, panel_target, expert_ids, gate_weights, gate_up_weight, down_weight
):
    seq_count = lax.axis_size("seq")
    expert_count = lax.axis_size("expert")
    owner_count = seq_count * expert_count
    pan_count = panels.shape[0]
    cap_panel = max(2, (3 * pan_count + 2 * seq_count - 1) // (2 * seq_count))
    slot_range = jnp.arange(pan_count, dtype=jnp.int32)
    owner_dev = panel_target // pan_count
    dest_seq = owner_dev // expert_count
    dest_slot = panel_target % pan_count
    onehot = (dest_seq[:, None] == jnp.arange(seq_count, dtype=jnp.int32)[None, :]).astype(
        jnp.int32
    )
    earlier = jnp.cumsum(onehot, axis=0) - onehot
    placing = dest_seq * cap_panel + jnp.sum(earlier * onehot, axis=1)
    outgoing = (
        jnp.zeros((seq_count * cap_panel,) + panels.shape[1:], panels.dtype).at[placing].set(panels)
    )
    labels = jnp.full((seq_count * cap_panel,), -1, jnp.int32).at[placing].set(dest_slot)
    arrived, arrived_labels = (
        lax.all_to_all(outgoing, "seq", split_axis=0, concat_axis=0, tiled=True),
        lax.all_to_all(labels, "seq", split_axis=0, concat_axis=0, tiled=True),
    )
    matches = (arrived_labels[None, :] == slot_range[:, None]).astype(jnp.bfloat16)
    image_rows = jnp.einsum(
        "qn,nrd->qrd", matches, arrived, preferred_element_type=jnp.float32
    ).astype(jnp.bfloat16)
    half_rows = jnp.concatenate([text_tokens, image_rows.reshape(-1, image_rows.shape[-1])], axis=0)
    tokens = lax.all_gather(half_rows, "tensor", axis=1, tiled=True)
    feature_width = tokens.shape[1]
    tok_count, top_count = expert_ids.shape
    experts_all = owner_count * gate_up_weight.shape[0]
    capacity = slot_capacity(tok_count, top_count, experts_all)
    flat_ids = expert_ids.reshape(-1)
    onehot_ids = (flat_ids[:, None] == jnp.arange(experts_all, dtype=jnp.int32)[None, :]).astype(
        jnp.int32
    )
    before = jnp.cumsum(onehot_ids, axis=0) - onehot_ids
    placing_ids = flat_ids * capacity + jnp.sum(before * onehot_ids, axis=1)
    source_rows = jnp.arange(tok_count * top_count, dtype=jnp.int32) // top_count
    outgoing_rows = (
        jnp.zeros((experts_all * capacity, feature_width), tokens.dtype)
        .at[placing_ids]
        .set(tokens[source_rows])
    )
    load_counts = jnp.sum(onehot_ids, axis=0).reshape(experts_all, 1)
    outgoing_rows = outgoing_rows.reshape(experts_all, capacity, feature_width)
    pair_weight = gate_up_weight[0]
    out_weight = down_weight[0]
    arrived_rows, arrived_loads = (
        lax.all_to_all(outgoing_rows, AXES, split_axis=0, concat_axis=0, tiled=True),
        lax.all_to_all(load_counts, AXES, split_axis=0, concat_axis=0, tiled=True),
    )
    arrived_rows = arrived_rows.reshape(-1, feature_width)
    slot_total = arrived_rows.shape[0]
    slot_index = jnp.arange(capacity, dtype=jnp.int32)
    is_live = (slot_index[None, :] < arrived_loads).reshape(-1)
    live_int = is_live.astype(jnp.int32)
    compact_at = jnp.cumsum(live_int) - live_int
    live_total = jnp.sum(live_int)
    compact_src = (
        jnp.zeros((slot_total,), jnp.int32)
        .at[jnp.where(is_live, compact_at, slot_total)]
        .set(jnp.arange(slot_total, dtype=jnp.int32), mode="drop")
    )

    def expert_block(block_no, partial_out):
        chosen = lax.dynamic_slice_in_dim(compact_src, block_no * 128, 128)
        block_rows = arrived_rows[chosen]
        gate_up = jnp.einsum(
            "rd,gfd->grf", block_rows, pair_weight, preferred_element_type=jnp.float32
        )
        hidden = (jax.nn.silu(gate_up[0]) * gate_up[1]).astype(jnp.bfloat16)
        result = jnp.dot(hidden, out_weight, preferred_element_type=jnp.float32)
        return lax.dynamic_update_slice_in_dim(partial_out, result, block_no * 128, 0)

    block_total = (live_total + 127) // 128
    padded_total = (slot_total + 127) // 128 * 128
    partial_out = lax.fori_loop(
        0, block_total, expert_block, jnp.zeros((padded_total, feature_width), jnp.float32)
    )
    summed = lax.psum_scatter(partial_out, "tensor", scatter_dimension=1, tiled=True).astype(
        jnp.bfloat16
    )
    out_width = summed.shape[1]
    returned = jnp.where(
        is_live[:, None], summed[jnp.where(is_live, compact_at, 0)], jnp.zeros((), jnp.bfloat16)
    )
    came_back = lax.all_to_all(
        returned.reshape(experts_all, capacity, out_width),
        AXES,
        split_axis=0,
        concat_axis=0,
        tiled=True,
    )
    half_width = came_back.shape[2]
    picked = came_back.reshape(-1, half_width)[placing_ids].reshape(
        tok_count, top_count, half_width
    )
    mixed_out = jnp.sum(gate_weights[:, :, None] * picked.astype(jnp.float32), axis=1)
    return mixed_out.astype(jnp.bfloat16)


def slot_capacity(tok_count, top_count, experts_all):
    return min(tok_count, (2 * tok_count * top_count // experts_all + 7) // 8 * 8)


class Ring:
    def __init__(self, seq_count, expert_count):
        self.seq, self.expert = seq_count, expert_count
        self.chips = 2 * seq_count
        self.half = seq_count
        self.devices = seq_count * expert_count
        self.slots = [(0, 0), (0, 1), (self.half, 0), (self.half, 1)]
        for s in range(1, self.half):
            self.slots += [(s, 0), (-s, 0), (s, 1), (-s, 1)]
        slot_of = {(r % self.chips, k): i for i, (r, k) in enumerate(self.slots)}
        self.owner_of = np.zeros((self.devices, len(self.slots)), np.int32)
        self.sources_of = np.zeros((self.devices, len(self.slots), seq_count), np.int32)
        for d in range(self.devices):
            p, c = self.place(d)
            for i, (r, k) in enumerate(self.slots):
                q = (p + r) % self.chips
                self.owner_of[d, i] = self.device(q, c ^ k)
                x = q // seq_count
                for z in range(seq_count):
                    pos = z if x == 0 else self.chips - 1 - z
                    self.sources_of[d, i, z] = slot_of[((pos - p) % self.chips, k)]

    def place(self, d):
        z, e = divmod(d, self.expert)
        x, c = divmod(e, 2)
        return (z if x == 0 else self.chips - 1 - z), c

    def device(self, pos, c):
        x, z = (0, pos) if pos < self.seq else (1, self.chips - 1 - pos)
        return z * self.expert + x * 2 + c

    def step(self, by):
        pairs = []
        for d in range(self.devices):
            p, c = self.place(d)
            pairs.append((d, self.device((p + by) % self.chips, c)))
        return pairs

    def swap(self):
        return [(d, d ^ 1) for d in range(self.devices)]


def kept(array):
    return pltpu.with_memory_space_constraint(array, pltpu.VMEM)


def distant(array):
    return pltpu.with_memory_space_constraint(array, pltpu.HBM)


def pack_kernel(
    experts, expert_count, text_ref, panels_ref, target_ref, ids_ref, gates_ref, out_ref, sems
):
    text_rows, wide = text_ref.shape
    rows, width = out_ref.shape[0], out_ref.shape[1] - wide
    pan_count = target_ref.shape[1]
    panel_rows = (rows - text_rows) // pan_count
    copies = [
        pltpu.make_async_copy(text_ref, out_ref.at[:text_rows, :wide], sems.at[0]),
        pltpu.make_async_copy(panels_ref, out_ref.at[text_rows:, :wide], sems.at[1]),
    ]
    for copy in copies:
        copy.start()
    lane = lax.broadcasted_iota(jnp.int32, (rows, width), 1)
    term = sum((lane >= i * experts).astype(jnp.int32) for i in range(1, 4))
    expert = (lane - term * experts).astype(jnp.float32)
    diagonal = lax.broadcasted_iota(jnp.int32, (rows, rows), 0) == lax.broadcasted_iota(
        jnp.int32, (rows, rows), 1
    )

    def upright(row):
        return jnp.sum(jnp.where(diagonal, row, 0.0), axis=1, keepdims=True)

    gate = jnp.zeros((rows, width), jnp.float32)
    for k in range(ids_ref.shape[0]):
        number = upright(ids_ref[k : k + 1, :].astype(jnp.float32))
        gate += jnp.where(number == expert, upright(gates_ref[k : k + 1, :]), 0.0)
    high = gate.astype(jnp.bfloat16).astype(jnp.float32)
    middle = (gate - high).astype(jnp.bfloat16).astype(jnp.float32)
    low = gate - high - middle
    panel = lax.broadcasted_iota(jnp.int32, (rows, pan_count), 1)
    row = lax.broadcasted_iota(jnp.int32, (rows, pan_count), 0) - text_rows
    past = row - panel * panel_rows
    mine = (past >= 0) & (past < panel_rows)
    target = jnp.sum(
        jnp.where(mine, target_ref[...].astype(jnp.float32), 0.0), axis=1, keepdims=True
    )
    within = jnp.sum(jnp.where(mine, past.astype(jnp.float32), 0.0), axis=1, keepdims=True)
    owner, seq = jnp.zeros_like(target), jnp.zeros_like(target)
    for i in range(1, experts):
        passed = jnp.where(target >= i * pan_count, 1.0, 0.0)
        owner += passed
        if i % expert_count == 0:
            seq += passed
    place = (target - owner * pan_count) * panel_rows + within
    tags = jnp.where(term == 0, high, jnp.where(term == 1, middle, jnp.where(term == 2, low, 0.0)))
    tags = jnp.where(lane == 3 * experts, seq, jnp.where(lane == 3 * experts + 1, place, tags))
    out_ref[:, wide:] = tags.astype(jnp.bfloat16)
    for copy in copies:
        copy.wait()


def pack_call(text_tokens, panels, panel_target, expert_ids, gate_weights, experts, expert_count):
    rows, wide = expert_ids.shape[0], text_tokens.shape[1]
    width = (3 * experts + 2 + 127) // 128 * 128
    here, far = pl.BlockSpec(memory_space=pltpu.VMEM), pl.BlockSpec(memory_space=pltpu.HBM)
    return pl.pallas_call(
        functools.partial(pack_kernel, experts, expert_count),
        in_specs=[far, far, here, here, here],
        out_specs=here,
        out_shape=pltpu.VMEM((rows, wide + width), jnp.bfloat16),
        scratch_shapes=[pltpu.SemaphoreType.DMA((2,))],
        compiler_params=pltpu.CompilerParams(vmem_limit_bytes=14 * 1024 * 1024),
    )(
        distant(text_tokens),
        distant(panels.reshape(-1, wide)),
        panel_target[None, :],
        expert_ids.T,
        gate_weights.T,
    )


def hidden_kernel(count, pieces, rows, first_row, chunk, fetch, *refs):
    x_refs, refs = refs[:count], refs[count:]
    if fetch == "gate_up":
        far_ref, out_ref, w_ref, x_all, sems = refs
    elif fetch == "down":
        w_ref, _, far_ref, out_ref, _, down_ref, x_all, sems = refs
    else:
        w_ref, _, out_ref, x_all = refs[0], refs[1], refs[2], refs[-1]
    ff, wide = w_ref.shape[2:]
    whole, rest = divmod(ff, chunk)
    total = len(pieces) * rows

    def fetched(i, width):
        part = pl.ds(pl.multiple_of(i * chunk, chunk), width)
        return pltpu.make_async_copy(far_ref.at[0, :, part], w_ref.at[0, :, part], sems.at[i])

    if fetch == "gate_up":
        for i in range(whole):
            fetched(i, chunk).start()
        if rest:
            fetched(whole, rest).start()
    if fetch == "down":
        pltpu.make_async_copy(far_ref, down_ref, sems.at[0]).start()
    for i, (block, start) in enumerate(pieces):
        x_all[i * rows : (i + 1) * rows, :] = x_refs[block][start : start + rows, :wide]
        at = first_row + i * rows
        out_ref[at : at + rows, ff:] = x_refs[block][start : start + rows, wide:]

    def step(i, width):
        if fetch == "gate_up":
            fetched(i, width).wait()
        part = pl.ds(pl.multiple_of(i * chunk, chunk), width)
        weight = w_ref[0, :, part, :].reshape(2 * width, wide)
        both = lax.dot_general(
            x_all[...], weight, (((1,), (1,)), ((), ())), preferred_element_type=jnp.float32
        )
        gate, up = both[:, :width], both[:, width:]
        hidden = (gate / (1.0 + jnp.exp(-gate)) * up).astype(out_ref.dtype)
        out_ref[first_row : first_row + total, part] = hidden

    @pl.loop(0, whole)
    def _(i):
        step(i, chunk)

    if rest:
        step(whole, rest)
    if fetch == "down":
        pltpu.make_async_copy(far_ref, down_ref, sems.at[0]).wait()


def hidden_call(
    blocks, pieces, rows, gate_up_weight, hidden, first_row, all_rows, down_weight=None, last=False
):
    width = blocks[0].shape[1]
    ff, wide = gate_up_weight.shape[2:]
    count = len(blocks)
    chunk = 256
    here, far = pl.BlockSpec(memory_space=pltpu.VMEM), pl.BlockSpec(memory_space=pltpu.HBM)
    args, in_specs = [kept(block) for block in blocks], [here] * count
    out_shape, aliases = [pltpu.VMEM((all_rows, ff + width - wide), jnp.bfloat16)], {}
    scratch = [pltpu.VMEM((len(pieces) * rows, wide), jnp.bfloat16)]
    fetch = None
    if hidden is None:
        fetch = "gate_up"
        args, in_specs = args + [distant(gate_up_weight)], in_specs + [far]
        out_shape.append(pltpu.VMEM(gate_up_weight.shape, gate_up_weight.dtype))
        scratch.append(pltpu.SemaphoreType.DMA((pl.cdiv(ff, chunk),)))
    else:
        args, in_specs = args + [kept(gate_up_weight), kept(hidden)], in_specs + [here, here]
        aliases = {count + 1: 0}
        if not last:
            out_shape.append(pltpu.VMEM(gate_up_weight.shape, gate_up_weight.dtype))
            aliases[count] = 1
        if down_weight is not None:
            fetch = "down"
            args, in_specs = args + [distant(down_weight)], in_specs + [far]
            out_shape.append(pltpu.VMEM(down_weight.shape, down_weight.dtype))
            scratch.append(pltpu.SemaphoreType.DMA((1,)))
    return pl.pallas_call(
        functools.partial(hidden_kernel, count, pieces, rows, first_row, chunk, fetch),
        in_specs=in_specs,
        out_specs=[here] * len(out_shape),
        out_shape=out_shape,
        scratch_shapes=scratch,
        input_output_aliases=aliases,
        compiler_params=pltpu.CompilerParams(vmem_limit_bytes=14 * 1024 * 1024),
        cost_estimate=pl.CostEstimate(
            flops=4 * len(pieces) * rows * wide * ff,
            bytes_accessed=4 * ff * wide + 2 * len(pieces) * rows * (wide + ff),
            transcendentals=len(pieces) * rows * ff,
        ),
    )(*args)


def down_kernel(
    slots, first_slot, rows, text_rows, seq_count, experts, chunk, places_ref, hidden_ref, w_ref,
    own_ref, other_ref, column, picked, scale,
):
    image_rows = rows - text_rows
    half = slots * rows // 2
    slot_total = hidden_ref.shape[0] // rows
    ff = w_ref.shape[1]
    width = hidden_ref.shape[1] - ff
    expert = places_ref[0]
    lane = lax.broadcasted_iota(jnp.int32, (1, width), 1)
    is_gate = (lane == expert) | (lane == expert + experts) | (lane == expert + 2 * experts)
    place_of = jnp.where(lane == 3 * experts, float(image_rows), 0.0)
    place_of = jnp.where(lane == 3 * experts + 1, 1.0, place_of)
    wanted = lax.broadcasted_iota(jnp.int32, (1, image_rows), 1)
    for j in range(slots):
        at = (first_slot + j) * rows
        picked[j * rows : j * rows + text_rows, :] = hidden_ref[at : at + text_rows, :ff]
        for z in range(seq_count):
            source = places_ref[1 + slot_total + (first_slot + j) * seq_count + z]
            start = pl.multiple_of(source * rows + text_rows, 16)
            column[z * image_rows : (z + 1) * image_rows, :] = hidden_ref[
                pl.ds(start, image_rows), :
            ]
        place = column[:, ff:].astype(jnp.float32) * place_of
        place = jnp.sum(place, axis=1, keepdims=True)
        first = places_ref[1 + first_slot + j] * image_rows
        match = jnp.where(place == (wanted + first).astype(jnp.float32), 1.0, 0.0)
        rows_here = lax.dot_general(
            match.astype(jnp.bfloat16),
            column[:, :ff],
            (((0,), (0,)), ((), ())),
            preferred_element_type=jnp.float32,
        )
        picked[j * rows + text_rows : (j + 1) * rows, :] = rows_here.astype(jnp.bfloat16)
        gates = jnp.where(is_gate, hidden_ref[at : at + rows, ff:].astype(jnp.float32), 0.0)
        scale[j * rows : (j + 1) * rows, :] = jnp.sum(gates, axis=1, keepdims=True)

    @pl.loop(0, w_ref.shape[2] // chunk)
    def _(i):
        part = pl.ds(pl.multiple_of(i * chunk, chunk), chunk)
        result = jnp.dot(picked[...], w_ref[0, :, part], preferred_element_type=jnp.float32)
        scaled = result.astype(jnp.bfloat16).astype(jnp.float32) * scale[...]
        scaled = scaled.astype(jnp.bfloat16)
        own_ref[:, part] = scaled[:half]
        other_ref[:, part] = scaled[half:]


def down_call(
    hidden, places, down_weight, first_slot, slots, rows, text_rows, seq_count, experts
):
    _, ff, wide = down_weight.shape
    half = slots * rows // 2
    here = pl.BlockSpec(memory_space=pltpu.VMEM)
    return pl.pallas_call(
        functools.partial(
            down_kernel, slots, first_slot, rows, text_rows, seq_count, experts, 512
        ),
        grid_spec=pltpu.PrefetchScalarGridSpec(
            num_scalar_prefetch=1,
            grid=(1,),
            in_specs=[here] * 2,
            out_specs=[here] * 2,
            scratch_shapes=[
                pltpu.VMEM((seq_count * (rows - text_rows), hidden.shape[1]), jnp.bfloat16),
                pltpu.VMEM((slots * rows, ff), jnp.bfloat16),
                pltpu.VMEM((slots * rows, 1), jnp.float32),
            ],
        ),
        out_shape=[pltpu.VMEM((half, wide), jnp.bfloat16)] * 2,
        compiler_params=pltpu.CompilerParams(vmem_limit_bytes=14 * 1024 * 1024),
        cost_estimate=pl.CostEstimate(
            flops=2 * slots * rows * wide * ff,
            bytes_accessed=2 * ff * wide + 2 * slots * rows * wide,
            transcendentals=0,
        ),
    )(places, kept(hidden), kept(down_weight))


def add_up(*parts):
    total = parts[0].astype(jnp.float32)
    for part in parts[1:]:
        total = total + part.astype(jnp.float32)
    return total.astype(jnp.bfloat16)


def ring_shards(
    text_tokens, panels, panel_target, expert_ids, gate_weights, gate_up_weight, down_weight
):
    seq_count, expert_count = lax.axis_size("seq"), lax.axis_size("expert")
    ring = Ring(seq_count, expert_count)
    text_rows, tok_count = text_tokens.shape[0], expert_ids.shape[0]
    me = lax.axis_index(AXES)

    def onward(array):
        return lax.ppermute(array, AXES, ring.step(1))

    def back(array):
        return lax.ppermute(array, AXES, ring.step(-1))

    def across(array):
        return lax.ppermute(array, AXES, ring.swap())

    own = pack_call(
        text_tokens, panels, panel_target, expert_ids, gate_weights, ring.devices, expert_count
    )
    seq_of = ring.owner_of // expert_count
    numbers = np.arange(ring.devices, dtype=np.int32)[:, None]
    places = np.concatenate([numbers, seq_of, ring.sources_of.reshape(ring.devices, -1)], axis=1)
    places = jnp.asarray(places)[me]

    before, after = onward(own), back(own)
    other = across(own)
    own, places = lax.optimization_barrier((own, places))

    all_rows = len(ring.slots) * tok_count

    def whole(blocks):
        return [(i, 0) for i in range(len(blocks))]

    blocks = [own, other]
    hidden, gate_up = hidden_call(
        blocks, whole(blocks), tok_count, gate_up_weight, None, 0, all_rows
    )
    hidden, before = lax.optimization_barrier((hidden, before))
    hidden, after = lax.optimization_barrier((hidden, after))
    cut = tok_count // 2
    for s in range(1, ring.half):
        here = [after, before]
        there = [across(after), across(before)]
        if s + 1 == ring.half:
            before, after = before[:cut], after[cut:]
        before, after = onward(before), back(after)
        first_row = 4 * s * tok_count
        extra = down_weight if s == 1 else None
        blocks = here + there
        hidden, gate_up, *down = hidden_call(
            blocks, whole(blocks), tok_count, gate_up, hidden, first_row, all_rows, extra
        )
        if down:
            (down_here,) = down
        hidden, before = lax.optimization_barrier((hidden, before))
        hidden, after = lax.optimization_barrier((hidden, after))
    far = [before, after, across(before), across(after)]
    first_row = 2 * tok_count
    (hidden,) = hidden_call(
        far, whole(far), cut, gate_up, hidden, first_row, all_rows, last=True
    )

    def outputs(first_slot, slots):
        mine, others = down_call(
            hidden, places, down_here, first_slot, slots, tok_count, text_rows, seq_count,
            ring.devices,
        )
        return mine, across(others)

    mine, swapped = outputs(2, 2)
    leaving = add_up(mine[:cut], swapped[:cut]), add_up(mine[cut:], swapped[cut:])
    for s in range(ring.half - 1, -1, -1):
        ahead, behind = onward(leaving[0]), back(leaving[1])
        if s == ring.half - 1:
            ahead = jnp.pad(ahead, ((0, tok_count - cut), (0, 0)))
            behind = jnp.pad(behind, ((cut, 0), (0, 0)))
        if s:
            mine, swapped = outputs(4 * s, 4)
            leaving = (
                add_up(ahead, mine[:tok_count], swapped[:tok_count]),
                add_up(behind, mine[tok_count:], swapped[tok_count:]),
            )
    mine, swapped = outputs(0, 2)
    return add_up(mine, swapped, ahead, behind)


def solution(mesh):
    placed = (
        P(("groups", "seq", "expert"), "tensor"),
        P(("groups", "seq", "expert"), None, "tensor"),
        P(("groups", "seq", "expert")),
        P(("groups", "seq", "expert"), None),
        P(("groups", "seq", "expert"), None),
        P(("seq", "expert"), None, "tensor", None),
        P(("seq", "expert"), "tensor", None),
    )

    def chosen(*args):
        seq_count, expert_count = mesh.shape["seq"], mesh.shape["expert"]
        owners = seq_count * expert_count
        tok_count, top_count = args[3].shape[0] // (mesh.shape["groups"] * owners), args[3].shape[1]
        experts_all = args[5].shape[0]
        slot_rows = experts_all * slot_capacity(tok_count, top_count, experts_all)
        dense = owners * tok_count <= 2 * slot_rows
        ring = dense and mesh.shape["tensor"] == 1 and expert_count == 4 and experts_all == owners
        ring = ring and seq_count > 2
        body = ring_shards if ring else slot_shards
        return jax.shard_map(
            body,
            mesh=mesh,
            in_specs=placed,
            out_specs=P(("groups", "seq", "expert"), "tensor"),
            check_vma=False,
        )(*args)

    return chosen
```

```python
import functools

import jax
import jax.numpy as jnp
import numpy as np
from jax import lax
from jax.experimental import pallas as pl
from jax.experimental.pallas import tpu as pltpu
from jax.sharding import PartitionSpec as P

AXES = ("seq", "expert")


def slot_shards(
    text_tokens, panels, panel_target, expert_ids, gate_weights, gate_up_weight, down_weight
):
    seq_count = lax.axis_size("seq")
    expert_count = lax.axis_size("expert")
    owner_count = seq_count * expert_count
    pan_count = panels.shape[0]
    cap_panel = max(2, (3 * pan_count + 2 * seq_count - 1) // (2 * seq_count))
    slot_range = jnp.arange(pan_count, dtype=jnp.int32)
    owner_dev = panel_target // pan_count
    dest_seq = owner_dev // expert_count
    dest_slot = panel_target % pan_count
    onehot = (dest_seq[:, None] == jnp.arange(seq_count, dtype=jnp.int32)[None, :]).astype(
        jnp.int32
    )
    earlier = jnp.cumsum(onehot, axis=0) - onehot
    placing = dest_seq * cap_panel + jnp.sum(earlier * onehot, axis=1)
    outgoing = (
        jnp.zeros((seq_count * cap_panel,) + panels.shape[1:], panels.dtype).at[placing].set(panels)
    )
    labels = jnp.full((seq_count * cap_panel,), -1, jnp.int32).at[placing].set(dest_slot)
    arrived, arrived_labels = (
        lax.all_to_all(outgoing, "seq", split_axis=0, concat_axis=0, tiled=True),
        lax.all_to_all(labels, "seq", split_axis=0, concat_axis=0, tiled=True),
    )
    matches = (arrived_labels[None, :] == slot_range[:, None]).astype(jnp.bfloat16)
    image_rows = jnp.einsum(
        "qn,nrd->qrd", matches, arrived, preferred_element_type=jnp.float32
    ).astype(jnp.bfloat16)
    half_rows = jnp.concatenate([text_tokens, image_rows.reshape(-1, image_rows.shape[-1])], axis=0)
    tokens = lax.all_gather(half_rows, "tensor", axis=1, tiled=True)
    feature_width = tokens.shape[1]
    tok_count, top_count = expert_ids.shape
    experts_all = owner_count * gate_up_weight.shape[0]
    capacity = slot_capacity(tok_count, top_count, experts_all)
    flat_ids = expert_ids.reshape(-1)
    onehot_ids = (flat_ids[:, None] == jnp.arange(experts_all, dtype=jnp.int32)[None, :]).astype(
        jnp.int32
    )
    before = jnp.cumsum(onehot_ids, axis=0) - onehot_ids
    placing_ids = flat_ids * capacity + jnp.sum(before * onehot_ids, axis=1)
    source_rows = jnp.arange(tok_count * top_count, dtype=jnp.int32) // top_count
    outgoing_rows = (
        jnp.zeros((experts_all * capacity, feature_width), tokens.dtype)
        .at[placing_ids]
        .set(tokens[source_rows])
    )
    load_counts = jnp.sum(onehot_ids, axis=0).reshape(experts_all, 1)
    outgoing_rows = outgoing_rows.reshape(experts_all, capacity, feature_width)
    pair_weight = gate_up_weight[0]
    out_weight = down_weight[0]
    arrived_rows, arrived_loads = (
        lax.all_to_all(outgoing_rows, AXES, split_axis=0, concat_axis=0, tiled=True),
        lax.all_to_all(load_counts, AXES, split_axis=0, concat_axis=0, tiled=True),
    )
    arrived_rows = arrived_rows.reshape(-1, feature_width)
    slot_total = arrived_rows.shape[0]
    slot_index = jnp.arange(capacity, dtype=jnp.int32)
    is_live = (slot_index[None, :] < arrived_loads).reshape(-1)
    live_int = is_live.astype(jnp.int32)
    compact_at = jnp.cumsum(live_int) - live_int
    live_total = jnp.sum(live_int)
    compact_src = (
        jnp.zeros((slot_total,), jnp.int32)
        .at[jnp.where(is_live, compact_at, slot_total)]
        .set(jnp.arange(slot_total, dtype=jnp.int32), mode="drop")
    )

    def expert_block(block_no, partial_out):
        chosen = lax.dynamic_slice_in_dim(compact_src, block_no * 128, 128)
        block_rows = arrived_rows[chosen]
        gate_up = jnp.einsum(
            "rd,gfd->grf", block_rows, pair_weight, preferred_element_type=jnp.float32
        )
        hidden = (jax.nn.silu(gate_up[0]) * gate_up[1]).astype(jnp.bfloat16)
        result = jnp.dot(hidden, out_weight, preferred_element_type=jnp.float32)
        return lax.dynamic_update_slice_in_dim(partial_out, result, block_no * 128, 0)

    block_total = (live_total + 127) // 128
    padded_total = (slot_total + 127) // 128 * 128
    partial_out = lax.fori_loop(
        0, block_total, expert_block, jnp.zeros((padded_total, feature_width), jnp.float32)
    )
    summed = lax.psum_scatter(partial_out, "tensor", scatter_dimension=1, tiled=True).astype(
        jnp.bfloat16
    )
    out_width = summed.shape[1]
    returned = jnp.where(
        is_live[:, None], summed[jnp.where(is_live, compact_at, 0)], jnp.zeros((), jnp.bfloat16)
    )
    came_back = lax.all_to_all(
        returned.reshape(experts_all, capacity, out_width),
        AXES,
        split_axis=0,
        concat_axis=0,
        tiled=True,
    )
    half_width = came_back.shape[2]
    picked = came_back.reshape(-1, half_width)[placing_ids].reshape(
        tok_count, top_count, half_width
    )
    mixed_out = jnp.sum(gate_weights[:, :, None] * picked.astype(jnp.float32), axis=1)
    return mixed_out.astype(jnp.bfloat16)


def slot_capacity(tok_count, top_count, experts_all):
    return min(tok_count, (2 * tok_count * top_count // experts_all + 7) // 8 * 8)


class Ring:
    def __init__(self, seq_count, expert_count):
        self.seq, self.expert = seq_count, expert_count
        self.chips = 2 * seq_count
        self.half = seq_count
        self.devices = seq_count * expert_count
        self.slots = [(0, 0), (0, 1), (self.half, 0), (self.half, 1)]
        for s in range(1, self.half):
            self.slots += [(s, 0), (-s, 0), (s, 1), (-s, 1)]
        slot_of = {(r % self.chips, k): i for i, (r, k) in enumerate(self.slots)}
        self.owner_of = np.zeros((self.devices, len(self.slots)), np.int32)
        self.sources_of = np.zeros((self.devices, len(self.slots), seq_count), np.int32)
        for d in range(self.devices):
            p, c = self.place(d)
            for i, (r, k) in enumerate(self.slots):
                q = (p + r) % self.chips
                self.owner_of[d, i] = self.device(q, c ^ k)
                x = q // seq_count
                for z in range(seq_count):
                    pos = z if x == 0 else self.chips - 1 - z
                    self.sources_of[d, i, z] = slot_of[((pos - p) % self.chips, k)]

    def place(self, d):
        z, e = divmod(d, self.expert)
        x, c = divmod(e, 2)
        return (z if x == 0 else self.chips - 1 - z), c

    def device(self, pos, c):
        x, z = (0, pos) if pos < self.seq else (1, self.chips - 1 - pos)
        return z * self.expert + x * 2 + c

    def step(self, by):
        pairs = []
        for d in range(self.devices):
            p, c = self.place(d)
            pairs.append((d, self.device((p + by) % self.chips, c)))
        return pairs

    def swap(self):
        return [(d, d ^ 1) for d in range(self.devices)]


def kept(array):
    return pltpu.with_memory_space_constraint(array, pltpu.VMEM)


def distant(array):
    return pltpu.with_memory_space_constraint(array, pltpu.HBM)


def pack_kernel(
    experts, expert_count, text_ref, panels_ref, target_ref, ids_ref, gates_ref, out_ref, sems
):
    text_rows, wide = text_ref.shape
    rows, width = out_ref.shape[0], out_ref.shape[1] - wide
    pan_count = target_ref.shape[1]
    panel_rows = (rows - text_rows) // pan_count
    copies = [
        pltpu.make_async_copy(text_ref, out_ref.at[:text_rows, :wide], sems.at[0]),
        pltpu.make_async_copy(panels_ref, out_ref.at[text_rows:, :wide], sems.at[1]),
    ]
    for copy in copies:
        copy.start()
    lane = lax.broadcasted_iota(jnp.int32, (rows, width), 1)
    term = sum((lane >= i * experts).astype(jnp.int32) for i in range(1, 4))
    expert = (lane - term * experts).astype(jnp.float32)
    diagonal = lax.broadcasted_iota(jnp.int32, (rows, rows), 0) == lax.broadcasted_iota(
        jnp.int32, (rows, rows), 1
    )

    def upright(row):
        return jnp.sum(jnp.where(diagonal, row, 0.0), axis=1, keepdims=True)

    gate = jnp.zeros((rows, width), jnp.float32)
    for k in range(ids_ref.shape[0]):
        number = upright(ids_ref[k : k + 1, :].astype(jnp.float32))
        gate += jnp.where(number == expert, upright(gates_ref[k : k + 1, :]), 0.0)
    high = gate.astype(jnp.bfloat16).astype(jnp.float32)
    middle = (gate - high).astype(jnp.bfloat16).astype(jnp.float32)
    low = gate - high - middle
    panel = lax.broadcasted_iota(jnp.int32, (rows, pan_count), 1)
    row = lax.broadcasted_iota(jnp.int32, (rows, pan_count), 0) - text_rows
    past = row - panel * panel_rows
    mine = (past >= 0) & (past < panel_rows)
    target = jnp.sum(
        jnp.where(mine, target_ref[...].astype(jnp.float32), 0.0), axis=1, keepdims=True
    )
    within = jnp.sum(jnp.where(mine, past.astype(jnp.float32), 0.0), axis=1, keepdims=True)
    owner, seq = jnp.zeros_like(target), jnp.zeros_like(target)
    for i in range(1, experts):
        passed = jnp.where(target >= i * pan_count, 1.0, 0.0)
        owner += passed
        if i % expert_count == 0:
            seq += passed
    place = (target - owner * pan_count) * panel_rows + within
    tags = jnp.where(term == 0, high, jnp.where(term == 1, middle, jnp.where(term == 2, low, 0.0)))
    tags = jnp.where(lane == 3 * experts, seq, jnp.where(lane == 3 * experts + 1, place, tags))
    out_ref[:, wide:] = tags.astype(jnp.bfloat16)
    for copy in copies:
        copy.wait()


def pack_call(text_tokens, panels, panel_target, expert_ids, gate_weights, experts, expert_count):
    rows, wide = expert_ids.shape[0], text_tokens.shape[1]
    width = (3 * experts + 2 + 127) // 128 * 128
    here, far = pl.BlockSpec(memory_space=pltpu.VMEM), pl.BlockSpec(memory_space=pltpu.HBM)
    return pl.pallas_call(
        functools.partial(pack_kernel, experts, expert_count),
        in_specs=[far, far, here, here, here],
        out_specs=here,
        out_shape=pltpu.VMEM((rows, wide + width), jnp.bfloat16),
        scratch_shapes=[pltpu.SemaphoreType.DMA((2,))],
        compiler_params=pltpu.CompilerParams(vmem_limit_bytes=14 * 1024 * 1024),
    )(
        distant(text_tokens),
        distant(panels.reshape(-1, wide)),
        panel_target[None, :],
        expert_ids.T,
        gate_weights.T,
    )


def hidden_kernel(count, pieces, rows, first_row, chunk, fetch, *refs):
    x_refs, refs = refs[:count], refs[count:]
    if fetch == "gate_up":
        far_ref, out_ref, w_ref, x_all, sems = refs
    elif fetch == "down":
        w_ref, _, far_ref, out_ref, _, down_ref, x_all, sems = refs
    else:
        w_ref, _, out_ref, x_all = refs[0], refs[1], refs[2], refs[-1]
    ff, wide = w_ref.shape[2:]
    whole, rest = divmod(ff, chunk)
    total = len(pieces) * rows

    def fetched(i, width):
        part = pl.ds(pl.multiple_of(i * chunk, chunk), width)
        return pltpu.make_async_copy(far_ref.at[0, :, part], w_ref.at[0, :, part], sems.at[i])

    if fetch == "gate_up":
        for i in range(whole):
            fetched(i, chunk).start()
        if rest:
            fetched(whole, rest).start()
    if fetch == "down":
        pltpu.make_async_copy(far_ref, down_ref, sems.at[0]).start()
    for i, (block, start) in enumerate(pieces):
        x_all[i * rows : (i + 1) * rows, :] = x_refs[block][start : start + rows, :wide]
        at = first_row + i * rows
        out_ref[at : at + rows, ff:] = x_refs[block][start : start + rows, wide:]

    def step(i, width):
        if fetch == "gate_up":
            fetched(i, width).wait()
        part = pl.ds(pl.multiple_of(i * chunk, chunk), width)
        weight = w_ref[0, :, part, :].reshape(2 * width, wide)
        both = lax.dot_general(
            x_all[...], weight, (((1,), (1,)), ((), ())), preferred_element_type=jnp.float32
        )
        gate, up = both[:, :width], both[:, width:]
        hidden = (gate / (1.0 + jnp.exp(-gate)) * up).astype(out_ref.dtype)
        out_ref[first_row : first_row + total, part] = hidden

    @pl.loop(0, whole)
    def _(i):
        step(i, chunk)

    if rest:
        step(whole, rest)
    if fetch == "down":
        pltpu.make_async_copy(far_ref, down_ref, sems.at[0]).wait()


def hidden_call(
    blocks, pieces, rows, gate_up_weight, hidden, first_row, all_rows, down_weight=None, last=False
):
    width = blocks[0].shape[1]
    ff, wide = gate_up_weight.shape[2:]
    count = len(blocks)
    chunk = 256
    here, far = pl.BlockSpec(memory_space=pltpu.VMEM), pl.BlockSpec(memory_space=pltpu.HBM)
    args, in_specs = [kept(block) for block in blocks], [here] * count
    out_shape, aliases = [pltpu.VMEM((all_rows, ff + width - wide), jnp.bfloat16)], {}
    scratch = [pltpu.VMEM((len(pieces) * rows, wide), jnp.bfloat16)]
    fetch = None
    if hidden is None:
        fetch = "gate_up"
        args, in_specs = args + [distant(gate_up_weight)], in_specs + [far]
        out_shape.append(pltpu.VMEM(gate_up_weight.shape, gate_up_weight.dtype))
        scratch.append(pltpu.SemaphoreType.DMA((pl.cdiv(ff, chunk),)))
    else:
        args, in_specs = args + [kept(gate_up_weight), kept(hidden)], in_specs + [here, here]
        aliases = {count + 1: 0}
        if not last:
            out_shape.append(pltpu.VMEM(gate_up_weight.shape, gate_up_weight.dtype))
            aliases[count] = 1
        if down_weight is not None:
            fetch = "down"
            args, in_specs = args + [distant(down_weight)], in_specs + [far]
            out_shape.append(pltpu.VMEM(down_weight.shape, down_weight.dtype))
            scratch.append(pltpu.SemaphoreType.DMA((1,)))
    return pl.pallas_call(
        functools.partial(hidden_kernel, count, pieces, rows, first_row, chunk, fetch),
        in_specs=in_specs,
        out_specs=[here] * len(out_shape),
        out_shape=out_shape,
        scratch_shapes=scratch,
        input_output_aliases=aliases,
        compiler_params=pltpu.CompilerParams(vmem_limit_bytes=14 * 1024 * 1024),
        cost_estimate=pl.CostEstimate(
            flops=4 * len(pieces) * rows * wide * ff,
            bytes_accessed=4 * ff * wide + 2 * len(pieces) * rows * (wide + ff),
            transcendentals=len(pieces) * rows * ff,
        ),
    )(*args)


def down_kernel(
    groups, rows, text_rows, seq_count, experts, chunk, places_ref, hidden_ref, w_ref, *refs
):
    out_refs, (column, picked, scale) = refs[:-3], refs[-3:]
    slots = [slot for group in groups for slot in group]
    image_rows = rows - text_rows
    slot_total = hidden_ref.shape[0] // rows
    ff = w_ref.shape[1]
    width = hidden_ref.shape[1] - ff
    expert = places_ref[0]
    lane = lax.broadcasted_iota(jnp.int32, (1, width), 1)
    is_gate = (lane == expert) | (lane == expert + experts) | (lane == expert + 2 * experts)
    place_of = jnp.where(lane == 3 * experts, float(image_rows), 0.0)
    place_of = jnp.where(lane == 3 * experts + 1, 1.0, place_of)
    wanted = lax.broadcasted_iota(jnp.int32, (1, image_rows), 1)
    for j, slot in enumerate(slots):
        at = slot * rows
        picked[j * rows : j * rows + text_rows, :] = hidden_ref[at : at + text_rows, :ff]
        for z in range(seq_count):
            source = places_ref[1 + slot_total + slot * seq_count + z]
            start = pl.multiple_of(source * rows + text_rows, 16)
            column[z * image_rows : (z + 1) * image_rows, :] = hidden_ref[
                pl.ds(start, image_rows), :
            ]
        place = column[:, ff:].astype(jnp.float32) * place_of
        place = jnp.sum(place, axis=1, keepdims=True)
        first = places_ref[1 + slot] * image_rows
        match = jnp.where(place == (wanted + first).astype(jnp.float32), 1.0, 0.0)
        rows_here = lax.dot_general(
            match.astype(jnp.bfloat16),
            column[:, :ff],
            (((0,), (0,)), ((), ())),
            preferred_element_type=jnp.float32,
        )
        picked[j * rows + text_rows : (j + 1) * rows, :] = rows_here.astype(jnp.bfloat16)
        gates = jnp.where(is_gate, hidden_ref[at : at + rows, ff:].astype(jnp.float32), 0.0)
        scale[j * rows : (j + 1) * rows, :] = jnp.sum(gates, axis=1, keepdims=True)

    @pl.loop(0, w_ref.shape[2] // chunk)
    def _(i):
        part = pl.ds(pl.multiple_of(i * chunk, chunk), chunk)
        result = jnp.dot(picked[...], w_ref[0, :, part], preferred_element_type=jnp.float32)
        scaled = result.astype(jnp.bfloat16).astype(jnp.float32) * scale[...]
        scaled = scaled.astype(jnp.bfloat16)
        start = 0
        for out_ref in out_refs:
            out_ref[:, part] = scaled[start : start + out_ref.shape[0]]
            start += out_ref.shape[0]


def down_call(hidden, places, down_weight, groups, rows, text_rows, seq_count, experts):
    _, ff, wide = down_weight.shape
    total = sum(len(group) for group in groups) * rows
    here = pl.BlockSpec(memory_space=pltpu.VMEM)
    return pl.pallas_call(
        functools.partial(down_kernel, groups, rows, text_rows, seq_count, experts, 512),
        grid_spec=pltpu.PrefetchScalarGridSpec(
            num_scalar_prefetch=1,
            grid=(1,),
            in_specs=[here] * 2,
            out_specs=[here] * len(groups),
            scratch_shapes=[
                pltpu.VMEM((seq_count * (rows - text_rows), hidden.shape[1]), jnp.bfloat16),
                pltpu.VMEM((total, ff), jnp.bfloat16),
                pltpu.VMEM((total, 1), jnp.float32),
            ],
        ),
        out_shape=[pltpu.VMEM((len(group) * rows, wide), jnp.bfloat16) for group in groups],
        compiler_params=pltpu.CompilerParams(vmem_limit_bytes=14 * 1024 * 1024),
        cost_estimate=pl.CostEstimate(
            flops=2 * total * wide * ff,
            bytes_accessed=2 * ff * wide + 2 * total * wide,
            transcendentals=0,
        ),
    )(places, kept(hidden), kept(down_weight))


def add_up(*parts):
    total = parts[0].astype(jnp.float32)
    for part in parts[1:]:
        total = total + part.astype(jnp.float32)
    return total.astype(jnp.bfloat16)


def ring_shards(
    text_tokens, panels, panel_target, expert_ids, gate_weights, gate_up_weight, down_weight
):
    seq_count, expert_count = lax.axis_size("seq"), lax.axis_size("expert")
    ring = Ring(seq_count, expert_count)
    text_rows, tok_count = text_tokens.shape[0], expert_ids.shape[0]
    me = lax.axis_index(AXES)

    def onward(array):
        return lax.ppermute(array, AXES, ring.step(1))

    def back(array):
        return lax.ppermute(array, AXES, ring.step(-1))

    def across(array):
        return lax.ppermute(array, AXES, ring.swap())

    own = pack_call(
        text_tokens, panels, panel_target, expert_ids, gate_weights, ring.devices, expert_count
    )
    seq_of = ring.owner_of // expert_count
    numbers = np.arange(ring.devices, dtype=np.int32)[:, None]
    places = np.concatenate([numbers, seq_of, ring.sources_of.reshape(ring.devices, -1)], axis=1)
    places = jnp.asarray(places)[me]

    before, after = onward(own), back(own)
    other = across(own)
    own, places = lax.optimization_barrier((own, places))

    all_rows = len(ring.slots) * tok_count

    def whole(blocks):
        return [(i, 0) for i in range(len(blocks))]

    blocks = [own, other]
    hidden, gate_up = hidden_call(
        blocks, whole(blocks), tok_count, gate_up_weight, None, 0, all_rows
    )
    hidden, before = lax.optimization_barrier((hidden, before))
    hidden, after = lax.optimization_barrier((hidden, after))
    cut = tok_count // 2
    for s in range(1, ring.half):
        here = [after, before]
        there = [across(after), across(before)]
        if s + 1 == ring.half:
            before, after = before[:cut], after[cut:]
        before, after = onward(before), back(after)
        first_row = 4 * s * tok_count
        extra = down_weight if s == 1 else None
        blocks = here + there
        hidden, gate_up, *down = hidden_call(
            blocks, whole(blocks), tok_count, gate_up, hidden, first_row, all_rows, extra
        )
        if down:
            (down_here,) = down
        hidden, before = lax.optimization_barrier((hidden, before))
        hidden, after = lax.optimization_barrier((hidden, after))
    far = [before, after, across(before), across(after)]
    first_row = 2 * tok_count
    (hidden,) = hidden_call(
        far, whole(far), cut, gate_up, hidden, first_row, all_rows, last=True
    )

    def outputs(*groups):
        return down_call(
            hidden, places, down_here, groups, tok_count, text_rows, seq_count, ring.devices
        )

    def summed(kind):
        if kind == ring.half:
            mine, others = outputs((2,), (3,))
        else:
            slots = range(4 * kind, 4 * kind + 4) if kind else range(2)
            (others,) = outputs(tuple(slots[len(slots) // 2 :]))
            (mine,) = outputs(tuple(slots[: len(slots) // 2]))
        return mine, across(others)

    mine, swapped = summed(ring.half)
    ahead = onward(add_up(mine[:cut], swapped[:cut]))
    behind = back(add_up(mine[cut:], swapped[cut:]))
    ahead = jnp.pad(ahead, ((0, tok_count - cut), (0, 0)))
    behind = jnp.pad(behind, ((cut, 0), (0, 0)))
    for s in range(ring.half - 1, 0, -1):
        mine, swapped = summed(s)
        ahead = onward(add_up(ahead, mine[:tok_count], swapped[:tok_count]))
        behind = back(add_up(behind, mine[tok_count:], swapped[tok_count:]))
    mine, swapped = summed(0)
    return add_up(mine, swapped, ahead, behind)


def solution(mesh):
    placed = (
        P(("groups", "seq", "expert"), "tensor"),
        P(("groups", "seq", "expert"), None, "tensor"),
        P(("groups", "seq", "expert")),
        P(("groups", "seq", "expert"), None),
        P(("groups", "seq", "expert"), None),
        P(("seq", "expert"), None, "tensor", None),
        P(("seq", "expert"), "tensor", None),
    )

    def chosen(*args):
        seq_count, expert_count = mesh.shape["seq"], mesh.shape["expert"]
        owners = seq_count * expert_count
        tok_count, top_count = args[3].shape[0] // (mesh.shape["groups"] * owners), args[3].shape[1]
        experts_all = args[5].shape[0]
        slot_rows = experts_all * slot_capacity(tok_count, top_count, experts_all)
        dense = owners * tok_count <= 2 * slot_rows
        ring = dense and mesh.shape["tensor"] == 1 and expert_count == 4 and experts_all == owners
        ring = ring and seq_count > 2
        body = ring_shards if ring else slot_shards
        return jax.shard_map(
            body,
            mesh=mesh,
            in_specs=placed,
            out_specs=P(("groups", "seq", "expert"), "tensor"),
            check_vma=False,
        )(*args)

    return chosen
```

```python
import functools

import jax
import jax.numpy as jnp
import numpy as np
from jax import lax
from jax.experimental import pallas as pl
from jax.experimental.pallas import tpu as pltpu
from jax.sharding import PartitionSpec as P

AXES = ("seq", "expert")


def slot_shards(
    text_tokens, panels, panel_target, expert_ids, gate_weights, gate_up_weight, down_weight
):
    seq_count = lax.axis_size("seq")
    expert_count = lax.axis_size("expert")
    owner_count = seq_count * expert_count
    pan_count = panels.shape[0]
    cap_panel = max(2, (3 * pan_count + 2 * seq_count - 1) // (2 * seq_count))
    slot_range = jnp.arange(pan_count, dtype=jnp.int32)
    owner_dev = panel_target // pan_count
    dest_seq = owner_dev // expert_count
    dest_slot = panel_target % pan_count
    onehot = (dest_seq[:, None] == jnp.arange(seq_count, dtype=jnp.int32)[None, :]).astype(
        jnp.int32
    )
    earlier = jnp.cumsum(onehot, axis=0) - onehot
    placing = dest_seq * cap_panel + jnp.sum(earlier * onehot, axis=1)
    outgoing = (
        jnp.zeros((seq_count * cap_panel,) + panels.shape[1:], panels.dtype).at[placing].set(panels)
    )
    labels = jnp.full((seq_count * cap_panel,), -1, jnp.int32).at[placing].set(dest_slot)
    arrived, arrived_labels = (
        lax.all_to_all(outgoing, "seq", split_axis=0, concat_axis=0, tiled=True),
        lax.all_to_all(labels, "seq", split_axis=0, concat_axis=0, tiled=True),
    )
    matches = (arrived_labels[None, :] == slot_range[:, None]).astype(jnp.bfloat16)
    image_rows = jnp.einsum(
        "qn,nrd->qrd", matches, arrived, preferred_element_type=jnp.float32
    ).astype(jnp.bfloat16)
    half_rows = jnp.concatenate([text_tokens, image_rows.reshape(-1, image_rows.shape[-1])], axis=0)
    tokens = lax.all_gather(half_rows, "tensor", axis=1, tiled=True)
    feature_width = tokens.shape[1]
    tok_count, top_count = expert_ids.shape
    experts_all = owner_count * gate_up_weight.shape[0]
    capacity = slot_capacity(tok_count, top_count, experts_all)
    flat_ids = expert_ids.reshape(-1)
    onehot_ids = (flat_ids[:, None] == jnp.arange(experts_all, dtype=jnp.int32)[None, :]).astype(
        jnp.int32
    )
    before = jnp.cumsum(onehot_ids, axis=0) - onehot_ids
    placing_ids = flat_ids * capacity + jnp.sum(before * onehot_ids, axis=1)
    source_rows = jnp.arange(tok_count * top_count, dtype=jnp.int32) // top_count
    outgoing_rows = (
        jnp.zeros((experts_all * capacity, feature_width), tokens.dtype)
        .at[placing_ids]
        .set(tokens[source_rows])
    )
    load_counts = jnp.sum(onehot_ids, axis=0).reshape(experts_all, 1)
    outgoing_rows = outgoing_rows.reshape(experts_all, capacity, feature_width)
    pair_weight = gate_up_weight[0]
    out_weight = down_weight[0]
    arrived_rows, arrived_loads = (
        lax.all_to_all(outgoing_rows, AXES, split_axis=0, concat_axis=0, tiled=True),
        lax.all_to_all(load_counts, AXES, split_axis=0, concat_axis=0, tiled=True),
    )
    arrived_rows = arrived_rows.reshape(-1, feature_width)
    slot_total = arrived_rows.shape[0]
    slot_index = jnp.arange(capacity, dtype=jnp.int32)
    is_live = (slot_index[None, :] < arrived_loads).reshape(-1)
    live_int = is_live.astype(jnp.int32)
    compact_at = jnp.cumsum(live_int) - live_int
    live_total = jnp.sum(live_int)
    compact_src = (
        jnp.zeros((slot_total,), jnp.int32)
        .at[jnp.where(is_live, compact_at, slot_total)]
        .set(jnp.arange(slot_total, dtype=jnp.int32), mode="drop")
    )

    def expert_block(block_no, partial_out):
        chosen = lax.dynamic_slice_in_dim(compact_src, block_no * 128, 128)
        block_rows = arrived_rows[chosen]
        gate_up = jnp.einsum(
            "rd,gfd->grf", block_rows, pair_weight, preferred_element_type=jnp.float32
        )
        hidden = (jax.nn.silu(gate_up[0]) * gate_up[1]).astype(jnp.bfloat16)
        result = jnp.dot(hidden, out_weight, preferred_element_type=jnp.float32)
        return lax.dynamic_update_slice_in_dim(partial_out, result, block_no * 128, 0)

    block_total = (live_total + 127) // 128
    padded_total = (slot_total + 127) // 128 * 128
    partial_out = lax.fori_loop(
        0, block_total, expert_block, jnp.zeros((padded_total, feature_width), jnp.float32)
    )
    summed = lax.psum_scatter(partial_out, "tensor", scatter_dimension=1, tiled=True).astype(
        jnp.bfloat16
    )
    out_width = summed.shape[1]
    returned = jnp.where(
        is_live[:, None], summed[jnp.where(is_live, compact_at, 0)], jnp.zeros((), jnp.bfloat16)
    )
    came_back = lax.all_to_all(
        returned.reshape(experts_all, capacity, out_width),
        AXES,
        split_axis=0,
        concat_axis=0,
        tiled=True,
    )
    half_width = came_back.shape[2]
    picked = came_back.reshape(-1, half_width)[placing_ids].reshape(
        tok_count, top_count, half_width
    )
    mixed_out = jnp.sum(gate_weights[:, :, None] * picked.astype(jnp.float32), axis=1)
    return mixed_out.astype(jnp.bfloat16)


def slot_capacity(tok_count, top_count, experts_all):
    return min(tok_count, (2 * tok_count * top_count // experts_all + 7) // 8 * 8)


class Ring:
    def __init__(self, seq_count, expert_count):
        self.seq, self.expert = seq_count, expert_count
        self.chips = 2 * seq_count
        self.half = seq_count
        self.devices = seq_count * expert_count
        self.slots = [(0, 0), (0, 1), (self.half, 0), (self.half, 1)]
        for s in range(1, self.half):
            self.slots += [(s, 0), (-s, 0), (s, 1), (-s, 1)]
        slot_of = {(r % self.chips, k): i for i, (r, k) in enumerate(self.slots)}
        self.owner_of = np.zeros((self.devices, len(self.slots)), np.int32)
        self.sources_of = np.zeros((self.devices, len(self.slots), seq_count), np.int32)
        for d in range(self.devices):
            p, c = self.place(d)
            for i, (r, k) in enumerate(self.slots):
                q = (p + r) % self.chips
                self.owner_of[d, i] = self.device(q, c ^ k)
                x = q // seq_count
                for z in range(seq_count):
                    pos = z if x == 0 else self.chips - 1 - z
                    self.sources_of[d, i, z] = slot_of[((pos - p) % self.chips, k)]

    def place(self, d):
        z, e = divmod(d, self.expert)
        x, c = divmod(e, 2)
        return (z if x == 0 else self.chips - 1 - z), c

    def device(self, pos, c):
        x, z = (0, pos) if pos < self.seq else (1, self.chips - 1 - pos)
        return z * self.expert + x * 2 + c

    def step(self, by):
        pairs = []
        for d in range(self.devices):
            p, c = self.place(d)
            pairs.append((d, self.device((p + by) % self.chips, c)))
        return pairs

    def swap(self):
        return [(d, d ^ 1) for d in range(self.devices)]


def kept(array):
    return pltpu.with_memory_space_constraint(array, pltpu.VMEM)


def distant(array):
    return pltpu.with_memory_space_constraint(array, pltpu.HBM)


def pack_kernel(
    experts, expert_count, text_ref, panels_ref, target_ref, ids_ref, gates_ref, out_ref, sems
):
    text_rows, wide = text_ref.shape
    rows, width = out_ref.shape[0], out_ref.shape[1] - wide
    pan_count = target_ref.shape[1]
    panel_rows = (rows - text_rows) // pan_count
    copies = [
        pltpu.make_async_copy(text_ref, out_ref.at[:text_rows, :wide], sems.at[0]),
        pltpu.make_async_copy(panels_ref, out_ref.at[text_rows:, :wide], sems.at[1]),
    ]
    for copy in copies:
        copy.start()
    lane = lax.broadcasted_iota(jnp.int32, (rows, width), 1)
    term = sum((lane >= i * experts).astype(jnp.int32) for i in range(1, 4))
    expert = (lane - term * experts).astype(jnp.float32)
    diagonal = lax.broadcasted_iota(jnp.int32, (rows, rows), 0) == lax.broadcasted_iota(
        jnp.int32, (rows, rows), 1
    )

    def upright(row):
        return jnp.sum(jnp.where(diagonal, row, 0.0), axis=1, keepdims=True)

    gate = jnp.zeros((rows, width), jnp.float32)
    for k in range(ids_ref.shape[0]):
        number = upright(ids_ref[k : k + 1, :].astype(jnp.float32))
        gate += jnp.where(number == expert, upright(gates_ref[k : k + 1, :]), 0.0)
    high = gate.astype(jnp.bfloat16).astype(jnp.float32)
    middle = (gate - high).astype(jnp.bfloat16).astype(jnp.float32)
    low = gate - high - middle
    panel = lax.broadcasted_iota(jnp.int32, (rows, pan_count), 1)
    row = lax.broadcasted_iota(jnp.int32, (rows, pan_count), 0) - text_rows
    past = row - panel * panel_rows
    mine = (past >= 0) & (past < panel_rows)
    target = jnp.sum(
        jnp.where(mine, target_ref[...].astype(jnp.float32), 0.0), axis=1, keepdims=True
    )
    within = jnp.sum(jnp.where(mine, past.astype(jnp.float32), 0.0), axis=1, keepdims=True)
    owner, seq = jnp.zeros_like(target), jnp.zeros_like(target)
    for i in range(1, experts):
        passed = jnp.where(target >= i * pan_count, 1.0, 0.0)
        owner += passed
        if i % expert_count == 0:
            seq += passed
    place = (target - owner * pan_count) * panel_rows + within
    tags = jnp.where(term == 0, high, jnp.where(term == 1, middle, jnp.where(term == 2, low, 0.0)))
    tags = jnp.where(lane == 3 * experts, seq, jnp.where(lane == 3 * experts + 1, place, tags))
    out_ref[:, wide:] = tags.astype(jnp.bfloat16)
    for copy in copies:
        copy.wait()


def pack_call(text_tokens, panels, panel_target, expert_ids, gate_weights, experts, expert_count):
    rows, wide = expert_ids.shape[0], text_tokens.shape[1]
    width = (3 * experts + 2 + 127) // 128 * 128
    here, far = pl.BlockSpec(memory_space=pltpu.VMEM), pl.BlockSpec(memory_space=pltpu.HBM)
    return pl.pallas_call(
        functools.partial(pack_kernel, experts, expert_count),
        in_specs=[far, far, here, here, here],
        out_specs=here,
        out_shape=pltpu.VMEM((rows, wide + width), jnp.bfloat16),
        scratch_shapes=[pltpu.SemaphoreType.DMA((2,))],
        compiler_params=pltpu.CompilerParams(vmem_limit_bytes=14 * 1024 * 1024),
    )(
        distant(text_tokens),
        distant(panels.reshape(-1, wide)),
        panel_target[None, :],
        expert_ids.T,
        gate_weights.T,
    )


def hidden_kernel(places, rows, chunk, fetch, *refs):
    x_refs, refs = refs[: len(places)], refs[len(places) :]
    if fetch == "gate_up":
        far_ref, out_ref, w_ref, x_all, sems = refs
    elif fetch == "down":
        w_ref, _, far_ref, out_ref, _, down_ref, x_all, sems = refs
    else:
        w_ref, _, out_ref, x_all = refs[0], refs[1], refs[2], refs[-1]
    ff, wide = w_ref.shape[2:]
    whole, rest = divmod(ff, chunk)

    def fetched(i, width):
        part = pl.ds(pl.multiple_of(i * chunk, chunk), width)
        return pltpu.make_async_copy(far_ref.at[0, :, part], w_ref.at[0, :, part], sems.at[i])

    if fetch == "gate_up":
        for i in range(whole):
            fetched(i, chunk).start()
        if rest:
            fetched(whole, rest).start()
    if fetch == "down":
        pltpu.make_async_copy(far_ref, down_ref, sems.at[0]).start()
    for i, at in enumerate(places):
        x_all[i * rows : (i + 1) * rows, :] = x_refs[i][:, :wide]
        out_ref[at : at + rows, ff:] = x_refs[i][:, wide:]

    def step(i, width):
        if fetch == "gate_up":
            fetched(i, width).wait()
        part = pl.ds(pl.multiple_of(i * chunk, chunk), width)
        weight = w_ref[0, :, part, :].reshape(2 * width, wide)
        both = lax.dot_general(
            x_all[...], weight, (((1,), (1,)), ((), ())), preferred_element_type=jnp.float32
        )
        gate, up = both[:, :width], both[:, width:]
        hidden = (gate / (1.0 + jnp.exp(-gate)) * up).astype(out_ref.dtype)
        for i, at in enumerate(places):
            out_ref[at : at + rows, part] = hidden[i * rows : (i + 1) * rows]

    @pl.loop(0, whole)
    def _(i):
        step(i, chunk)

    if rest:
        step(whole, rest)
    if fetch == "down":
        pltpu.make_async_copy(far_ref, down_ref, sems.at[0]).wait()


def hidden_call(blocks, places, gate_up_weight, hidden, all_rows, down_weight=None, last=False):
    rows, width = blocks[0].shape
    ff, wide = gate_up_weight.shape[2:]
    count = len(blocks)
    chunk = 256
    here, far = pl.BlockSpec(memory_space=pltpu.VMEM), pl.BlockSpec(memory_space=pltpu.HBM)
    args, in_specs = [kept(block) for block in blocks], [here] * count
    out_shape, aliases = [pltpu.VMEM((all_rows, ff + width - wide), jnp.bfloat16)], {}
    scratch = [pltpu.VMEM((count * rows, wide), jnp.bfloat16)]
    fetch = None
    if hidden is None:
        fetch = "gate_up"
        args, in_specs = args + [distant(gate_up_weight)], in_specs + [far]
        out_shape.append(pltpu.VMEM(gate_up_weight.shape, gate_up_weight.dtype))
        scratch.append(pltpu.SemaphoreType.DMA((pl.cdiv(ff, chunk),)))
    else:
        args, in_specs = args + [kept(gate_up_weight), kept(hidden)], in_specs + [here, here]
        aliases = {count + 1: 0}
        if not last:
            out_shape.append(pltpu.VMEM(gate_up_weight.shape, gate_up_weight.dtype))
            aliases[count] = 1
        if down_weight is not None:
            fetch = "down"
            args, in_specs = args + [distant(down_weight)], in_specs + [far]
            out_shape.append(pltpu.VMEM(down_weight.shape, down_weight.dtype))
            scratch.append(pltpu.SemaphoreType.DMA((1,)))
    return pl.pallas_call(
        functools.partial(hidden_kernel, tuple(places), rows, chunk, fetch),
        in_specs=in_specs,
        out_specs=[here] * len(out_shape),
        out_shape=out_shape,
        scratch_shapes=scratch,
        input_output_aliases=aliases,
        compiler_params=pltpu.CompilerParams(vmem_limit_bytes=14 * 1024 * 1024),
        cost_estimate=pl.CostEstimate(
            flops=4 * count * rows * wide * ff,
            bytes_accessed=4 * ff * wide + 2 * count * rows * (wide + ff),
            transcendentals=count * rows * ff,
        ),
    )(*args)


def down_kernel(
    groups, rows, text_rows, seq_count, experts, chunk, places_ref, hidden_ref, w_ref, *refs
):
    out_refs, (column, picked, scale) = refs[:-3], refs[-3:]
    slots = [slot for group in groups for slot in group]
    image_rows = rows - text_rows
    slot_total = hidden_ref.shape[0] // rows
    ff = w_ref.shape[1]
    width = hidden_ref.shape[1] - ff
    expert = places_ref[0]
    lane = lax.broadcasted_iota(jnp.int32, (1, width), 1)
    is_gate = (lane == expert) | (lane == expert + experts) | (lane == expert + 2 * experts)
    place_of = jnp.where(lane == 3 * experts, float(image_rows), 0.0)
    place_of = jnp.where(lane == 3 * experts + 1, 1.0, place_of)
    wanted = lax.broadcasted_iota(jnp.int32, (1, image_rows), 1)
    for j, slot in enumerate(slots):
        at = slot * rows
        picked[j * rows : j * rows + text_rows, :] = hidden_ref[at : at + text_rows, :ff]
        for z in range(seq_count):
            source = places_ref[1 + slot_total + slot * seq_count + z]
            start = pl.multiple_of(source * rows + text_rows, 16)
            column[z * image_rows : (z + 1) * image_rows, :] = hidden_ref[
                pl.ds(start, image_rows), :
            ]
        place = column[:, ff:].astype(jnp.float32) * place_of
        place = jnp.sum(place, axis=1, keepdims=True)
        first = places_ref[1 + slot] * image_rows
        match = jnp.where(place == (wanted + first).astype(jnp.float32), 1.0, 0.0)
        rows_here = lax.dot_general(
            match.astype(jnp.bfloat16),
            column[:, :ff],
            (((0,), (0,)), ((), ())),
            preferred_element_type=jnp.float32,
        )
        picked[j * rows + text_rows : (j + 1) * rows, :] = rows_here.astype(jnp.bfloat16)
        gates = jnp.where(is_gate, hidden_ref[at : at + rows, ff:].astype(jnp.float32), 0.0)
        scale[j * rows : (j + 1) * rows, :] = jnp.sum(gates, axis=1, keepdims=True)

    @pl.loop(0, w_ref.shape[2] // chunk)
    def _(i):
        part = pl.ds(pl.multiple_of(i * chunk, chunk), chunk)
        result = jnp.dot(picked[...], w_ref[0, :, part], preferred_element_type=jnp.float32)
        scaled = result.astype(jnp.bfloat16).astype(jnp.float32) * scale[...]
        scaled = scaled.astype(jnp.bfloat16)
        start = 0
        for out_ref in out_refs:
            out_ref[:, part] = scaled[start : start + out_ref.shape[0]]
            start += out_ref.shape[0]


def down_call(hidden, places, down_weight, groups, rows, text_rows, seq_count, experts):
    _, ff, wide = down_weight.shape
    total = sum(len(group) for group in groups) * rows
    here = pl.BlockSpec(memory_space=pltpu.VMEM)
    return pl.pallas_call(
        functools.partial(down_kernel, groups, rows, text_rows, seq_count, experts, 512),
        grid_spec=pltpu.PrefetchScalarGridSpec(
            num_scalar_prefetch=1,
            grid=(1,),
            in_specs=[here] * 2,
            out_specs=[here] * len(groups),
            scratch_shapes=[
                pltpu.VMEM((seq_count * (rows - text_rows), hidden.shape[1]), jnp.bfloat16),
                pltpu.VMEM((total, ff), jnp.bfloat16),
                pltpu.VMEM((total, 1), jnp.float32),
            ],
        ),
        out_shape=[pltpu.VMEM((len(group) * rows, wide), jnp.bfloat16) for group in groups],
        compiler_params=pltpu.CompilerParams(vmem_limit_bytes=14 * 1024 * 1024),
        cost_estimate=pl.CostEstimate(
            flops=2 * total * wide * ff,
            bytes_accessed=2 * ff * wide + 2 * total * wide,
            transcendentals=0,
        ),
    )(places, kept(hidden), kept(down_weight))


def add_up(*parts):
    total = parts[0].astype(jnp.float32)
    for part in parts[1:]:
        total = total + part.astype(jnp.float32)
    return total.astype(jnp.bfloat16)


def ring_shards(
    text_tokens, panels, panel_target, expert_ids, gate_weights, gate_up_weight, down_weight
):
    seq_count, expert_count = lax.axis_size("seq"), lax.axis_size("expert")
    ring = Ring(seq_count, expert_count)
    text_rows, tok_count = text_tokens.shape[0], expert_ids.shape[0]
    me = lax.axis_index(AXES)

    def onward(array):
        return lax.ppermute(array, AXES, ring.step(1))

    def back(array):
        return lax.ppermute(array, AXES, ring.step(-1))

    def across(array):
        return lax.ppermute(array, AXES, ring.swap())

    own = pack_call(
        text_tokens, panels, panel_target, expert_ids, gate_weights, ring.devices, expert_count
    )
    seq_of = ring.owner_of // expert_count
    numbers = np.arange(ring.devices, dtype=np.int32)[:, None]
    places = np.concatenate([numbers, seq_of, ring.sources_of.reshape(ring.devices, -1)], axis=1)
    places = jnp.asarray(places)[me]

    before, after = onward(own), back(own)
    other = across(own)
    own, places = lax.optimization_barrier((own, places))

    all_rows = len(ring.slots) * tok_count

    def rows_of(*slots):
        return [slot * tok_count for slot in slots]

    hidden, gate_up = hidden_call([own, other], rows_of(0, 1), gate_up_weight, None, all_rows)
    hidden, before = lax.optimization_barrier((hidden, before))
    hidden, after = lax.optimization_barrier((hidden, after))
    cut = tok_count // 2
    swapped, swapped_rows = [], []
    for s in range(1, ring.half):
        blocks, places_here = [after, before, *swapped], rows_of(4 * s, 4 * s + 1) + swapped_rows
        swapped, swapped_rows = [across(after), across(before)], rows_of(4 * s + 2, 4 * s + 3)
        if s + 1 == ring.half:
            before, after = before[:cut], after[cut:]
        before, after = onward(before), back(after)
        extra = down_weight if s == 1 else None
        hidden, gate_up, *down = hidden_call(
            blocks, places_here, gate_up, hidden, all_rows, extra
        )
        if down:
            (down_here,) = down
        hidden, before, swapped = lax.optimization_barrier((hidden, before, swapped))
        hidden, after = lax.optimization_barrier((hidden, after))
    far = [before, after, across(before), across(after)]
    hidden, gate_up = hidden_call(swapped, swapped_rows, gate_up, hidden, all_rows)
    far_rows = [2 * tok_count + i * cut for i in range(4)]
    (hidden,) = hidden_call(far, far_rows, gate_up, hidden, all_rows, last=True)

    def outputs(*groups):
        return down_call(
            hidden, places, down_here, groups, tok_count, text_rows, seq_count, ring.devices
        )

    def summed(kind):
        if kind == ring.half:
            mine, others = outputs((2,), (3,))
        else:
            slots = range(4 * kind, 4 * kind + 4) if kind else range(2)
            (others,) = outputs(tuple(slots[len(slots) // 2 :]))
            (mine,) = outputs(tuple(slots[: len(slots) // 2]))
        return mine, across(others)

    mine, swapped = summed(ring.half)
    ahead = onward(add_up(mine[:cut], swapped[:cut]))
    behind = back(add_up(mine[cut:], swapped[cut:]))
    ahead = jnp.pad(ahead, ((0, tok_count - cut), (0, 0)))
    behind = jnp.pad(behind, ((cut, 0), (0, 0)))
    for s in range(ring.half - 1, 0, -1):
        mine, swapped = summed(s)
        ahead = onward(add_up(ahead, mine[:tok_count], swapped[:tok_count]))
        behind = back(add_up(behind, mine[tok_count:], swapped[tok_count:]))
    mine, swapped = summed(0)
    return add_up(mine, swapped, ahead, behind)


def solution(mesh):
    placed = (
        P(("groups", "seq", "expert"), "tensor"),
        P(("groups", "seq", "expert"), None, "tensor"),
        P(("groups", "seq", "expert")),
        P(("groups", "seq", "expert"), None),
        P(("groups", "seq", "expert"), None),
        P(("seq", "expert"), None, "tensor", None),
        P(("seq", "expert"), "tensor", None),
    )

    def chosen(*args):
        seq_count, expert_count = mesh.shape["seq"], mesh.shape["expert"]
        owners = seq_count * expert_count
        tok_count, top_count = args[3].shape[0] // (mesh.shape["groups"] * owners), args[3].shape[1]
        experts_all = args[5].shape[0]
        slot_rows = experts_all * slot_capacity(tok_count, top_count, experts_all)
        dense = owners * tok_count <= 2 * slot_rows
        ring = dense and mesh.shape["tensor"] == 1 and expert_count == 4 and experts_all == owners
        ring = ring and seq_count > 2
        body = ring_shards if ring else slot_shards
        return jax.shard_map(
            body,
            mesh=mesh,
            in_specs=placed,
            out_specs=P(("groups", "seq", "expert"), "tensor"),
            check_vma=False,
        )(*args)

    return chosen
```

```python
import functools

import jax
import jax.numpy as jnp
import numpy as np
from jax import lax
from jax.experimental import pallas as pl
from jax.experimental.pallas import tpu as pltpu
from jax.sharding import PartitionSpec as P

AXES = ("seq", "expert")


def slot_shards(
    text_tokens, panels, panel_target, expert_ids, gate_weights, gate_up_weight, down_weight
):
    seq_count = lax.axis_size("seq")
    expert_count = lax.axis_size("expert")
    owner_count = seq_count * expert_count
    pan_count = panels.shape[0]
    cap_panel = max(2, (3 * pan_count + 2 * seq_count - 1) // (2 * seq_count))
    slot_range = jnp.arange(pan_count, dtype=jnp.int32)
    owner_dev = panel_target // pan_count
    dest_seq = owner_dev // expert_count
    dest_slot = panel_target % pan_count
    onehot = (dest_seq[:, None] == jnp.arange(seq_count, dtype=jnp.int32)[None, :]).astype(
        jnp.int32
    )
    earlier = jnp.cumsum(onehot, axis=0) - onehot
    placing = dest_seq * cap_panel + jnp.sum(earlier * onehot, axis=1)
    outgoing = (
        jnp.zeros((seq_count * cap_panel,) + panels.shape[1:], panels.dtype).at[placing].set(panels)
    )
    labels = jnp.full((seq_count * cap_panel,), -1, jnp.int32).at[placing].set(dest_slot)
    arrived, arrived_labels = (
        lax.all_to_all(outgoing, "seq", split_axis=0, concat_axis=0, tiled=True),
        lax.all_to_all(labels, "seq", split_axis=0, concat_axis=0, tiled=True),
    )
    matches = (arrived_labels[None, :] == slot_range[:, None]).astype(jnp.bfloat16)
    image_rows = jnp.einsum(
        "qn,nrd->qrd", matches, arrived, preferred_element_type=jnp.float32
    ).astype(jnp.bfloat16)
    half_rows = jnp.concatenate([text_tokens, image_rows.reshape(-1, image_rows.shape[-1])], axis=0)
    tokens = lax.all_gather(half_rows, "tensor", axis=1, tiled=True)
    feature_width = tokens.shape[1]
    tok_count, top_count = expert_ids.shape
    experts_all = owner_count * gate_up_weight.shape[0]
    capacity = slot_capacity(tok_count, top_count, experts_all)
    flat_ids = expert_ids.reshape(-1)
    onehot_ids = (flat_ids[:, None] == jnp.arange(experts_all, dtype=jnp.int32)[None, :]).astype(
        jnp.int32
    )
    before = jnp.cumsum(onehot_ids, axis=0) - onehot_ids
    placing_ids = flat_ids * capacity + jnp.sum(before * onehot_ids, axis=1)
    source_rows = jnp.arange(tok_count * top_count, dtype=jnp.int32) // top_count
    outgoing_rows = (
        jnp.zeros((experts_all * capacity, feature_width), tokens.dtype)
        .at[placing_ids]
        .set(tokens[source_rows])
    )
    load_counts = jnp.sum(onehot_ids, axis=0).reshape(experts_all, 1)
    outgoing_rows = outgoing_rows.reshape(experts_all, capacity, feature_width)
    pair_weight = gate_up_weight[0]
    out_weight = down_weight[0]
    arrived_rows, arrived_loads = (
        lax.all_to_all(outgoing_rows, AXES, split_axis=0, concat_axis=0, tiled=True),
        lax.all_to_all(load_counts, AXES, split_axis=0, concat_axis=0, tiled=True),
    )
    arrived_rows = arrived_rows.reshape(-1, feature_width)
    slot_total = arrived_rows.shape[0]
    slot_index = jnp.arange(capacity, dtype=jnp.int32)
    is_live = (slot_index[None, :] < arrived_loads).reshape(-1)
    live_int = is_live.astype(jnp.int32)
    compact_at = jnp.cumsum(live_int) - live_int
    live_total = jnp.sum(live_int)
    compact_src = (
        jnp.zeros((slot_total,), jnp.int32)
        .at[jnp.where(is_live, compact_at, slot_total)]
        .set(jnp.arange(slot_total, dtype=jnp.int32), mode="drop")
    )

    def expert_block(block_no, partial_out):
        chosen = lax.dynamic_slice_in_dim(compact_src, block_no * 128, 128)
        block_rows = arrived_rows[chosen]
        gate_up = jnp.einsum(
            "rd,gfd->grf", block_rows, pair_weight, preferred_element_type=jnp.float32
        )
        hidden = (jax.nn.silu(gate_up[0]) * gate_up[1]).astype(jnp.bfloat16)
        result = jnp.dot(hidden, out_weight, preferred_element_type=jnp.float32)
        return lax.dynamic_update_slice_in_dim(partial_out, result, block_no * 128, 0)

    block_total = (live_total + 127) // 128
    padded_total = (slot_total + 127) // 128 * 128
    partial_out = lax.fori_loop(
        0, block_total, expert_block, jnp.zeros((padded_total, feature_width), jnp.float32)
    )
    summed = lax.psum_scatter(partial_out, "tensor", scatter_dimension=1, tiled=True).astype(
        jnp.bfloat16
    )
    out_width = summed.shape[1]
    returned = jnp.where(
        is_live[:, None], summed[jnp.where(is_live, compact_at, 0)], jnp.zeros((), jnp.bfloat16)
    )
    came_back = lax.all_to_all(
        returned.reshape(experts_all, capacity, out_width),
        AXES,
        split_axis=0,
        concat_axis=0,
        tiled=True,
    )
    half_width = came_back.shape[2]
    picked = came_back.reshape(-1, half_width)[placing_ids].reshape(
        tok_count, top_count, half_width
    )
    mixed_out = jnp.sum(gate_weights[:, :, None] * picked.astype(jnp.float32), axis=1)
    return mixed_out.astype(jnp.bfloat16)


def slot_capacity(tok_count, top_count, experts_all):
    return min(tok_count, (2 * tok_count * top_count // experts_all + 7) // 8 * 8)


class Ring:
    def __init__(self, seq_count, expert_count):
        self.seq, self.expert = seq_count, expert_count
        self.chips = 2 * seq_count
        self.half = seq_count
        self.devices = seq_count * expert_count
        self.slot_count = 4 * self.half
        self.owner_of = np.zeros((self.devices, self.slot_count), np.int32)
        self.sources_of = np.zeros((self.devices, self.slot_count, seq_count), np.int32)
        for d in range(self.devices):
            p, c = self.place(d)
            slots = [(0, 0), (0, 1), (self.half, 0), (self.half, 1)]
            for s in range(1, self.half):
                along = -s if c else s
                slots += [(-along, 0), (-along, 1), (along, 0), (along, 1)]
            slot_of = {(r % self.chips, k): i for i, (r, k) in enumerate(slots)}
            for i, (r, k) in enumerate(slots):
                q = (p + r) % self.chips
                self.owner_of[d, i] = self.device(q, c ^ k)
                x = q // seq_count
                for z in range(seq_count):
                    pos = z if x == 0 else self.chips - 1 - z
                    self.sources_of[d, i, z] = slot_of[((pos - p) % self.chips, k)]

    def place(self, d):
        z, e = divmod(d, self.expert)
        x, c = divmod(e, 2)
        return (z if x == 0 else self.chips - 1 - z), c

    def device(self, pos, c):
        x, z = (0, pos) if pos < self.seq else (1, self.chips - 1 - pos)
        return z * self.expert + x * 2 + c

    def step(self):
        pairs = []
        for d in range(self.devices):
            p, c = self.place(d)
            pairs.append((d, self.device((p + (-1 if c else 1)) % self.chips, c)))
        return pairs

    def swap(self):
        return [(d, d ^ 1) for d in range(self.devices)]


def kept(array):
    return pltpu.with_memory_space_constraint(array, pltpu.VMEM)


def distant(array):
    return pltpu.with_memory_space_constraint(array, pltpu.HBM)


def pack_kernel(
    experts, expert_count, text_ref, panels_ref, target_ref, ids_ref, gates_ref, out_ref, sems
):
    text_rows, wide = text_ref.shape
    rows, width = out_ref.shape[0], out_ref.shape[1] - wide
    pan_count = target_ref.shape[1]
    panel_rows = (rows - text_rows) // pan_count
    copies = [
        pltpu.make_async_copy(text_ref, out_ref.at[:text_rows, :wide], sems.at[0]),
        pltpu.make_async_copy(panels_ref, out_ref.at[text_rows:, :wide], sems.at[1]),
    ]
    for copy in copies:
        copy.start()
    lane = lax.broadcasted_iota(jnp.int32, (rows, width), 1)
    term = sum((lane >= i * experts).astype(jnp.int32) for i in range(1, 4))
    expert = (lane - term * experts).astype(jnp.float32)
    diagonal = lax.broadcasted_iota(jnp.int32, (rows, rows), 0) == lax.broadcasted_iota(
        jnp.int32, (rows, rows), 1
    )

    def upright(row):
        return jnp.sum(jnp.where(diagonal, row, 0.0), axis=1, keepdims=True)

    gate = jnp.zeros((rows, width), jnp.float32)
    for k in range(ids_ref.shape[0]):
        number = upright(ids_ref[k : k + 1, :].astype(jnp.float32))
        gate += jnp.where(number == expert, upright(gates_ref[k : k + 1, :]), 0.0)
    high = gate.astype(jnp.bfloat16).astype(jnp.float32)
    middle = (gate - high).astype(jnp.bfloat16).astype(jnp.float32)
    low = gate - high - middle
    panel = lax.broadcasted_iota(jnp.int32, (rows, pan_count), 1)
    row = lax.broadcasted_iota(jnp.int32, (rows, pan_count), 0) - text_rows
    past = row - panel * panel_rows
    mine = (past >= 0) & (past < panel_rows)
    target = jnp.sum(
        jnp.where(mine, target_ref[...].astype(jnp.float32), 0.0), axis=1, keepdims=True
    )
    within = jnp.sum(jnp.where(mine, past.astype(jnp.float32), 0.0), axis=1, keepdims=True)
    owner, seq = jnp.zeros_like(target), jnp.zeros_like(target)
    for i in range(1, experts):
        passed = jnp.where(target >= i * pan_count, 1.0, 0.0)
        owner += passed
        if i % expert_count == 0:
            seq += passed
    place = (target - owner * pan_count) * panel_rows + within
    tags = jnp.where(term == 0, high, jnp.where(term == 1, middle, jnp.where(term == 2, low, 0.0)))
    tags = jnp.where(lane == 3 * experts, seq, jnp.where(lane == 3 * experts + 1, place, tags))
    out_ref[:, wide:] = tags.astype(jnp.bfloat16)
    for copy in copies:
        copy.wait()


def pack_call(text_tokens, panels, panel_target, expert_ids, gate_weights, experts, expert_count):
    rows, wide = expert_ids.shape[0], text_tokens.shape[1]
    width = (3 * experts + 2 + 127) // 128 * 128
    here, far = pl.BlockSpec(memory_space=pltpu.VMEM), pl.BlockSpec(memory_space=pltpu.HBM)
    return pl.pallas_call(
        functools.partial(pack_kernel, experts, expert_count),
        in_specs=[far, far, here, here, here],
        out_specs=here,
        out_shape=pltpu.VMEM((rows, wide + width), jnp.bfloat16),
        scratch_shapes=[pltpu.SemaphoreType.DMA((2,))],
        compiler_params=pltpu.CompilerParams(vmem_limit_bytes=14 * 1024 * 1024),
    )(
        distant(text_tokens),
        distant(panels.reshape(-1, wide)),
        panel_target[None, :],
        expert_ids.T,
        gate_weights.T,
    )


def hidden_kernel(places, rows, chunk, fetch, *refs):
    x_refs, refs = refs[: len(places)], refs[len(places) :]
    if fetch == "gate_up":
        far_ref, out_ref, w_ref, x_all, sems = refs
    elif fetch == "down":
        w_ref, _, far_ref, out_ref, _, down_ref, x_all, sems = refs
    else:
        w_ref, _, out_ref, x_all = refs[0], refs[1], refs[2], refs[-1]
    ff, wide = w_ref.shape[2:]
    whole, rest = divmod(ff, chunk)

    def fetched(i, width):
        part = pl.ds(pl.multiple_of(i * chunk, chunk), width)
        return pltpu.make_async_copy(far_ref.at[0, :, part], w_ref.at[0, :, part], sems.at[i])

    if fetch == "gate_up":
        for i in range(whole):
            fetched(i, chunk).start()
        if rest:
            fetched(whole, rest).start()
    if fetch == "down":
        pltpu.make_async_copy(far_ref, down_ref, sems.at[0]).start()
    for i, at in enumerate(places):
        x_all[i * rows : (i + 1) * rows, :] = x_refs[i][:, :wide]
        out_ref[at : at + rows, ff:] = x_refs[i][:, wide:]

    def step(i, width):
        if fetch == "gate_up":
            fetched(i, width).wait()
        part = pl.ds(pl.multiple_of(i * chunk, chunk), width)
        weight = w_ref[0, :, part, :].reshape(2 * width, wide)
        both = lax.dot_general(
            x_all[...], weight, (((1,), (1,)), ((), ())), preferred_element_type=jnp.float32
        )
        gate, up = both[:, :width], both[:, width:]
        hidden = (gate / (1.0 + jnp.exp(-gate)) * up).astype(out_ref.dtype)
        for i, at in enumerate(places):
            out_ref[at : at + rows, part] = hidden[i * rows : (i + 1) * rows]

    @pl.loop(0, whole)
    def _(i):
        step(i, chunk)

    if rest:
        step(whole, rest)
    if fetch == "down":
        pltpu.make_async_copy(far_ref, down_ref, sems.at[0]).wait()


def hidden_call(blocks, places, gate_up_weight, hidden, all_rows, down_weight=None, last=False):
    rows, width = blocks[0].shape
    ff, wide = gate_up_weight.shape[2:]
    count = len(blocks)
    chunk = 256
    here, far = pl.BlockSpec(memory_space=pltpu.VMEM), pl.BlockSpec(memory_space=pltpu.HBM)
    args, in_specs = [kept(block) for block in blocks], [here] * count
    out_shape, aliases = [pltpu.VMEM((all_rows, ff + width - wide), jnp.bfloat16)], {}
    scratch = [pltpu.VMEM((count * rows, wide), jnp.bfloat16)]
    fetch = None
    if hidden is None:
        fetch = "gate_up"
        args, in_specs = args + [distant(gate_up_weight)], in_specs + [far]
        out_shape.append(pltpu.VMEM(gate_up_weight.shape, gate_up_weight.dtype))
        scratch.append(pltpu.SemaphoreType.DMA((pl.cdiv(ff, chunk),)))
    else:
        args, in_specs = args + [kept(gate_up_weight), kept(hidden)], in_specs + [here, here]
        aliases = {count + 1: 0}
        if not last:
            out_shape.append(pltpu.VMEM(gate_up_weight.shape, gate_up_weight.dtype))
            aliases[count] = 1
        if down_weight is not None:
            fetch = "down"
            args, in_specs = args + [distant(down_weight)], in_specs + [far]
            out_shape.append(pltpu.VMEM(down_weight.shape, down_weight.dtype))
            scratch.append(pltpu.SemaphoreType.DMA((1,)))
    return pl.pallas_call(
        functools.partial(hidden_kernel, tuple(places), rows, chunk, fetch),
        in_specs=in_specs,
        out_specs=[here] * len(out_shape),
        out_shape=out_shape,
        scratch_shapes=scratch,
        input_output_aliases=aliases,
        compiler_params=pltpu.CompilerParams(vmem_limit_bytes=14 * 1024 * 1024),
        cost_estimate=pl.CostEstimate(
            flops=4 * count * rows * wide * ff,
            bytes_accessed=4 * ff * wide + 2 * count * rows * (wide + ff),
            transcendentals=count * rows * ff,
        ),
    )(*args)


def down_kernel(
    groups, rows, text_rows, seq_count, experts, chunk, places_ref, hidden_ref, w_ref, *refs
):
    out_refs, (column, picked, scale) = refs[:-3], refs[-3:]
    slots = [slot for group in groups for slot in group]
    image_rows = rows - text_rows
    slot_total = hidden_ref.shape[0] // rows
    ff = w_ref.shape[1]
    width = hidden_ref.shape[1] - ff
    expert = places_ref[0]
    lane = lax.broadcasted_iota(jnp.int32, (1, width), 1)
    is_gate = (lane == expert) | (lane == expert + experts) | (lane == expert + 2 * experts)
    place_of = jnp.where(lane == 3 * experts, float(image_rows), 0.0)
    place_of = jnp.where(lane == 3 * experts + 1, 1.0, place_of)
    wanted = lax.broadcasted_iota(jnp.int32, (1, image_rows), 1)
    for j, slot in enumerate(slots):
        at = slot * rows
        picked[j * rows : j * rows + text_rows, :] = hidden_ref[at : at + text_rows, :ff]
        for z in range(seq_count):
            source = places_ref[1 + slot_total + slot * seq_count + z]
            start = pl.multiple_of(source * rows + text_rows, 16)
            column[z * image_rows : (z + 1) * image_rows, :] = hidden_ref[
                pl.ds(start, image_rows), :
            ]
        place = column[:, ff:].astype(jnp.float32) * place_of
        place = jnp.sum(place, axis=1, keepdims=True)
        first = places_ref[1 + slot] * image_rows
        match = jnp.where(place == (wanted + first).astype(jnp.float32), 1.0, 0.0)
        rows_here = lax.dot_general(
            match.astype(jnp.bfloat16),
            column[:, :ff],
            (((0,), (0,)), ((), ())),
            preferred_element_type=jnp.float32,
        )
        picked[j * rows + text_rows : (j + 1) * rows, :] = rows_here.astype(jnp.bfloat16)
        gates = jnp.where(is_gate, hidden_ref[at : at + rows, ff:].astype(jnp.float32), 0.0)
        scale[j * rows : (j + 1) * rows, :] = jnp.sum(gates, axis=1, keepdims=True)

    @pl.loop(0, w_ref.shape[2] // chunk)
    def _(i):
        part = pl.ds(pl.multiple_of(i * chunk, chunk), chunk)
        result = jnp.dot(picked[...], w_ref[0, :, part], preferred_element_type=jnp.float32)
        scaled = result.astype(jnp.bfloat16).astype(jnp.float32) * scale[...]
        scaled = scaled.astype(jnp.bfloat16)
        start = 0
        for out_ref in out_refs:
            out_ref[:, part] = scaled[start : start + out_ref.shape[0]]
            start += out_ref.shape[0]


def down_call(hidden, places, down_weight, groups, rows, text_rows, seq_count, experts):
    _, ff, wide = down_weight.shape
    total = sum(len(group) for group in groups) * rows
    here = pl.BlockSpec(memory_space=pltpu.VMEM)
    return pl.pallas_call(
        functools.partial(down_kernel, groups, rows, text_rows, seq_count, experts, 512),
        grid_spec=pltpu.PrefetchScalarGridSpec(
            num_scalar_prefetch=1,
            grid=(1,),
            in_specs=[here] * 2,
            out_specs=[here] * len(groups),
            scratch_shapes=[
                pltpu.VMEM((seq_count * (rows - text_rows), hidden.shape[1]), jnp.bfloat16),
                pltpu.VMEM((total, ff), jnp.bfloat16),
                pltpu.VMEM((total, 1), jnp.float32),
            ],
        ),
        out_shape=[pltpu.VMEM((len(group) * rows, wide), jnp.bfloat16) for group in groups],
        compiler_params=pltpu.CompilerParams(vmem_limit_bytes=14 * 1024 * 1024),
        cost_estimate=pl.CostEstimate(
            flops=2 * total * wide * ff,
            bytes_accessed=2 * ff * wide + 2 * total * wide,
            transcendentals=0,
        ),
    )(places, kept(hidden), kept(down_weight))


def add_up(*parts):
    total = parts[0].astype(jnp.float32)
    for part in parts[1:]:
        total = total + part.astype(jnp.float32)
    return total.astype(jnp.bfloat16)


def ring_shards(
    text_tokens, panels, panel_target, expert_ids, gate_weights, gate_up_weight, down_weight
):
    seq_count, expert_count = lax.axis_size("seq"), lax.axis_size("expert")
    ring = Ring(seq_count, expert_count)
    text_rows, tok_count = text_tokens.shape[0], expert_ids.shape[0]
    me = lax.axis_index(AXES)

    def along(array):
        return lax.ppermute(array, AXES, ring.step())

    def across(array):
        return lax.ppermute(array, AXES, ring.swap())

    own = pack_call(
        text_tokens, panels, panel_target, expert_ids, gate_weights, ring.devices, expert_count
    )
    seq_of = ring.owner_of // expert_count
    numbers = np.arange(ring.devices, dtype=np.int32)[:, None]
    places = np.concatenate([numbers, seq_of, ring.sources_of.reshape(ring.devices, -1)], axis=1)
    places = jnp.asarray(places)[me]

    all_rows = ring.slot_count * tok_count

    def tied(*values):
        return lax.optimization_barrier(values)

    def rows_of(*slots):
        return [slot * tok_count for slot in slots]

    lead = along(own)
    other = across(own)
    own, places = tied(own, places)
    hidden, gate_up = hidden_call([own, other], rows_of(0, 1), gate_up_weight, None, all_rows)
    trail = along(other)
    hidden, lead = tied(hidden, lead)
    hidden, trail = tied(hidden, trail)
    swapped, swapped_rows = [], []
    for s in range(1, ring.half):
        blocks, block_rows = [lead, trail, *swapped], rows_of(4 * s, 4 * s + 1) + swapped_rows
        next_lead = along(lead)
        next_trail = along(trail) if s + 1 < ring.half else None
        lead_across, trail_across = across(lead), across(trail)
        extra = down_weight if s == 1 else None
        hidden, gate_up, *down = hidden_call(blocks, block_rows, gate_up, hidden, all_rows, extra)
        if down:
            (down_here,) = down
        hidden, lead, lead_across = tied(hidden, next_lead, lead_across)
        if s + 1 < ring.half:
            hidden, trail, trail_across = tied(hidden, next_trail, trail_across)
        swapped, swapped_rows = [lead_across, trail_across], rows_of(4 * s + 3, 4 * s + 2)
    far = [lead, across(lead)]
    hidden, gate_up = hidden_call(swapped, swapped_rows, gate_up, hidden, all_rows)
    (hidden,) = hidden_call(far, rows_of(2, 3), gate_up, hidden, all_rows, last=True)

    def outputs(hidden, *groups):
        return down_call(
            hidden, places, down_here, groups, tok_count, text_rows, seq_count, ring.devices
        )

    def for_other(hidden, s):
        first, *rest = outputs(hidden, *(((4 * s + 1,), (4 * s,)) if s else ((1,),)))
        first, hidden = tied(first, hidden)
        return [first, *rest], hidden

    mine, others = outputs(hidden, (2,), (3,))
    mine, hidden = tied(mine, hidden)
    others_next, hidden = for_other(hidden, ring.half - 1)
    near = [across(array) for array in others_next]
    total, hidden = tied(add_up(mine, across(others)), hidden)
    lead, trail = along(total), []
    leading, trailing = outputs(hidden, (4 * ring.half - 2,), (4 * ring.half - 1,))
    leading, hidden = tied(leading, hidden)
    for s in range(ring.half - 1, 0, -1):
        others_next, hidden = for_other(hidden, s - 1)
        trail = [along(add_up(trailing, near[1], *trail))]
        if s > 1:
            next_leading, trailing = outputs(hidden, (4 * s - 2,), (4 * s - 1,))
        else:
            (next_leading,) = outputs(hidden, (0,))
        next_leading, hidden = tied(next_leading, hidden)
        total, hidden = tied(add_up(leading, near[0], lead), hidden)
        lead, leading = along(total), next_leading
        if s > 1:
            near = [across(array) for array in others_next]
    return add_up(leading, across(add_up(*others_next, *trail)), lead)


def solution(mesh):
    placed = (
        P(("groups", "seq", "expert"), "tensor"),
        P(("groups", "seq", "expert"), None, "tensor"),
        P(("groups", "seq", "expert")),
        P(("groups", "seq", "expert"), None),
        P(("groups", "seq", "expert"), None),
        P(("seq", "expert"), None, "tensor", None),
        P(("seq", "expert"), "tensor", None),
    )

    def chosen(*args):
        seq_count, expert_count = mesh.shape["seq"], mesh.shape["expert"]
        owners = seq_count * expert_count
        tok_count, top_count = args[3].shape[0] // (mesh.shape["groups"] * owners), args[3].shape[1]
        experts_all = args[5].shape[0]
        slot_rows = experts_all * slot_capacity(tok_count, top_count, experts_all)
        dense = owners * tok_count <= 2 * slot_rows
        ring = dense and mesh.shape["tensor"] == 1 and expert_count == 4 and experts_all == owners
        ring = ring and seq_count > 2
        body = ring_shards if ring else slot_shards
        return jax.shard_map(
            body,
            mesh=mesh,
            in_specs=placed,
            out_specs=P(("groups", "seq", "expert"), "tensor"),
            check_vma=False,
        )(*args)

    return chosen
```

```python
import functools

import jax
import jax.numpy as jnp
import numpy as np
from jax import lax
from jax.experimental import pallas as pl
from jax.experimental.pallas import tpu as pltpu
from jax.sharding import PartitionSpec as P

AXES = ("seq", "expert")


def slot_shards(
    text_tokens, panels, panel_target, expert_ids, gate_weights, gate_up_weight, down_weight
):
    seq_count = lax.axis_size("seq")
    expert_count = lax.axis_size("expert")
    owner_count = seq_count * expert_count
    pan_count = panels.shape[0]
    cap_panel = max(2, (3 * pan_count + 2 * seq_count - 1) // (2 * seq_count))
    slot_range = jnp.arange(pan_count, dtype=jnp.int32)
    owner_dev = panel_target // pan_count
    dest_seq = owner_dev // expert_count
    dest_slot = panel_target % pan_count
    onehot = (dest_seq[:, None] == jnp.arange(seq_count, dtype=jnp.int32)[None, :]).astype(
        jnp.int32
    )
    earlier = jnp.cumsum(onehot, axis=0) - onehot
    placing = dest_seq * cap_panel + jnp.sum(earlier * onehot, axis=1)
    outgoing = (
        jnp.zeros((seq_count * cap_panel,) + panels.shape[1:], panels.dtype).at[placing].set(panels)
    )
    labels = jnp.full((seq_count * cap_panel,), -1, jnp.int32).at[placing].set(dest_slot)
    arrived, arrived_labels = (
        lax.all_to_all(outgoing, "seq", split_axis=0, concat_axis=0, tiled=True),
        lax.all_to_all(labels, "seq", split_axis=0, concat_axis=0, tiled=True),
    )
    matches = (arrived_labels[None, :] == slot_range[:, None]).astype(jnp.bfloat16)
    image_rows = jnp.einsum(
        "qn,nrd->qrd", matches, arrived, preferred_element_type=jnp.float32
    ).astype(jnp.bfloat16)
    half_rows = jnp.concatenate([text_tokens, image_rows.reshape(-1, image_rows.shape[-1])], axis=0)
    tokens = lax.all_gather(half_rows, "tensor", axis=1, tiled=True)
    feature_width = tokens.shape[1]
    tok_count, top_count = expert_ids.shape
    experts_all = owner_count * gate_up_weight.shape[0]
    capacity = slot_capacity(tok_count, top_count, experts_all)
    flat_ids = expert_ids.reshape(-1)
    onehot_ids = (flat_ids[:, None] == jnp.arange(experts_all, dtype=jnp.int32)[None, :]).astype(
        jnp.int32
    )
    before = jnp.cumsum(onehot_ids, axis=0) - onehot_ids
    placing_ids = flat_ids * capacity + jnp.sum(before * onehot_ids, axis=1)
    source_rows = jnp.arange(tok_count * top_count, dtype=jnp.int32) // top_count
    outgoing_rows = (
        jnp.zeros((experts_all * capacity, feature_width), tokens.dtype)
        .at[placing_ids]
        .set(tokens[source_rows])
    )
    load_counts = jnp.sum(onehot_ids, axis=0).reshape(experts_all, 1)
    outgoing_rows = outgoing_rows.reshape(experts_all, capacity, feature_width)
    pair_weight = gate_up_weight[0]
    out_weight = down_weight[0]
    arrived_rows, arrived_loads = (
        lax.all_to_all(outgoing_rows, AXES, split_axis=0, concat_axis=0, tiled=True),
        lax.all_to_all(load_counts, AXES, split_axis=0, concat_axis=0, tiled=True),
    )
    arrived_rows = arrived_rows.reshape(-1, feature_width)
    slot_total = arrived_rows.shape[0]
    slot_index = jnp.arange(capacity, dtype=jnp.int32)
    is_live = (slot_index[None, :] < arrived_loads).reshape(-1)
    live_int = is_live.astype(jnp.int32)
    compact_at = jnp.cumsum(live_int) - live_int
    live_total = jnp.sum(live_int)
    compact_src = (
        jnp.zeros((slot_total,), jnp.int32)
        .at[jnp.where(is_live, compact_at, slot_total)]
        .set(jnp.arange(slot_total, dtype=jnp.int32), mode="drop")
    )

    def expert_block(block_no, partial_out):
        chosen = lax.dynamic_slice_in_dim(compact_src, block_no * 128, 128)
        block_rows = arrived_rows[chosen]
        gate_up = jnp.einsum(
            "rd,gfd->grf", block_rows, pair_weight, preferred_element_type=jnp.float32
        )
        hidden = (jax.nn.silu(gate_up[0]) * gate_up[1]).astype(jnp.bfloat16)
        result = jnp.dot(hidden, out_weight, preferred_element_type=jnp.float32)
        return lax.dynamic_update_slice_in_dim(partial_out, result, block_no * 128, 0)

    block_total = (live_total + 127) // 128
    padded_total = (slot_total + 127) // 128 * 128
    partial_out = lax.fori_loop(
        0, block_total, expert_block, jnp.zeros((padded_total, feature_width), jnp.float32)
    )
    summed = lax.psum_scatter(partial_out, "tensor", scatter_dimension=1, tiled=True).astype(
        jnp.bfloat16
    )
    out_width = summed.shape[1]
    returned = jnp.where(
        is_live[:, None], summed[jnp.where(is_live, compact_at, 0)], jnp.zeros((), jnp.bfloat16)
    )
    came_back = lax.all_to_all(
        returned.reshape(experts_all, capacity, out_width),
        AXES,
        split_axis=0,
        concat_axis=0,
        tiled=True,
    )
    half_width = came_back.shape[2]
    picked = came_back.reshape(-1, half_width)[placing_ids].reshape(
        tok_count, top_count, half_width
    )
    mixed_out = jnp.sum(gate_weights[:, :, None] * picked.astype(jnp.float32), axis=1)
    return mixed_out.astype(jnp.bfloat16)


def slot_capacity(tok_count, top_count, experts_all):
    return min(tok_count, (2 * tok_count * top_count // experts_all + 7) // 8 * 8)


class Ring:
    def __init__(self, seq_count, expert_count):
        self.seq, self.expert = seq_count, expert_count
        self.chips = 2 * seq_count
        self.half = seq_count
        self.devices = seq_count * expert_count
        self.slot_count = 4 * self.half
        self.owner_of = np.zeros((self.devices, self.slot_count), np.int32)
        self.sources_of = np.zeros((self.devices, self.slot_count, seq_count), np.int32)
        for d in range(self.devices):
            p, c = self.place(d)
            slots = [(0, 0), (0, 1), (self.half, 0), (self.half, 1)]
            for s in range(1, self.half):
                along = -s if c else s
                slots += [(-along, 0), (-along, 1), (along, 0), (along, 1)]
            slot_of = {(r % self.chips, k): i for i, (r, k) in enumerate(slots)}
            for i, (r, k) in enumerate(slots):
                q = (p + r) % self.chips
                self.owner_of[d, i] = self.device(q, c ^ k)
                x = q // seq_count
                for z in range(seq_count):
                    pos = z if x == 0 else self.chips - 1 - z
                    self.sources_of[d, i, z] = slot_of[((pos - p) % self.chips, k)]

    def place(self, d):
        z, e = divmod(d, self.expert)
        x, c = divmod(e, 2)
        return (z if x == 0 else self.chips - 1 - z), c

    def device(self, pos, c):
        x, z = (0, pos) if pos < self.seq else (1, self.chips - 1 - pos)
        return z * self.expert + x * 2 + c

    def step(self):
        pairs = []
        for d in range(self.devices):
            p, c = self.place(d)
            pairs.append((d, self.device((p + (-1 if c else 1)) % self.chips, c)))
        return pairs

    def swap(self):
        return [(d, d ^ 1) for d in range(self.devices)]


def kept(array):
    return pltpu.with_memory_space_constraint(array, pltpu.VMEM)


def distant(array):
    return pltpu.with_memory_space_constraint(array, pltpu.HBM)


def pack_kernel(
    experts, expert_count, text_ref, panels_ref, target_ref, ids_ref, gates_ref, out_ref, sems
):
    text_rows, wide = text_ref.shape
    rows, width = out_ref.shape[0], out_ref.shape[1] - wide
    pan_count = target_ref.shape[1]
    panel_rows = (rows - text_rows) // pan_count
    copies = [
        pltpu.make_async_copy(text_ref, out_ref.at[:text_rows, :wide], sems.at[0]),
        pltpu.make_async_copy(panels_ref, out_ref.at[text_rows:, :wide], sems.at[1]),
    ]
    for copy in copies:
        copy.start()
    lane = lax.broadcasted_iota(jnp.int32, (rows, width), 1)
    term = sum((lane >= i * experts).astype(jnp.int32) for i in range(1, 4))
    expert = (lane - term * experts).astype(jnp.float32)
    diagonal = lax.broadcasted_iota(jnp.int32, (rows, rows), 0) == lax.broadcasted_iota(
        jnp.int32, (rows, rows), 1
    )

    def upright(row):
        return jnp.sum(jnp.where(diagonal, row, 0.0), axis=1, keepdims=True)

    gate = jnp.zeros((rows, width), jnp.float32)
    for k in range(ids_ref.shape[0]):
        number = upright(ids_ref[k : k + 1, :].astype(jnp.float32))
        gate += jnp.where(number == expert, upright(gates_ref[k : k + 1, :]), 0.0)
    high = gate.astype(jnp.bfloat16).astype(jnp.float32)
    middle = (gate - high).astype(jnp.bfloat16).astype(jnp.float32)
    low = gate - high - middle
    panel = lax.broadcasted_iota(jnp.int32, (rows, pan_count), 1)
    row = lax.broadcasted_iota(jnp.int32, (rows, pan_count), 0) - text_rows
    past = row - panel * panel_rows
    mine = (past >= 0) & (past < panel_rows)
    target = jnp.sum(
        jnp.where(mine, target_ref[...].astype(jnp.float32), 0.0), axis=1, keepdims=True
    )
    within = jnp.sum(jnp.where(mine, past.astype(jnp.float32), 0.0), axis=1, keepdims=True)
    owner, seq = jnp.zeros_like(target), jnp.zeros_like(target)
    for i in range(1, experts):
        passed = jnp.where(target >= i * pan_count, 1.0, 0.0)
        owner += passed
        if i % expert_count == 0:
            seq += passed
    place = (target - owner * pan_count) * panel_rows + within
    tags = jnp.where(term == 0, high, jnp.where(term == 1, middle, jnp.where(term == 2, low, 0.0)))
    tags = jnp.where(lane == 3 * experts, seq, jnp.where(lane == 3 * experts + 1, place, tags))
    out_ref[:, wide:] = tags.astype(jnp.bfloat16)
    for copy in copies:
        copy.wait()


def pack_call(text_tokens, panels, panel_target, expert_ids, gate_weights, experts, expert_count):
    rows, wide = expert_ids.shape[0], text_tokens.shape[1]
    width = (3 * experts + 2 + 127) // 128 * 128
    here, far = pl.BlockSpec(memory_space=pltpu.VMEM), pl.BlockSpec(memory_space=pltpu.HBM)
    return pl.pallas_call(
        functools.partial(pack_kernel, experts, expert_count),
        in_specs=[far, far, here, here, here],
        out_specs=here,
        out_shape=pltpu.VMEM((rows, wide + width), jnp.bfloat16),
        scratch_shapes=[pltpu.SemaphoreType.DMA((2,))],
        compiler_params=pltpu.CompilerParams(vmem_limit_bytes=14 * 1024 * 1024),
    )(
        distant(text_tokens),
        distant(panels.reshape(-1, wide)),
        panel_target[None, :],
        expert_ids.T,
        gate_weights.T,
    )


def hidden_kernel(places, rows, chunk, fetch, *refs):
    x_refs, refs = refs[: len(places)], refs[len(places) :]
    if fetch == "gate_up":
        far_ref, out_ref, w_ref, x_all, sems = refs
    elif fetch == "down":
        w_ref, _, far_ref, out_ref, _, down_ref, x_all, sems = refs
    else:
        w_ref, _, out_ref, x_all = refs[0], refs[1], refs[2], refs[-1]
    ff, wide = w_ref.shape[2:]
    whole, rest = divmod(ff, chunk)

    def fetched(i, width):
        part = pl.ds(pl.multiple_of(i * chunk, chunk), width)
        return pltpu.make_async_copy(far_ref.at[0, :, part], w_ref.at[0, :, part], sems.at[i])

    if fetch == "gate_up":
        for i in range(whole):
            fetched(i, chunk).start()
        if rest:
            fetched(whole, rest).start()
    if fetch == "down":
        pltpu.make_async_copy(far_ref, down_ref, sems.at[0]).start()
    for i, at in enumerate(places):
        x_all[i * rows : (i + 1) * rows, :] = x_refs[i][:, :wide]
        out_ref[at : at + rows, ff:] = x_refs[i][:, wide:]

    def step(i, width):
        if fetch == "gate_up":
            fetched(i, width).wait()
        part = pl.ds(pl.multiple_of(i * chunk, chunk), width)
        weight = w_ref[0, :, part, :].reshape(2 * width, wide)
        both = lax.dot_general(
            x_all[...], weight, (((1,), (1,)), ((), ())), preferred_element_type=jnp.float32
        )
        gate, up = both[:, :width], both[:, width:]
        hidden = (gate / (1.0 + jnp.exp(-gate)) * up).astype(out_ref.dtype)
        for i, at in enumerate(places):
            out_ref[at : at + rows, part] = hidden[i * rows : (i + 1) * rows]

    @pl.loop(0, whole)
    def _(i):
        step(i, chunk)

    if rest:
        step(whole, rest)
    if fetch == "down":
        pltpu.make_async_copy(far_ref, down_ref, sems.at[0]).wait()


def hidden_call(blocks, places, gate_up_weight, hidden, all_rows, down_weight=None, last=False):
    rows, width = blocks[0].shape
    ff, wide = gate_up_weight.shape[2:]
    count = len(blocks)
    chunk = 256
    here, far = pl.BlockSpec(memory_space=pltpu.VMEM), pl.BlockSpec(memory_space=pltpu.HBM)
    args, in_specs = [kept(block) for block in blocks], [here] * count
    out_shape, aliases = [pltpu.VMEM((all_rows, ff + width - wide), jnp.bfloat16)], {}
    scratch = [pltpu.VMEM((count * rows, wide), jnp.bfloat16)]
    fetch = None
    if hidden is None:
        fetch = "gate_up"
        args, in_specs = args + [distant(gate_up_weight)], in_specs + [far]
        out_shape.append(pltpu.VMEM(gate_up_weight.shape, gate_up_weight.dtype))
        scratch.append(pltpu.SemaphoreType.DMA((pl.cdiv(ff, chunk),)))
    else:
        args, in_specs = args + [kept(gate_up_weight), kept(hidden)], in_specs + [here, here]
        aliases = {count + 1: 0}
        if not last:
            out_shape.append(pltpu.VMEM(gate_up_weight.shape, gate_up_weight.dtype))
            aliases[count] = 1
        if down_weight is not None:
            fetch = "down"
            args, in_specs = args + [distant(down_weight)], in_specs + [far]
            out_shape.append(pltpu.VMEM(down_weight.shape, down_weight.dtype))
            scratch.append(pltpu.SemaphoreType.DMA((1,)))
    return pl.pallas_call(
        functools.partial(hidden_kernel, tuple(places), rows, chunk, fetch),
        in_specs=in_specs,
        out_specs=[here] * len(out_shape),
        out_shape=out_shape,
        scratch_shapes=scratch,
        input_output_aliases=aliases,
        compiler_params=pltpu.CompilerParams(vmem_limit_bytes=14 * 1024 * 1024),
        cost_estimate=pl.CostEstimate(
            flops=4 * count * rows * wide * ff,
            bytes_accessed=4 * ff * wide + 2 * count * rows * (wide + ff),
            transcendentals=count * rows * ff,
        ),
    )(*args)


def down_kernel(
    groups, rows, text_rows, seq_count, experts, chunk, places_ref, hidden_ref, w_ref, *refs
):
    out_refs, (column, picked, scale) = refs[:-3], refs[-3:]
    slots = [slot for group in groups for slot in group]
    image_rows = rows - text_rows
    slot_total = hidden_ref.shape[0] // rows
    ff = w_ref.shape[1]
    width = hidden_ref.shape[1] - ff
    expert = places_ref[0]
    lane = lax.broadcasted_iota(jnp.int32, (1, width), 1)
    is_gate = (lane == expert) | (lane == expert + experts) | (lane == expert + 2 * experts)
    place_of = jnp.where(lane == 3 * experts, float(image_rows), 0.0)
    place_of = jnp.where(lane == 3 * experts + 1, 1.0, place_of)
    wanted = lax.broadcasted_iota(jnp.int32, (1, image_rows), 1)
    for j, slot in enumerate(slots):
        at = slot * rows
        picked[j * rows : j * rows + text_rows, :] = hidden_ref[at : at + text_rows, :ff]
        for z in range(seq_count):
            source = places_ref[1 + slot_total + slot * seq_count + z]
            start = pl.multiple_of(source * rows + text_rows, 16)
            column[z * image_rows : (z + 1) * image_rows, :] = hidden_ref[
                pl.ds(start, image_rows), :
            ]
        place = column[:, ff:].astype(jnp.float32) * place_of
        place = jnp.sum(place, axis=1, keepdims=True)
        first = places_ref[1 + slot] * image_rows
        match = jnp.where(place == (wanted + first).astype(jnp.float32), 1.0, 0.0)
        rows_here = lax.dot_general(
            match.astype(jnp.bfloat16),
            column[:, :ff],
            (((0,), (0,)), ((), ())),
            preferred_element_type=jnp.float32,
        )
        picked[j * rows + text_rows : (j + 1) * rows, :] = rows_here.astype(jnp.bfloat16)
        gates = jnp.where(is_gate, hidden_ref[at : at + rows, ff:].astype(jnp.float32), 0.0)
        scale[j * rows : (j + 1) * rows, :] = jnp.sum(gates, axis=1, keepdims=True)

    @pl.loop(0, w_ref.shape[2] // chunk)
    def _(i):
        part = pl.ds(pl.multiple_of(i * chunk, chunk), chunk)
        result = jnp.dot(picked[...], w_ref[0, :, part], preferred_element_type=jnp.float32)
        scaled = result.astype(jnp.bfloat16).astype(jnp.float32) * scale[...]
        scaled = scaled.astype(jnp.bfloat16)
        start = 0
        for out_ref in out_refs:
            out_ref[:, part] = scaled[start : start + out_ref.shape[0]]
            start += out_ref.shape[0]


def down_call(hidden, places, down_weight, groups, rows, text_rows, seq_count, experts):
    _, ff, wide = down_weight.shape
    total = sum(len(group) for group in groups) * rows
    here = pl.BlockSpec(memory_space=pltpu.VMEM)
    return pl.pallas_call(
        functools.partial(down_kernel, groups, rows, text_rows, seq_count, experts, 512),
        grid_spec=pltpu.PrefetchScalarGridSpec(
            num_scalar_prefetch=1,
            grid=(1,),
            in_specs=[here] * 2,
            out_specs=[here] * len(groups),
            scratch_shapes=[
                pltpu.VMEM((seq_count * (rows - text_rows), hidden.shape[1]), jnp.bfloat16),
                pltpu.VMEM((total, ff), jnp.bfloat16),
                pltpu.VMEM((total, 1), jnp.float32),
            ],
        ),
        out_shape=[pltpu.VMEM((len(group) * rows, wide), jnp.bfloat16) for group in groups],
        compiler_params=pltpu.CompilerParams(vmem_limit_bytes=14 * 1024 * 1024),
        cost_estimate=pl.CostEstimate(
            flops=2 * total * wide * ff,
            bytes_accessed=2 * ff * wide + 2 * total * wide,
            transcendentals=0,
        ),
    )(places, kept(hidden), kept(down_weight))


def add_up(*parts):
    total = parts[0].astype(jnp.float32)
    for part in parts[1:]:
        total = total + part.astype(jnp.float32)
    return total.astype(jnp.bfloat16)


def ring_shards(
    text_tokens, panels, panel_target, expert_ids, gate_weights, gate_up_weight, down_weight
):
    seq_count, expert_count = lax.axis_size("seq"), lax.axis_size("expert")
    ring = Ring(seq_count, expert_count)
    text_rows, tok_count = text_tokens.shape[0], expert_ids.shape[0]
    me = lax.axis_index(AXES)

    def along(array):
        return lax.ppermute(array, AXES, ring.step())

    def across(array):
        return lax.ppermute(array, AXES, ring.swap())

    own = pack_call(
        text_tokens, panels, panel_target, expert_ids, gate_weights, ring.devices, expert_count
    )
    seq_of = ring.owner_of // expert_count
    numbers = np.arange(ring.devices, dtype=np.int32)[:, None]
    places = np.concatenate([numbers, seq_of, ring.sources_of.reshape(ring.devices, -1)], axis=1)
    places = jnp.asarray(places)[me]

    all_rows = ring.slot_count * tok_count

    def tied(*values):
        return lax.optimization_barrier(values)

    def rows_of(*slots):
        return [slot * tok_count for slot in slots]

    lead = along(own)
    other = across(own)
    own, places = tied(own, places)
    hidden, gate_up = hidden_call([own, other], rows_of(0, 1), gate_up_weight, None, all_rows)
    trail = along(other)
    hidden, lead = tied(hidden, lead)
    hidden, trail = tied(hidden, trail)
    swapped = swapped_rows = None
    for s in range(1, ring.half):
        next_lead = along(lead)
        lead_across = across(lead)
        if swapped:
            hidden, gate_up = hidden_call(swapped, swapped_rows, gate_up, hidden, all_rows)
            hidden, trail = tied(hidden, trail)
        next_trail = along(trail) if s + 1 < ring.half else None
        trail_across = across(trail)
        extra = down_weight if s == 1 else None
        hidden, gate_up, *down = hidden_call(
            [lead, trail], rows_of(4 * s, 4 * s + 1), gate_up, hidden, all_rows, extra
        )
        if down:
            (down_here,) = down
        hidden, lead, lead_across, trail_across = tied(
            hidden, next_lead, lead_across, trail_across
        )
        trail = next_trail
        swapped, swapped_rows = [lead_across, trail_across], rows_of(4 * s + 3, 4 * s + 2)
    far = [lead, across(lead)]
    hidden, gate_up = hidden_call(swapped, swapped_rows, gate_up, hidden, all_rows)
    (hidden,) = hidden_call(far, rows_of(2, 3), gate_up, hidden, all_rows, last=True)

    def outputs(hidden, *groups):
        return down_call(
            hidden, places, down_here, groups, tok_count, text_rows, seq_count, ring.devices
        )

    def for_other(hidden, s):
        first, *rest = outputs(hidden, *(((4 * s + 1,), (4 * s,)) if s else ((1,),)))
        first, hidden = tied(first, hidden)
        return [first, *rest], hidden

    def for_own(hidden, s):
        first, *rest = outputs(hidden, *(((4 * s + 2,), (4 * s + 3,)) if s else ((0,),)))
        first, hidden = tied(first, hidden)
        return [first, *rest], hidden

    def sent(hidden, *parts):
        total, hidden = tied(add_up(*parts), hidden)
        return along(total), hidden

    mine, others = outputs(hidden, (2,), (3,))
    mine, hidden = tied(mine, hidden)
    swapped, hidden = for_other(hidden, ring.half - 1)
    swapped = [across(array) for array in swapped]
    lead, hidden = sent(hidden, mine, across(others))
    mine, hidden = for_own(hidden, ring.half - 1)
    trail, hidden = sent(hidden, mine[1], swapped[1])
    for s in range(ring.half - 1, 0, -1):
        next_swapped, hidden = for_other(hidden, s - 1)
        if s > 1:
            next_swapped = [across(array) for array in next_swapped]
        lead, hidden = sent(hidden, mine[0], swapped[0], lead)
        mine, hidden = for_own(hidden, s - 1)
        swapped = next_swapped
        if s > 1:
            trail, hidden = sent(hidden, mine[1], swapped[1], trail)
    return add_up(mine[0], across(add_up(swapped[0], trail)), lead)


def solution(mesh):
    placed = (
        P(("groups", "seq", "expert"), "tensor"),
        P(("groups", "seq", "expert"), None, "tensor"),
        P(("groups", "seq", "expert")),
        P(("groups", "seq", "expert"), None),
        P(("groups", "seq", "expert"), None),
        P(("seq", "expert"), None, "tensor", None),
        P(("seq", "expert"), "tensor", None),
    )

    def chosen(*args):
        seq_count, expert_count = mesh.shape["seq"], mesh.shape["expert"]
        owners = seq_count * expert_count
        tok_count, top_count = args[3].shape[0] // (mesh.shape["groups"] * owners), args[3].shape[1]
        experts_all = args[5].shape[0]
        slot_rows = experts_all * slot_capacity(tok_count, top_count, experts_all)
        dense = owners * tok_count <= 2 * slot_rows
        ring = dense and mesh.shape["tensor"] == 1 and expert_count == 4 and experts_all == owners
        ring = ring and seq_count > 2
        body = ring_shards if ring else slot_shards
        return jax.shard_map(
            body,
            mesh=mesh,
            in_specs=placed,
            out_specs=P(("groups", "seq", "expert"), "tensor"),
            check_vma=False,
        )(*args)

    return chosen
```

```python
import functools

import jax
import jax.numpy as jnp
import numpy as np
from jax import lax
from jax.experimental import pallas as pl
from jax.experimental.pallas import tpu as pltpu
from jax.sharding import PartitionSpec as P

AXES = ("seq", "expert")


def slot_shards(
    text_tokens, panels, panel_target, expert_ids, gate_weights, gate_up_weight, down_weight
):
    seq_count = lax.axis_size("seq")
    expert_count = lax.axis_size("expert")
    owner_count = seq_count * expert_count
    pan_count = panels.shape[0]
    cap_panel = max(2, (3 * pan_count + 2 * seq_count - 1) // (2 * seq_count))
    slot_range = jnp.arange(pan_count, dtype=jnp.int32)
    owner_dev = panel_target // pan_count
    dest_seq = owner_dev // expert_count
    dest_slot = panel_target % pan_count
    onehot = (dest_seq[:, None] == jnp.arange(seq_count, dtype=jnp.int32)[None, :]).astype(
        jnp.int32
    )
    earlier = jnp.cumsum(onehot, axis=0) - onehot
    placing = dest_seq * cap_panel + jnp.sum(earlier * onehot, axis=1)
    outgoing = (
        jnp.zeros((seq_count * cap_panel,) + panels.shape[1:], panels.dtype).at[placing].set(panels)
    )
    labels = jnp.full((seq_count * cap_panel,), -1, jnp.int32).at[placing].set(dest_slot)
    arrived, arrived_labels = (
        lax.all_to_all(outgoing, "seq", split_axis=0, concat_axis=0, tiled=True),
        lax.all_to_all(labels, "seq", split_axis=0, concat_axis=0, tiled=True),
    )
    matches = (arrived_labels[None, :] == slot_range[:, None]).astype(jnp.bfloat16)
    image_rows = jnp.einsum(
        "qn,nrd->qrd", matches, arrived, preferred_element_type=jnp.float32
    ).astype(jnp.bfloat16)
    half_rows = jnp.concatenate([text_tokens, image_rows.reshape(-1, image_rows.shape[-1])], axis=0)
    tokens = lax.all_gather(half_rows, "tensor", axis=1, tiled=True)
    feature_width = tokens.shape[1]
    tok_count, top_count = expert_ids.shape
    experts_all = owner_count * gate_up_weight.shape[0]
    capacity = slot_capacity(tok_count, top_count, experts_all)
    flat_ids = expert_ids.reshape(-1)
    onehot_ids = (flat_ids[:, None] == jnp.arange(experts_all, dtype=jnp.int32)[None, :]).astype(
        jnp.int32
    )
    before = jnp.cumsum(onehot_ids, axis=0) - onehot_ids
    placing_ids = flat_ids * capacity + jnp.sum(before * onehot_ids, axis=1)
    source_rows = jnp.arange(tok_count * top_count, dtype=jnp.int32) // top_count
    outgoing_rows = (
        jnp.zeros((experts_all * capacity, feature_width), tokens.dtype)
        .at[placing_ids]
        .set(tokens[source_rows])
    )
    load_counts = jnp.sum(onehot_ids, axis=0).reshape(experts_all, 1)
    outgoing_rows = outgoing_rows.reshape(experts_all, capacity, feature_width)
    pair_weight = gate_up_weight[0]
    out_weight = down_weight[0]
    arrived_rows, arrived_loads = (
        lax.all_to_all(outgoing_rows, AXES, split_axis=0, concat_axis=0, tiled=True),
        lax.all_to_all(load_counts, AXES, split_axis=0, concat_axis=0, tiled=True),
    )
    arrived_rows = arrived_rows.reshape(-1, feature_width)
    slot_total = arrived_rows.shape[0]
    slot_index = jnp.arange(capacity, dtype=jnp.int32)
    is_live = (slot_index[None, :] < arrived_loads).reshape(-1)
    live_int = is_live.astype(jnp.int32)
    compact_at = jnp.cumsum(live_int) - live_int
    live_total = jnp.sum(live_int)
    compact_src = (
        jnp.zeros((slot_total,), jnp.int32)
        .at[jnp.where(is_live, compact_at, slot_total)]
        .set(jnp.arange(slot_total, dtype=jnp.int32), mode="drop")
    )

    def expert_block(block_no, partial_out):
        chosen = lax.dynamic_slice_in_dim(compact_src, block_no * 128, 128)
        block_rows = arrived_rows[chosen]
        gate_up = jnp.einsum(
            "rd,gfd->grf", block_rows, pair_weight, preferred_element_type=jnp.float32
        )
        hidden = (jax.nn.silu(gate_up[0]) * gate_up[1]).astype(jnp.bfloat16)
        result = jnp.dot(hidden, out_weight, preferred_element_type=jnp.float32)
        return lax.dynamic_update_slice_in_dim(partial_out, result, block_no * 128, 0)

    block_total = (live_total + 127) // 128
    padded_total = (slot_total + 127) // 128 * 128
    partial_out = lax.fori_loop(
        0, block_total, expert_block, jnp.zeros((padded_total, feature_width), jnp.float32)
    )
    summed = lax.psum_scatter(partial_out, "tensor", scatter_dimension=1, tiled=True).astype(
        jnp.bfloat16
    )
    out_width = summed.shape[1]
    returned = jnp.where(
        is_live[:, None], summed[jnp.where(is_live, compact_at, 0)], jnp.zeros((), jnp.bfloat16)
    )
    came_back = lax.all_to_all(
        returned.reshape(experts_all, capacity, out_width),
        AXES,
        split_axis=0,
        concat_axis=0,
        tiled=True,
    )
    half_width = came_back.shape[2]
    picked = came_back.reshape(-1, half_width)[placing_ids].reshape(
        tok_count, top_count, half_width
    )
    mixed_out = jnp.sum(gate_weights[:, :, None] * picked.astype(jnp.float32), axis=1)
    return mixed_out.astype(jnp.bfloat16)


def slot_capacity(tok_count, top_count, experts_all):
    return min(tok_count, (2 * tok_count * top_count // experts_all + 7) // 8 * 8)


class Ring:
    def __init__(self, seq_count, expert_count):
        self.seq, self.expert = seq_count, expert_count
        self.chips = 2 * seq_count
        self.half = seq_count
        self.devices = seq_count * expert_count
        self.slot_count = 4 * self.half
        self.owner_of = np.zeros((self.devices, self.slot_count), np.int32)
        self.sources_of = np.zeros((self.devices, self.slot_count, seq_count), np.int32)
        for d in range(self.devices):
            p, c = self.place(d)
            slots = [(0, 0), (0, 1), (self.half, 0), (self.half, 1)]
            for s in range(1, self.half):
                along = -s if c else s
                slots += [(-along, 0), (-along, 1), (along, 0), (along, 1)]
            slot_of = {(r % self.chips, k): i for i, (r, k) in enumerate(slots)}
            for i, (r, k) in enumerate(slots):
                q = (p + r) % self.chips
                self.owner_of[d, i] = self.device(q, c ^ k)
                x = q // seq_count
                for z in range(seq_count):
                    pos = z if x == 0 else self.chips - 1 - z
                    self.sources_of[d, i, z] = slot_of[((pos - p) % self.chips, k)]

    def place(self, d):
        z, e = divmod(d, self.expert)
        x, c = divmod(e, 2)
        return (z if x == 0 else self.chips - 1 - z), c

    def device(self, pos, c):
        x, z = (0, pos) if pos < self.seq else (1, self.chips - 1 - pos)
        return z * self.expert + x * 2 + c

    def step(self):
        pairs = []
        for d in range(self.devices):
            p, c = self.place(d)
            pairs.append((d, self.device((p + (-1 if c else 1)) % self.chips, c)))
        return pairs

    def swap(self):
        return [(d, d ^ 1) for d in range(self.devices)]


def kept(array):
    return pltpu.with_memory_space_constraint(array, pltpu.VMEM)


def distant(array):
    return pltpu.with_memory_space_constraint(array, pltpu.HBM)


def pack_kernel(
    experts, expert_count, text_ref, panels_ref, target_hbm, ids_hbm, gates_hbm, out_ref,
    target_ref, ids_ref, gates_ref, sems,
):
    text_rows, wide = text_ref.shape
    rows, width = out_ref.shape[0], out_ref.shape[1] - wide
    pan_count = target_ref.shape[1]
    panel_rows = (rows - text_rows) // pan_count
    copies = [
        pltpu.make_async_copy(text_ref, out_ref.at[:text_rows, :wide], sems.at[0]),
        pltpu.make_async_copy(panels_ref, out_ref.at[text_rows:, :wide], sems.at[1]),
    ]
    tables = [
        pltpu.make_async_copy(target_hbm, target_ref, sems.at[2]),
        pltpu.make_async_copy(ids_hbm, ids_ref, sems.at[3]),
        pltpu.make_async_copy(gates_hbm, gates_ref, sems.at[4]),
    ]
    for copy in tables + copies:
        copy.start()
    for copy in tables:
        copy.wait()
    lane = lax.broadcasted_iota(jnp.int32, (rows, width), 1)
    term = sum((lane >= i * experts).astype(jnp.int32) for i in range(1, 4))
    expert = (lane - term * experts).astype(jnp.float32)
    diagonal = lax.broadcasted_iota(jnp.int32, (rows, rows), 0) == lax.broadcasted_iota(
        jnp.int32, (rows, rows), 1
    )

    def upright(row):
        return jnp.sum(jnp.where(diagonal, row, 0.0), axis=1, keepdims=True)

    gate = jnp.zeros((rows, width), jnp.float32)
    for k in range(ids_ref.shape[0]):
        number = upright(ids_ref[k : k + 1, :].astype(jnp.float32))
        gate += jnp.where(number == expert, upright(gates_ref[k : k + 1, :]), 0.0)
    high = gate.astype(jnp.bfloat16).astype(jnp.float32)
    middle = (gate - high).astype(jnp.bfloat16).astype(jnp.float32)
    low = gate - high - middle
    panel = lax.broadcasted_iota(jnp.int32, (rows, pan_count), 1)
    row = lax.broadcasted_iota(jnp.int32, (rows, pan_count), 0) - text_rows
    past = row - panel * panel_rows
    mine = (past >= 0) & (past < panel_rows)
    target = jnp.sum(
        jnp.where(mine, target_ref[...].astype(jnp.float32), 0.0), axis=1, keepdims=True
    )
    within = jnp.sum(jnp.where(mine, past.astype(jnp.float32), 0.0), axis=1, keepdims=True)
    owner, seq = jnp.zeros_like(target), jnp.zeros_like(target)
    for i in range(1, experts):
        passed = jnp.where(target >= i * pan_count, 1.0, 0.0)
        owner += passed
        if i % expert_count == 0:
            seq += passed
    place = (target - owner * pan_count) * panel_rows + within
    tags = jnp.where(term == 0, high, jnp.where(term == 1, middle, jnp.where(term == 2, low, 0.0)))
    tags = jnp.where(lane == 3 * experts, seq, jnp.where(lane == 3 * experts + 1, place, tags))
    out_ref[:, wide:] = tags.astype(jnp.bfloat16)
    for copy in copies:
        copy.wait()


def pack_call(text_tokens, panels, panel_target, expert_ids, gate_weights, experts, expert_count):
    rows, wide = expert_ids.shape[0], text_tokens.shape[1]
    width = (3 * experts + 2 + 127) // 128 * 128
    here, far = pl.BlockSpec(memory_space=pltpu.VMEM), pl.BlockSpec(memory_space=pltpu.HBM)
    return pl.pallas_call(
        functools.partial(pack_kernel, experts, expert_count),
        in_specs=[far] * 5,
        out_specs=here,
        out_shape=pltpu.VMEM((rows, wide + width), jnp.bfloat16),
        scratch_shapes=[
            pltpu.VMEM((1, panel_target.shape[0]), jnp.int32),
            pltpu.VMEM(expert_ids.shape[::-1], jnp.int32),
            pltpu.VMEM(gate_weights.shape[::-1], jnp.float32),
            pltpu.SemaphoreType.DMA((5,)),
        ],
        compiler_params=pltpu.CompilerParams(vmem_limit_bytes=14 * 1024 * 1024),
    )(
        distant(text_tokens),
        distant(panels.reshape(-1, wide)),
        distant(panel_target[None, :]),
        distant(expert_ids.T),
        distant(gate_weights.T),
    )


def hidden_kernel(places, rows, chunk, fetch, *refs):
    x_refs, refs = refs[: len(places)], refs[len(places) :]
    if fetch == "gate_up":
        far_ref, out_ref, w_ref, x_all, sems = refs
    elif fetch == "down":
        w_ref, _, far_ref, out_ref, _, down_ref, x_all, sems = refs
    else:
        w_ref, _, out_ref, x_all = refs[0], refs[1], refs[2], refs[-1]
    ff, wide = w_ref.shape[2:]
    whole, rest = divmod(ff, chunk)

    def fetched(i, width):
        part = pl.ds(pl.multiple_of(i * chunk, chunk), width)
        return pltpu.make_async_copy(far_ref.at[0, :, part], w_ref.at[0, :, part], sems.at[i])

    if fetch == "gate_up":
        for i in range(whole):
            fetched(i, chunk).start()
        if rest:
            fetched(whole, rest).start()
    if fetch == "down":
        pltpu.make_async_copy(far_ref, down_ref, sems.at[0]).start()
    for i, at in enumerate(places):
        x_all[i * rows : (i + 1) * rows, :] = x_refs[i][:, :wide]
        out_ref[at : at + rows, ff:] = x_refs[i][:, wide:]

    def step(i, width):
        if fetch == "gate_up":
            fetched(i, width).wait()
        part = pl.ds(i * chunk, width)
        weight = w_ref[0, :, part, :].reshape(2 * width, wide)
        both = lax.dot_general(
            x_all[...], weight, (((1,), (1,)), ((), ())), preferred_element_type=jnp.float32
        )
        gate, up = both[:, :width], both[:, width:]
        gate = 0.5 * gate
        hidden = (gate * (1.0 + jnp.tanh(gate)) * up).astype(out_ref.dtype)
        for i, at in enumerate(places):
            out_ref[at : at + rows, part] = hidden[i * rows : (i + 1) * rows]

    for i, width in enumerate([chunk] * whole + [rest] * (rest > 0)):
        step(i, width)
    if fetch == "down":
        pltpu.make_async_copy(far_ref, down_ref, sems.at[0]).wait()


def hidden_call(blocks, places, gate_up_weight, hidden, all_rows, down_weight=None, last=False):
    rows, width = blocks[0].shape
    ff, wide = gate_up_weight.shape[2:]
    count = len(blocks)
    chunk = 256
    here, far = pl.BlockSpec(memory_space=pltpu.VMEM), pl.BlockSpec(memory_space=pltpu.HBM)
    args, in_specs = [kept(block) for block in blocks], [here] * count
    out_shape, aliases = [pltpu.VMEM((all_rows, ff + width - wide), jnp.bfloat16)], {}
    scratch = [pltpu.VMEM((count * rows, wide), jnp.bfloat16)]
    fetch = None
    if hidden is None:
        fetch = "gate_up"
        args, in_specs = args + [distant(gate_up_weight)], in_specs + [far]
        out_shape.append(pltpu.VMEM(gate_up_weight.shape, gate_up_weight.dtype))
        scratch.append(pltpu.SemaphoreType.DMA((pl.cdiv(ff, chunk),)))
    else:
        args, in_specs = args + [kept(gate_up_weight), kept(hidden)], in_specs + [here, here]
        aliases = {count + 1: 0}
        if not last:
            out_shape.append(pltpu.VMEM(gate_up_weight.shape, gate_up_weight.dtype))
            aliases[count] = 1
        if down_weight is not None:
            fetch = "down"
            args, in_specs = args + [distant(down_weight)], in_specs + [far]
            out_shape.append(pltpu.VMEM(down_weight.shape, down_weight.dtype))
            scratch.append(pltpu.SemaphoreType.DMA((1,)))
    return pl.pallas_call(
        functools.partial(hidden_kernel, tuple(places), rows, chunk, fetch),
        in_specs=in_specs,
        out_specs=[here] * len(out_shape),
        out_shape=out_shape,
        scratch_shapes=scratch,
        input_output_aliases=aliases,
        compiler_params=pltpu.CompilerParams(vmem_limit_bytes=14 * 1024 * 1024),
        cost_estimate=pl.CostEstimate(
            flops=4 * count * rows * wide * ff,
            bytes_accessed=4 * ff * wide + 2 * count * rows * (wide + ff),
            transcendentals=count * rows * ff,
        ),
    )(*args)


def down_kernel(
    groups, rows, text_rows, seq_count, experts, chunk, places_ref, hidden_ref, w_ref, *refs
):
    out_refs, (column, picked, scale) = refs[:-3], refs[-3:]
    slots = [slot for group in groups for slot in group]
    image_rows = rows - text_rows
    slot_total = hidden_ref.shape[0] // rows
    ff = w_ref.shape[1]
    width = hidden_ref.shape[1] - ff
    expert = places_ref[0]
    lane = lax.broadcasted_iota(jnp.int32, (1, width), 1)
    is_gate = (lane == expert) | (lane == expert + experts) | (lane == expert + 2 * experts)
    place_of = jnp.where(lane == 3 * experts, float(image_rows), 0.0)
    place_of = jnp.where(lane == 3 * experts + 1, 1.0, place_of)
    wanted = lax.broadcasted_iota(jnp.int32, (1, image_rows), 1)
    for j, slot in enumerate(slots):
        at = slot * rows
        picked[j * rows : j * rows + text_rows, :] = hidden_ref[at : at + text_rows, :ff]
        for z in range(seq_count):
            source = places_ref[1 + slot_total + slot * seq_count + z]
            start = pl.multiple_of(source * rows + text_rows, 16)
            column[z * image_rows : (z + 1) * image_rows, :] = hidden_ref[
                pl.ds(start, image_rows), :
            ]
        place = column[:, ff:].astype(jnp.float32) * place_of
        place = jnp.sum(place, axis=1, keepdims=True)
        first = places_ref[1 + slot] * image_rows
        match = jnp.where(place == (wanted + first).astype(jnp.float32), 1.0, 0.0)
        rows_here = lax.dot_general(
            match.astype(jnp.bfloat16),
            column[:, :ff],
            (((0,), (0,)), ((), ())),
            preferred_element_type=jnp.float32,
        )
        picked[j * rows + text_rows : (j + 1) * rows, :] = rows_here.astype(jnp.bfloat16)
        gates = jnp.where(is_gate, hidden_ref[at : at + rows, ff:].astype(jnp.float32), 0.0)
        scale[j * rows : (j + 1) * rows, :] = jnp.sum(gates, axis=1, keepdims=True)

    for i in range(w_ref.shape[2] // chunk):
        part = pl.ds(i * chunk, chunk)
        result = jnp.dot(picked[...], w_ref[0, :, part], preferred_element_type=jnp.float32)
        scaled = result.astype(jnp.bfloat16).astype(jnp.float32) * scale[...]
        scaled = scaled.astype(jnp.bfloat16)
        start = 0
        for out_ref in out_refs:
            out_ref[:, part] = scaled[start : start + out_ref.shape[0]]
            start += out_ref.shape[0]


def down_call(hidden, places, down_weight, groups, rows, text_rows, seq_count, experts):
    _, ff, wide = down_weight.shape
    total = sum(len(group) for group in groups) * rows
    here = pl.BlockSpec(memory_space=pltpu.VMEM)
    return pl.pallas_call(
        functools.partial(down_kernel, groups, rows, text_rows, seq_count, experts, 512),
        grid_spec=pltpu.PrefetchScalarGridSpec(
            num_scalar_prefetch=1,
            grid=(1,),
            in_specs=[here] * 2,
            out_specs=[here] * len(groups),
            scratch_shapes=[
                pltpu.VMEM((seq_count * (rows - text_rows), hidden.shape[1]), jnp.bfloat16),
                pltpu.VMEM((total, ff), jnp.bfloat16),
                pltpu.VMEM((total, 1), jnp.float32),
            ],
        ),
        out_shape=[pltpu.VMEM((len(group) * rows, wide), jnp.bfloat16) for group in groups],
        compiler_params=pltpu.CompilerParams(vmem_limit_bytes=14 * 1024 * 1024),
        cost_estimate=pl.CostEstimate(
            flops=2 * total * wide * ff,
            bytes_accessed=2 * ff * wide + 2 * total * wide,
            transcendentals=0,
        ),
    )(places, kept(hidden), kept(down_weight))


def add_up(*parts):
    total = parts[0].astype(jnp.float32)
    for part in parts[1:]:
        total = total + part.astype(jnp.float32)
    return total.astype(jnp.bfloat16)


def ring_shards(
    text_tokens, panels, panel_target, expert_ids, gate_weights, gate_up_weight, down_weight
):
    seq_count, expert_count = lax.axis_size("seq"), lax.axis_size("expert")
    ring = Ring(seq_count, expert_count)
    text_rows, tok_count = text_tokens.shape[0], expert_ids.shape[0]
    me = lax.axis_index(AXES)

    def along(array):
        return lax.ppermute(array, AXES, ring.step())

    def across(array):
        return lax.ppermute(array, AXES, ring.swap())

    own = pack_call(
        text_tokens, panels, panel_target, expert_ids, gate_weights, ring.devices, expert_count
    )
    seq_of = ring.owner_of // expert_count
    numbers = np.arange(ring.devices, dtype=np.int32)[:, None]
    places = np.concatenate([numbers, seq_of, ring.sources_of.reshape(ring.devices, -1)], axis=1)
    places = jnp.asarray(places)[me]

    all_rows = ring.slot_count * tok_count

    def tied(*values):
        return lax.optimization_barrier(values)

    def rows_of(*slots):
        return [slot * tok_count for slot in slots]

    lead = along(own)
    other = across(own)
    own, places = tied(own, places)
    hidden, gate_up = hidden_call([own, other], rows_of(0, 1), gate_up_weight, None, all_rows)
    trail = along(other)
    hidden, lead = tied(hidden, lead)
    hidden, trail = tied(hidden, trail)
    swapped = swapped_rows = None
    for s in range(1, ring.half):
        next_lead = along(lead)
        lead_across = across(lead)
        if swapped:
            hidden, gate_up = hidden_call(swapped, swapped_rows, gate_up, hidden, all_rows)
            hidden, trail = tied(hidden, trail)
        next_trail = along(trail) if s + 1 < ring.half else None
        trail_across = across(trail)
        extra = down_weight if s == 1 else None
        hidden, gate_up, *down = hidden_call(
            [lead, trail], rows_of(4 * s, 4 * s + 1), gate_up, hidden, all_rows, extra
        )
        if down:
            (down_here,) = down
        hidden, lead, lead_across, trail_across = tied(
            hidden, next_lead, lead_across, trail_across
        )
        trail = next_trail
        swapped, swapped_rows = [lead_across, trail_across], rows_of(4 * s + 3, 4 * s + 2)
    far = [lead, across(lead)]
    hidden, gate_up = hidden_call(swapped, swapped_rows, gate_up, hidden, all_rows)
    (hidden,) = hidden_call(far, rows_of(2, 3), gate_up, hidden, all_rows, last=True)

    def outputs(hidden, *groups):
        return down_call(
            hidden, places, down_here, groups, tok_count, text_rows, seq_count, ring.devices
        )

    def for_other(hidden, s):
        first, *rest = outputs(hidden, *(((4 * s + 1,), (4 * s,)) if s else ((1,),)))
        first, hidden = tied(first, hidden)
        return [first, *rest], hidden

    def for_own(hidden, s):
        first, *rest = outputs(hidden, *(((4 * s + 2,), (4 * s + 3,)) if s else ((0,),)))
        first, hidden = tied(first, hidden)
        return [first, *rest], hidden

    def sent(hidden, *parts):
        total, hidden = tied(add_up(*parts), hidden)
        return along(total), hidden

    mine, others = outputs(hidden, (2,), (3,))
    mine, hidden = tied(mine, hidden)
    swapped, hidden = for_other(hidden, ring.half - 1)
    swapped = [across(array) for array in swapped]
    lead, hidden = sent(hidden, mine, across(others))
    mine, hidden = for_own(hidden, ring.half - 1)
    trail, hidden = sent(hidden, mine[1], swapped[1])
    for s in range(ring.half - 1, 0, -1):
        next_swapped, hidden = for_other(hidden, s - 1)
        if s > 1:
            next_swapped = [across(array) for array in next_swapped]
        lead, hidden = sent(hidden, mine[0], swapped[0], lead)
        mine, hidden = for_own(hidden, s - 1)
        swapped = next_swapped
        if s > 1:
            trail, hidden = sent(hidden, mine[1], swapped[1], trail)
    return add_up(mine[0], across(add_up(swapped[0], trail)), lead)


def solution(mesh):
    placed = (
        P(("groups", "seq", "expert"), "tensor"),
        P(("groups", "seq", "expert"), None, "tensor"),
        P(("groups", "seq", "expert")),
        P(("groups", "seq", "expert"), None),
        P(("groups", "seq", "expert"), None),
        P(("seq", "expert"), None, "tensor", None),
        P(("seq", "expert"), "tensor", None),
    )

    def chosen(*args):
        seq_count, expert_count = mesh.shape["seq"], mesh.shape["expert"]
        owners = seq_count * expert_count
        tok_count, top_count = args[3].shape[0] // (mesh.shape["groups"] * owners), args[3].shape[1]
        experts_all = args[5].shape[0]
        slot_rows = experts_all * slot_capacity(tok_count, top_count, experts_all)
        dense = owners * tok_count <= 2 * slot_rows
        ring = dense and mesh.shape["tensor"] == 1 and expert_count == 4 and experts_all == owners
        ring = ring and seq_count > 2
        body = ring_shards if ring else slot_shards
        return jax.shard_map(
            body,
            mesh=mesh,
            in_specs=placed,
            out_specs=P(("groups", "seq", "expert"), "tensor"),
            check_vma=False,
        )(*args)

    return chosen
```

```python
import functools

import jax
import jax.numpy as jnp
import numpy as np
from jax import lax
from jax.experimental import pallas as pl
from jax.experimental.pallas import tpu as pltpu
from jax.sharding import PartitionSpec as P

AXES = ("seq", "expert")


def slot_shards(
    text_tokens, panels, panel_target, expert_ids, gate_weights, gate_up_weight, down_weight
):
    seq_count = lax.axis_size("seq")
    expert_count = lax.axis_size("expert")
    owner_count = seq_count * expert_count
    pan_count = panels.shape[0]
    cap_panel = max(2, (3 * pan_count + 2 * seq_count - 1) // (2 * seq_count))
    slot_range = jnp.arange(pan_count, dtype=jnp.int32)
    owner_dev = panel_target // pan_count
    dest_seq = owner_dev // expert_count
    dest_slot = panel_target % pan_count
    onehot = (dest_seq[:, None] == jnp.arange(seq_count, dtype=jnp.int32)[None, :]).astype(
        jnp.int32
    )
    earlier = jnp.cumsum(onehot, axis=0) - onehot
    placing = dest_seq * cap_panel + jnp.sum(earlier * onehot, axis=1)
    outgoing = (
        jnp.zeros((seq_count * cap_panel,) + panels.shape[1:], panels.dtype).at[placing].set(panels)
    )
    labels = jnp.full((seq_count * cap_panel,), -1, jnp.int32).at[placing].set(dest_slot)
    arrived, arrived_labels = (
        lax.all_to_all(outgoing, "seq", split_axis=0, concat_axis=0, tiled=True),
        lax.all_to_all(labels, "seq", split_axis=0, concat_axis=0, tiled=True),
    )
    matches = (arrived_labels[None, :] == slot_range[:, None]).astype(jnp.bfloat16)
    image_rows = jnp.einsum(
        "qn,nrd->qrd", matches, arrived, preferred_element_type=jnp.float32
    ).astype(jnp.bfloat16)
    half_rows = jnp.concatenate([text_tokens, image_rows.reshape(-1, image_rows.shape[-1])], axis=0)
    tokens = lax.all_gather(half_rows, "tensor", axis=1, tiled=True)
    feature_width = tokens.shape[1]
    tok_count, top_count = expert_ids.shape
    experts_all = owner_count * gate_up_weight.shape[0]
    capacity = slot_capacity(tok_count, top_count, experts_all)
    flat_ids = expert_ids.reshape(-1)
    onehot_ids = (flat_ids[:, None] == jnp.arange(experts_all, dtype=jnp.int32)[None, :]).astype(
        jnp.int32
    )
    before = jnp.cumsum(onehot_ids, axis=0) - onehot_ids
    placing_ids = flat_ids * capacity + jnp.sum(before * onehot_ids, axis=1)
    source_rows = jnp.arange(tok_count * top_count, dtype=jnp.int32) // top_count
    outgoing_rows = (
        jnp.zeros((experts_all * capacity, feature_width), tokens.dtype)
        .at[placing_ids]
        .set(tokens[source_rows])
    )
    load_counts = jnp.sum(onehot_ids, axis=0).reshape(experts_all, 1)
    outgoing_rows = outgoing_rows.reshape(experts_all, capacity, feature_width)
    pair_weight = gate_up_weight[0]
    out_weight = down_weight[0]
    arrived_rows, arrived_loads = (
        lax.all_to_all(outgoing_rows, AXES, split_axis=0, concat_axis=0, tiled=True),
        lax.all_to_all(load_counts, AXES, split_axis=0, concat_axis=0, tiled=True),
    )
    arrived_rows = arrived_rows.reshape(-1, feature_width)
    slot_total = arrived_rows.shape[0]
    slot_index = jnp.arange(capacity, dtype=jnp.int32)
    is_live = (slot_index[None, :] < arrived_loads).reshape(-1)
    live_int = is_live.astype(jnp.int32)
    compact_at = jnp.cumsum(live_int) - live_int
    live_total = jnp.sum(live_int)
    compact_src = (
        jnp.zeros((slot_total,), jnp.int32)
        .at[jnp.where(is_live, compact_at, slot_total)]
        .set(jnp.arange(slot_total, dtype=jnp.int32), mode="drop")
    )

    def expert_block(block_no, partial_out):
        chosen = lax.dynamic_slice_in_dim(compact_src, block_no * 128, 128)
        block_rows = arrived_rows[chosen]
        gate_up = jnp.einsum(
            "rd,gfd->grf", block_rows, pair_weight, preferred_element_type=jnp.float32
        )
        hidden = (jax.nn.silu(gate_up[0]) * gate_up[1]).astype(jnp.bfloat16)
        result = jnp.dot(hidden, out_weight, preferred_element_type=jnp.float32)
        return lax.dynamic_update_slice_in_dim(partial_out, result, block_no * 128, 0)

    block_total = (live_total + 127) // 128
    padded_total = (slot_total + 127) // 128 * 128
    partial_out = lax.fori_loop(
        0, block_total, expert_block, jnp.zeros((padded_total, feature_width), jnp.float32)
    )
    summed = lax.psum_scatter(partial_out, "tensor", scatter_dimension=1, tiled=True).astype(
        jnp.bfloat16
    )
    out_width = summed.shape[1]
    returned = jnp.where(
        is_live[:, None], summed[jnp.where(is_live, compact_at, 0)], jnp.zeros((), jnp.bfloat16)
    )
    came_back = lax.all_to_all(
        returned.reshape(experts_all, capacity, out_width),
        AXES,
        split_axis=0,
        concat_axis=0,
        tiled=True,
    )
    half_width = came_back.shape[2]
    picked = came_back.reshape(-1, half_width)[placing_ids].reshape(
        tok_count, top_count, half_width
    )
    mixed_out = jnp.sum(gate_weights[:, :, None] * picked.astype(jnp.float32), axis=1)
    return mixed_out.astype(jnp.bfloat16)


def slot_capacity(tok_count, top_count, experts_all):
    return min(tok_count, (2 * tok_count * top_count // experts_all + 7) // 8 * 8)


class Ring:
    def __init__(self, seq_count, expert_count):
        self.seq, self.expert = seq_count, expert_count
        self.chips = 2 * seq_count
        self.half = seq_count
        self.devices = seq_count * expert_count
        self.slot_count = 4 * self.half
        self.owner_of = np.zeros((self.devices, self.slot_count), np.int32)
        self.sources_of = np.zeros((self.devices, self.slot_count, seq_count), np.int32)
        for d in range(self.devices):
            p, c = self.place(d)
            slots = [(0, 0), (0, 1), (self.half, 0), (self.half, 1)]
            for s in range(1, self.half):
                along = -s if c else s
                slots += [(-along, 0), (-along, 1), (along, 0), (along, 1)]
            slot_of = {(r % self.chips, k): i for i, (r, k) in enumerate(slots)}
            for i, (r, k) in enumerate(slots):
                q = (p + r) % self.chips
                self.owner_of[d, i] = self.device(q, c ^ k)
                x = q // seq_count
                for z in range(seq_count):
                    pos = z if x == 0 else self.chips - 1 - z
                    self.sources_of[d, i, z] = slot_of[((pos - p) % self.chips, k)]

    def place(self, d):
        z, e = divmod(d, self.expert)
        x, c = divmod(e, 2)
        return (z if x == 0 else self.chips - 1 - z), c

    def device(self, pos, c):
        x, z = (0, pos) if pos < self.seq else (1, self.chips - 1 - pos)
        return z * self.expert + x * 2 + c

    def step(self):
        pairs = []
        for d in range(self.devices):
            p, c = self.place(d)
            pairs.append((d, self.device((p + (-1 if c else 1)) % self.chips, c)))
        return pairs

    def swap(self):
        return [(d, d ^ 1) for d in range(self.devices)]


def kept(array):
    return pltpu.with_memory_space_constraint(array, pltpu.VMEM)


def distant(array):
    return pltpu.with_memory_space_constraint(array, pltpu.HBM)


def steps(count, unroll, body):
    if unroll:
        for i in range(count):
            body(i)
    else:
        pl.loop(0, count)(body)


def chunk_start(i, chunk):
    return i * chunk if isinstance(i, int) else pl.multiple_of(i * chunk, chunk)


def pack_kernel(
    experts, expert_count, text_ref, panels_ref, target_hbm, ids_hbm, gates_hbm, out_ref,
    target_ref, ids_ref, gates_ref, sems,
):
    text_rows, wide = text_ref.shape
    rows, width = out_ref.shape[0], out_ref.shape[1] - wide
    pan_count = target_ref.shape[1]
    panel_rows = (rows - text_rows) // pan_count
    copies = [
        pltpu.make_async_copy(text_ref, out_ref.at[:text_rows, :wide], sems.at[0]),
        pltpu.make_async_copy(panels_ref, out_ref.at[text_rows:, :wide], sems.at[1]),
    ]
    tables = [
        pltpu.make_async_copy(target_hbm, target_ref, sems.at[2]),
        pltpu.make_async_copy(ids_hbm, ids_ref, sems.at[3]),
        pltpu.make_async_copy(gates_hbm, gates_ref, sems.at[4]),
    ]
    for copy in tables + copies:
        copy.start()
    for copy in tables:
        copy.wait()
    lane = lax.broadcasted_iota(jnp.int32, (rows, width), 1)
    term = sum((lane >= i * experts).astype(jnp.int32) for i in range(1, 4))
    expert = (lane - term * experts).astype(jnp.float32)
    diagonal = lax.broadcasted_iota(jnp.int32, (rows, rows), 0) == lax.broadcasted_iota(
        jnp.int32, (rows, rows), 1
    )

    def upright(row):
        return jnp.sum(jnp.where(diagonal, row, 0.0), axis=1, keepdims=True)

    gate = jnp.zeros((rows, width), jnp.float32)
    for k in range(ids_ref.shape[0]):
        number = upright(ids_ref[k : k + 1, :].astype(jnp.float32))
        gate += jnp.where(number == expert, upright(gates_ref[k : k + 1, :]), 0.0)
    high = gate.astype(jnp.bfloat16).astype(jnp.float32)
    middle = (gate - high).astype(jnp.bfloat16).astype(jnp.float32)
    low = gate - high - middle
    panel = lax.broadcasted_iota(jnp.int32, (rows, pan_count), 1)
    row = lax.broadcasted_iota(jnp.int32, (rows, pan_count), 0) - text_rows
    past = row - panel * panel_rows
    mine = (past >= 0) & (past < panel_rows)
    target = jnp.sum(
        jnp.where(mine, target_ref[...].astype(jnp.float32), 0.0), axis=1, keepdims=True
    )
    within = jnp.sum(jnp.where(mine, past.astype(jnp.float32), 0.0), axis=1, keepdims=True)
    owner, seq = jnp.zeros_like(target), jnp.zeros_like(target)
    for i in range(1, experts):
        passed = jnp.where(target >= i * pan_count, 1.0, 0.0)
        owner += passed
        if i % expert_count == 0:
            seq += passed
    place = (target - owner * pan_count) * panel_rows + within
    tags = jnp.where(term == 0, high, jnp.where(term == 1, middle, jnp.where(term == 2, low, 0.0)))
    tags = jnp.where(lane == 3 * experts, seq, jnp.where(lane == 3 * experts + 1, place, tags))
    out_ref[:, wide:] = tags.astype(jnp.bfloat16)
    for copy in copies:
        copy.wait()


def pack_call(text_tokens, panels, panel_target, expert_ids, gate_weights, experts, expert_count):
    rows, wide = expert_ids.shape[0], text_tokens.shape[1]
    width = (3 * experts + 2 + 127) // 128 * 128
    here, far = pl.BlockSpec(memory_space=pltpu.VMEM), pl.BlockSpec(memory_space=pltpu.HBM)
    return pl.pallas_call(
        functools.partial(pack_kernel, experts, expert_count),
        in_specs=[far] * 5,
        out_specs=here,
        out_shape=pltpu.VMEM((rows, wide + width), jnp.bfloat16),
        scratch_shapes=[
            pltpu.VMEM((1, panel_target.shape[0]), jnp.int32),
            pltpu.VMEM(expert_ids.shape[::-1], jnp.int32),
            pltpu.VMEM(gate_weights.shape[::-1], jnp.float32),
            pltpu.SemaphoreType.DMA((5,)),
        ],
        compiler_params=pltpu.CompilerParams(vmem_limit_bytes=14 * 1024 * 1024),
    )(
        distant(text_tokens),
        distant(panels.reshape(-1, wide)),
        distant(panel_target[None, :]),
        distant(expert_ids.T),
        distant(gate_weights.T),
    )


def hidden_kernel(places, rows, chunk, fetch, unroll, *refs):
    x_refs, refs = refs[: len(places)], refs[len(places) :]
    if fetch == "gate_up":
        far_ref, out_ref, w_ref, x_all, sems = refs
    elif fetch == "down":
        w_ref, _, far_ref, out_ref, _, down_ref, x_all, sems = refs
    else:
        w_ref, _, out_ref, x_all = refs[0], refs[1], refs[2], refs[-1]
    ff, wide = w_ref.shape[2:]
    whole, rest = divmod(ff, chunk)

    def fetched(i, width):
        part = pl.ds(pl.multiple_of(i * chunk, chunk), width)
        return pltpu.make_async_copy(far_ref.at[0, :, part], w_ref.at[0, :, part], sems.at[i])

    if fetch == "gate_up":
        for i in range(whole):
            fetched(i, chunk).start()
        if rest:
            fetched(whole, rest).start()
    if fetch == "down":
        pltpu.make_async_copy(far_ref, down_ref, sems.at[0]).start()
    for i, at in enumerate(places):
        x_all[i * rows : (i + 1) * rows, :] = x_refs[i][:, :wide]
        out_ref[at : at + rows, ff:] = x_refs[i][:, wide:]

    def step(i, width):
        if fetch == "gate_up":
            fetched(i, width).wait()
        part = pl.ds(chunk_start(i, chunk), width)
        weight = w_ref[0, :, part, :].reshape(2 * width, wide)
        both = lax.dot_general(
            x_all[...], weight, (((1,), (1,)), ((), ())), preferred_element_type=jnp.float32
        )
        gate, up = both[:, :width], both[:, width:]
        gate = 0.5 * gate
        hidden = (gate * (1.0 + jnp.tanh(gate)) * up).astype(out_ref.dtype)
        for i, at in enumerate(places):
            out_ref[at : at + rows, part] = hidden[i * rows : (i + 1) * rows]

    def full_step(i):
        step(i, chunk)

    steps(whole, unroll, full_step)
    if rest:
        step(whole, rest)
    if fetch == "down":
        pltpu.make_async_copy(far_ref, down_ref, sems.at[0]).wait()


def hidden_call(
    blocks, places, gate_up_weight, hidden, all_rows, down_weight=None, last=False, unroll=False
):
    rows, width = blocks[0].shape
    ff, wide = gate_up_weight.shape[2:]
    count = len(blocks)
    chunk = 256
    here, far = pl.BlockSpec(memory_space=pltpu.VMEM), pl.BlockSpec(memory_space=pltpu.HBM)
    args, in_specs = [kept(block) for block in blocks], [here] * count
    out_shape, aliases = [pltpu.VMEM((all_rows, ff + width - wide), jnp.bfloat16)], {}
    scratch = [pltpu.VMEM((count * rows, wide), jnp.bfloat16)]
    fetch = None
    if hidden is None:
        fetch = "gate_up"
        args, in_specs = args + [distant(gate_up_weight)], in_specs + [far]
        out_shape.append(pltpu.VMEM(gate_up_weight.shape, gate_up_weight.dtype))
        scratch.append(pltpu.SemaphoreType.DMA((pl.cdiv(ff, chunk),)))
    else:
        args, in_specs = args + [kept(gate_up_weight), kept(hidden)], in_specs + [here, here]
        aliases = {count + 1: 0}
        if not last:
            out_shape.append(pltpu.VMEM(gate_up_weight.shape, gate_up_weight.dtype))
            aliases[count] = 1
        if down_weight is not None:
            fetch = "down"
            args, in_specs = args + [distant(down_weight)], in_specs + [far]
            out_shape.append(pltpu.VMEM(down_weight.shape, down_weight.dtype))
            scratch.append(pltpu.SemaphoreType.DMA((1,)))
    return pl.pallas_call(
        functools.partial(hidden_kernel, tuple(places), rows, chunk, fetch, unroll),
        in_specs=in_specs,
        out_specs=[here] * len(out_shape),
        out_shape=out_shape,
        scratch_shapes=scratch,
        input_output_aliases=aliases,
        compiler_params=pltpu.CompilerParams(vmem_limit_bytes=14 * 1024 * 1024),
        cost_estimate=pl.CostEstimate(
            flops=4 * count * rows * wide * ff,
            bytes_accessed=4 * ff * wide + 2 * count * rows * (wide + ff),
            transcendentals=count * rows * ff,
        ),
    )(*args)


def down_kernel(
    groups, rows, text_rows, seq_count, experts, chunk, unroll, places_ref, hidden_ref, w_ref, *refs
):
    out_refs, (column, picked, scale) = refs[:-3], refs[-3:]
    slots = [slot for group in groups for slot in group]
    image_rows = rows - text_rows
    slot_total = hidden_ref.shape[0] // rows
    ff = w_ref.shape[1]
    width = hidden_ref.shape[1] - ff
    expert = places_ref[0]
    lane = lax.broadcasted_iota(jnp.int32, (1, width), 1)
    is_gate = (lane == expert) | (lane == expert + experts) | (lane == expert + 2 * experts)
    place_of = jnp.where(lane == 3 * experts, float(image_rows), 0.0)
    place_of = jnp.where(lane == 3 * experts + 1, 1.0, place_of)
    wanted = lax.broadcasted_iota(jnp.int32, (1, image_rows), 1)
    for j, slot in enumerate(slots):
        at = slot * rows
        picked[j * rows : j * rows + text_rows, :] = hidden_ref[at : at + text_rows, :ff]
        for z in range(seq_count):
            source = places_ref[1 + slot_total + slot * seq_count + z]
            start = pl.multiple_of(source * rows + text_rows, 16)
            column[z * image_rows : (z + 1) * image_rows, :] = hidden_ref[
                pl.ds(start, image_rows), :
            ]
        place = column[:, ff:].astype(jnp.float32) * place_of
        place = jnp.sum(place, axis=1, keepdims=True)
        first = places_ref[1 + slot] * image_rows
        match = jnp.where(place == (wanted + first).astype(jnp.float32), 1.0, 0.0)
        rows_here = lax.dot_general(
            match.astype(jnp.bfloat16),
            column[:, :ff],
            (((0,), (0,)), ((), ())),
            preferred_element_type=jnp.float32,
        )
        picked[j * rows + text_rows : (j + 1) * rows, :] = rows_here.astype(jnp.bfloat16)
        gates = jnp.where(is_gate, hidden_ref[at : at + rows, ff:].astype(jnp.float32), 0.0)
        scale[j * rows : (j + 1) * rows, :] = jnp.sum(gates, axis=1, keepdims=True)

    def step(i):
        part = pl.ds(chunk_start(i, chunk), chunk)
        result = jnp.dot(picked[...], w_ref[0, :, part], preferred_element_type=jnp.float32)
        scaled = result.astype(jnp.bfloat16).astype(jnp.float32) * scale[...]
        scaled = scaled.astype(jnp.bfloat16)
        start = 0
        for out_ref in out_refs:
            out_ref[:, part] = scaled[start : start + out_ref.shape[0]]
            start += out_ref.shape[0]

    steps(w_ref.shape[2] // chunk, unroll, step)


def down_call(
    hidden, places, down_weight, groups, rows, text_rows, seq_count, experts, unroll
):
    _, ff, wide = down_weight.shape
    total = sum(len(group) for group in groups) * rows
    here = pl.BlockSpec(memory_space=pltpu.VMEM)
    return pl.pallas_call(
        functools.partial(
            down_kernel, groups, rows, text_rows, seq_count, experts, 512, unroll
        ),
        grid_spec=pltpu.PrefetchScalarGridSpec(
            num_scalar_prefetch=1,
            grid=(1,),
            in_specs=[here] * 2,
            out_specs=[here] * len(groups),
            scratch_shapes=[
                pltpu.VMEM((seq_count * (rows - text_rows), hidden.shape[1]), jnp.bfloat16),
                pltpu.VMEM((total, ff), jnp.bfloat16),
                pltpu.VMEM((total, 1), jnp.float32),
            ],
        ),
        out_shape=[pltpu.VMEM((len(group) * rows, wide), jnp.bfloat16) for group in groups],
        compiler_params=pltpu.CompilerParams(vmem_limit_bytes=14 * 1024 * 1024),
        cost_estimate=pl.CostEstimate(
            flops=2 * total * wide * ff,
            bytes_accessed=2 * ff * wide + 2 * total * wide,
            transcendentals=0,
        ),
    )(places, kept(hidden), kept(down_weight))


def add_up(*parts):
    total = parts[0].astype(jnp.float32)
    for part in parts[1:]:
        total = total + part.astype(jnp.float32)
    return total.astype(jnp.bfloat16)


def ring_shards(
    text_tokens, panels, panel_target, expert_ids, gate_weights, gate_up_weight, down_weight
):
    seq_count, expert_count = lax.axis_size("seq"), lax.axis_size("expert")
    ring = Ring(seq_count, expert_count)
    text_rows, tok_count = text_tokens.shape[0], expert_ids.shape[0]
    me = lax.axis_index(AXES)

    def along(array):
        return lax.ppermute(array, AXES, ring.step())

    def across(array):
        return lax.ppermute(array, AXES, ring.swap())

    own = pack_call(
        text_tokens, panels, panel_target, expert_ids, gate_weights, ring.devices, expert_count
    )
    seq_of = ring.owner_of // expert_count
    numbers = np.arange(ring.devices, dtype=np.int32)[:, None]
    places = np.concatenate([numbers, seq_of, ring.sources_of.reshape(ring.devices, -1)], axis=1)
    places = jnp.asarray(places)[me]

    all_rows = ring.slot_count * tok_count

    def tied(*values):
        return lax.optimization_barrier(values)

    def rows_of(*slots):
        return [slot * tok_count for slot in slots]

    lead = along(own)
    other = across(own)
    own, places = tied(own, places)
    hidden, gate_up = hidden_call([own, other], rows_of(0, 1), gate_up_weight, None, all_rows)
    trail = along(other)
    hidden, lead = tied(hidden, lead)
    hidden, trail = tied(hidden, trail)
    swapped = swapped_rows = None
    for s in range(1, ring.half):
        next_lead = along(lead)
        lead_across = across(lead)
        if swapped:
            hidden, gate_up = hidden_call(swapped, swapped_rows, gate_up, hidden, all_rows)
            hidden, trail = tied(hidden, trail)
        next_trail = along(trail) if s + 1 < ring.half else None
        trail_across = across(trail)
        extra = down_weight if s == 1 else None
        hidden, gate_up, *down = hidden_call(
            [lead, trail], rows_of(4 * s, 4 * s + 1), gate_up, hidden, all_rows, extra,
            unroll=s + 1 == ring.half,
        )
        if down:
            (down_here,) = down
        hidden, lead, lead_across, trail_across = tied(
            hidden, next_lead, lead_across, trail_across
        )
        trail = next_trail
        swapped, swapped_rows = [lead_across, trail_across], rows_of(4 * s + 3, 4 * s + 2)
    hidden, gate_up = hidden_call(swapped, swapped_rows, gate_up, hidden, all_rows, unroll=True)
    far = [lead, across(lead)]
    (hidden,) = hidden_call(
        far, rows_of(2, 3), gate_up, hidden, all_rows, last=True, unroll=True
    )

    def outputs(hidden, *groups, unroll=False):
        return down_call(
            hidden, places, down_here, groups, tok_count, text_rows, seq_count, ring.devices, unroll
        )

    def for_other(hidden, s):
        groups = ((4 * s + 1,), (4 * s,)) if s else ((1,),)
        first, *rest = outputs(hidden, *groups, unroll=s + 2 >= ring.half)
        first, hidden = tied(first, hidden)
        return [first, *rest], hidden

    def for_own(hidden, s):
        groups = ((4 * s + 2,), (4 * s + 3,)) if s else ((0,),)
        first, *rest = outputs(hidden, *groups, unroll=s + 1 >= ring.half)
        first, hidden = tied(first, hidden)
        return [first, *rest], hidden

    def sent(hidden, *parts):
        total, hidden = tied(add_up(*parts), hidden)
        return along(total), hidden

    mine, others = outputs(hidden, (2,), (3,), unroll=True)
    mine, hidden = tied(mine, hidden)
    swapped, hidden = for_other(hidden, ring.half - 1)
    swapped = [across(array) for array in swapped]
    lead, hidden = sent(hidden, mine, across(others))
    mine, hidden = for_own(hidden, ring.half - 1)
    trail, hidden = sent(hidden, mine[1], swapped[1])
    for s in range(ring.half - 1, 0, -1):
        next_swapped, hidden = for_other(hidden, s - 1)
        if s > 1:
            next_swapped = [across(array) for array in next_swapped]
        lead, hidden = sent(hidden, mine[0], swapped[0], lead)
        mine, hidden = for_own(hidden, s - 1)
        swapped = next_swapped
        if s > 1:
            trail, hidden = sent(hidden, mine[1], swapped[1], trail)
    return add_up(mine[0], across(add_up(swapped[0], trail)), lead)


def solution(mesh):
    placed = (
        P(("groups", "seq", "expert"), "tensor"),
        P(("groups", "seq", "expert"), None, "tensor"),
        P(("groups", "seq", "expert")),
        P(("groups", "seq", "expert"), None),
        P(("groups", "seq", "expert"), None),
        P(("seq", "expert"), None, "tensor", None),
        P(("seq", "expert"), "tensor", None),
    )

    def chosen(*args):
        seq_count, expert_count = mesh.shape["seq"], mesh.shape["expert"]
        owners = seq_count * expert_count
        tok_count, top_count = args[3].shape[0] // (mesh.shape["groups"] * owners), args[3].shape[1]
        experts_all = args[5].shape[0]
        slot_rows = experts_all * slot_capacity(tok_count, top_count, experts_all)
        dense = owners * tok_count <= 2 * slot_rows
        ring = dense and mesh.shape["tensor"] == 1 and expert_count == 4 and experts_all == owners
        ring = ring and seq_count > 2
        body = ring_shards if ring else slot_shards
        return jax.shard_map(
            body,
            mesh=mesh,
            in_specs=placed,
            out_specs=P(("groups", "seq", "expert"), "tensor"),
            check_vma=False,
        )(*args)

    return chosen
```

```python
import functools

import jax
import jax.numpy as jnp
import numpy as np
from jax import lax
from jax.experimental import pallas as pl
from jax.experimental.pallas import tpu as pltpu
from jax.sharding import PartitionSpec as P

AXES = ("seq", "expert")


def slot_shards(
    text_tokens, panels, panel_target, expert_ids, gate_weights, gate_up_weight, down_weight
):
    seq_count = lax.axis_size("seq")
    expert_count = lax.axis_size("expert")
    owner_count = seq_count * expert_count
    pan_count = panels.shape[0]
    cap_panel = max(2, (3 * pan_count + 2 * seq_count - 1) // (2 * seq_count))
    slot_range = jnp.arange(pan_count, dtype=jnp.int32)
    owner_dev = panel_target // pan_count
    dest_seq = owner_dev // expert_count
    dest_slot = panel_target % pan_count
    onehot = (dest_seq[:, None] == jnp.arange(seq_count, dtype=jnp.int32)[None, :]).astype(
        jnp.int32
    )
    earlier = jnp.cumsum(onehot, axis=0) - onehot
    placing = dest_seq * cap_panel + jnp.sum(earlier * onehot, axis=1)
    outgoing = (
        jnp.zeros((seq_count * cap_panel,) + panels.shape[1:], panels.dtype).at[placing].set(panels)
    )
    labels = jnp.full((seq_count * cap_panel,), -1, jnp.int32).at[placing].set(dest_slot)
    arrived, arrived_labels = (
        lax.all_to_all(outgoing, "seq", split_axis=0, concat_axis=0, tiled=True),
        lax.all_to_all(labels, "seq", split_axis=0, concat_axis=0, tiled=True),
    )
    matches = (arrived_labels[None, :] == slot_range[:, None]).astype(jnp.bfloat16)
    image_rows = jnp.einsum(
        "qn,nrd->qrd", matches, arrived, preferred_element_type=jnp.float32
    ).astype(jnp.bfloat16)
    half_rows = jnp.concatenate([text_tokens, image_rows.reshape(-1, image_rows.shape[-1])], axis=0)
    tokens = lax.all_gather(half_rows, "tensor", axis=1, tiled=True)
    feature_width = tokens.shape[1]
    tok_count, top_count = expert_ids.shape
    experts_all = owner_count * gate_up_weight.shape[0]
    capacity = slot_capacity(tok_count, top_count, experts_all)
    flat_ids = expert_ids.reshape(-1)
    onehot_ids = (flat_ids[:, None] == jnp.arange(experts_all, dtype=jnp.int32)[None, :]).astype(
        jnp.int32
    )
    before = jnp.cumsum(onehot_ids, axis=0) - onehot_ids
    placing_ids = flat_ids * capacity + jnp.sum(before * onehot_ids, axis=1)
    source_rows = jnp.arange(tok_count * top_count, dtype=jnp.int32) // top_count
    outgoing_rows = (
        jnp.zeros((experts_all * capacity, feature_width), tokens.dtype)
        .at[placing_ids]
        .set(tokens[source_rows])
    )
    load_counts = jnp.sum(onehot_ids, axis=0).reshape(experts_all, 1)
    outgoing_rows = outgoing_rows.reshape(experts_all, capacity, feature_width)
    pair_weight = gate_up_weight[0]
    out_weight = down_weight[0]
    arrived_rows, arrived_loads = (
        lax.all_to_all(outgoing_rows, AXES, split_axis=0, concat_axis=0, tiled=True),
        lax.all_to_all(load_counts, AXES, split_axis=0, concat_axis=0, tiled=True),
    )
    arrived_rows = arrived_rows.reshape(-1, feature_width)
    slot_total = arrived_rows.shape[0]
    slot_index = jnp.arange(capacity, dtype=jnp.int32)
    is_live = (slot_index[None, :] < arrived_loads).reshape(-1)
    live_int = is_live.astype(jnp.int32)
    compact_at = jnp.cumsum(live_int) - live_int
    live_total = jnp.sum(live_int)
    compact_src = (
        jnp.zeros((slot_total,), jnp.int32)
        .at[jnp.where(is_live, compact_at, slot_total)]
        .set(jnp.arange(slot_total, dtype=jnp.int32), mode="drop")
    )

    def expert_block(block_no, partial_out):
        chosen = lax.dynamic_slice_in_dim(compact_src, block_no * 128, 128)
        block_rows = arrived_rows[chosen]
        gate_up = jnp.einsum(
            "rd,gfd->grf", block_rows, pair_weight, preferred_element_type=jnp.float32
        )
        hidden = (jax.nn.silu(gate_up[0]) * gate_up[1]).astype(jnp.bfloat16)
        result = jnp.dot(hidden, out_weight, preferred_element_type=jnp.float32)
        return lax.dynamic_update_slice_in_dim(partial_out, result, block_no * 128, 0)

    block_total = (live_total + 127) // 128
    padded_total = (slot_total + 127) // 128 * 128
    partial_out = lax.fori_loop(
        0, block_total, expert_block, jnp.zeros((padded_total, feature_width), jnp.float32)
    )
    summed = lax.psum_scatter(partial_out, "tensor", scatter_dimension=1, tiled=True).astype(
        jnp.bfloat16
    )
    out_width = summed.shape[1]
    returned = jnp.where(
        is_live[:, None], summed[jnp.where(is_live, compact_at, 0)], jnp.zeros((), jnp.bfloat16)
    )
    came_back = lax.all_to_all(
        returned.reshape(experts_all, capacity, out_width),
        AXES,
        split_axis=0,
        concat_axis=0,
        tiled=True,
    )
    half_width = came_back.shape[2]
    picked = came_back.reshape(-1, half_width)[placing_ids].reshape(
        tok_count, top_count, half_width
    )
    mixed_out = jnp.sum(gate_weights[:, :, None] * picked.astype(jnp.float32), axis=1)
    return mixed_out.astype(jnp.bfloat16)


def slot_capacity(tok_count, top_count, experts_all):
    return min(tok_count, (2 * tok_count * top_count // experts_all + 7) // 8 * 8)


class Ring:
    def __init__(self, seq_count, expert_count):
        self.seq, self.expert = seq_count, expert_count
        self.chips = 2 * seq_count
        self.half = seq_count
        self.devices = seq_count * expert_count
        self.slot_count = 4 * self.half
        self.owner_of = np.zeros((self.devices, self.slot_count), np.int32)
        self.sources_of = np.zeros((self.devices, self.slot_count, seq_count), np.int32)
        for d in range(self.devices):
            p, c = self.place(d)
            slots = [(0, 0), (0, 1), (self.half, 0), (self.half, 1)]
            for s in range(1, self.half):
                along = -s if c else s
                slots += [(-along, 0), (-along, 1), (along, 0), (along, 1)]
            slot_of = {(r % self.chips, k): i for i, (r, k) in enumerate(slots)}
            for i, (r, k) in enumerate(slots):
                q = (p + r) % self.chips
                self.owner_of[d, i] = self.device(q, c ^ k)
                x = q // seq_count
                for z in range(seq_count):
                    pos = z if x == 0 else self.chips - 1 - z
                    self.sources_of[d, i, z] = slot_of[((pos - p) % self.chips, k)]

    def place(self, d):
        z, e = divmod(d, self.expert)
        x, c = divmod(e, 2)
        return (z if x == 0 else self.chips - 1 - z), c

    def device(self, pos, c):
        x, z = (0, pos) if pos < self.seq else (1, self.chips - 1 - pos)
        return z * self.expert + x * 2 + c

    def step(self):
        pairs = []
        for d in range(self.devices):
            p, c = self.place(d)
            pairs.append((d, self.device((p + (-1 if c else 1)) % self.chips, c)))
        return pairs

    def swap(self):
        return [(d, d ^ 1) for d in range(self.devices)]


def kept(array):
    return pltpu.with_memory_space_constraint(array, pltpu.VMEM)


def distant(array):
    return pltpu.with_memory_space_constraint(array, pltpu.HBM)


def steps(count, unroll, body):
    if unroll:
        for i in range(count):
            body(i)
    else:
        pl.loop(0, count)(body)


def chunk_start(i, chunk):
    return i * chunk if isinstance(i, int) else pl.multiple_of(i * chunk, chunk)


def pack_kernel(
    experts, expert_count, text_ref, panels_ref, target_hbm, ids_hbm, gates_hbm, out_ref,
    target_ref, ids_ref, gates_ref, sems,
):
    text_rows, wide = text_ref.shape
    rows, width = out_ref.shape[0], out_ref.shape[1] - wide
    pan_count = target_ref.shape[1]
    panel_rows = (rows - text_rows) // pan_count
    copies = [
        pltpu.make_async_copy(text_ref, out_ref.at[:text_rows, :wide], sems.at[0]),
        pltpu.make_async_copy(panels_ref, out_ref.at[text_rows:, :wide], sems.at[1]),
    ]
    tables = [
        pltpu.make_async_copy(target_hbm, target_ref, sems.at[2]),
        pltpu.make_async_copy(ids_hbm, ids_ref, sems.at[3]),
        pltpu.make_async_copy(gates_hbm, gates_ref, sems.at[4]),
    ]
    for copy in tables + copies:
        copy.start()
    for copy in tables:
        copy.wait()
    lane = lax.broadcasted_iota(jnp.int32, (rows, width), 1)
    term = sum((lane >= i * experts).astype(jnp.int32) for i in range(1, 4))
    expert = (lane - term * experts).astype(jnp.float32)
    diagonal = lax.broadcasted_iota(jnp.int32, (rows, rows), 0) == lax.broadcasted_iota(
        jnp.int32, (rows, rows), 1
    )

    def upright(row):
        return jnp.sum(jnp.where(diagonal, row, 0.0), axis=1, keepdims=True)

    gate = jnp.zeros((rows, width), jnp.float32)
    for k in range(ids_ref.shape[0]):
        number = upright(ids_ref[k : k + 1, :].astype(jnp.float32))
        gate += jnp.where(number == expert, upright(gates_ref[k : k + 1, :]), 0.0)
    high = gate.astype(jnp.bfloat16).astype(jnp.float32)
    middle = (gate - high).astype(jnp.bfloat16).astype(jnp.float32)
    low = gate - high - middle
    panel = lax.broadcasted_iota(jnp.int32, (rows, pan_count), 1)
    row = lax.broadcasted_iota(jnp.int32, (rows, pan_count), 0) - text_rows
    past = row - panel * panel_rows
    mine = (past >= 0) & (past < panel_rows)
    target = jnp.sum(
        jnp.where(mine, target_ref[...].astype(jnp.float32), 0.0), axis=1, keepdims=True
    )
    within = jnp.sum(jnp.where(mine, past.astype(jnp.float32), 0.0), axis=1, keepdims=True)
    owner, seq = jnp.zeros_like(target), jnp.zeros_like(target)
    for i in range(1, experts):
        passed = jnp.where(target >= i * pan_count, 1.0, 0.0)
        owner += passed
        if i % expert_count == 0:
            seq += passed
    place = (target - owner * pan_count) * panel_rows + within
    tags = jnp.where(term == 0, high, jnp.where(term == 1, middle, jnp.where(term == 2, low, 0.0)))
    tags = jnp.where(lane == 3 * experts, seq, jnp.where(lane == 3 * experts + 1, place, tags))
    out_ref[:, wide:] = tags.astype(jnp.bfloat16)
    for copy in copies:
        copy.wait()


def pack_call(text_tokens, panels, panel_target, expert_ids, gate_weights, experts, expert_count):
    rows, wide = expert_ids.shape[0], text_tokens.shape[1]
    width = (3 * experts + 2 + 127) // 128 * 128
    here, far = pl.BlockSpec(memory_space=pltpu.VMEM), pl.BlockSpec(memory_space=pltpu.HBM)
    return pl.pallas_call(
        functools.partial(pack_kernel, experts, expert_count),
        in_specs=[far] * 5,
        out_specs=here,
        out_shape=pltpu.VMEM((rows, wide + width), jnp.bfloat16),
        scratch_shapes=[
            pltpu.VMEM((1, panel_target.shape[0]), jnp.int32),
            pltpu.VMEM(expert_ids.shape[::-1], jnp.int32),
            pltpu.VMEM(gate_weights.shape[::-1], jnp.float32),
            pltpu.SemaphoreType.DMA((5,)),
        ],
        compiler_params=pltpu.CompilerParams(vmem_limit_bytes=14 * 1024 * 1024),
    )(
        distant(text_tokens),
        distant(panels.reshape(-1, wide)),
        distant(panel_target[None, :]),
        distant(expert_ids.T),
        distant(gate_weights.T),
    )


def hidden_kernel(places, rows, chunk, fetch, unroll, *refs):
    x_refs, refs = refs[: len(places)], refs[len(places) :]
    if fetch == "gate_up":
        far_ref, out_ref, w_ref, x_all, sems = refs
    elif fetch == "down":
        w_ref, _, far_ref, out_ref, _, down_ref, x_all, sems = refs
    else:
        w_ref, _, out_ref, x_all = refs[0], refs[1], refs[2], refs[-1]
    ff, wide = w_ref.shape[2:]
    whole, rest = divmod(ff, chunk)

    def fetched(i, width):
        part = pl.ds(pl.multiple_of(i * chunk, chunk), width)
        return pltpu.make_async_copy(far_ref.at[0, :, part], w_ref.at[0, :, part], sems.at[i])

    if fetch == "gate_up":
        for i in range(whole):
            fetched(i, chunk).start()
        if rest:
            fetched(whole, rest).start()
    if fetch == "down":
        pltpu.make_async_copy(far_ref, down_ref, sems.at[0]).start()
    for i, at in enumerate(places):
        x_all[i * rows : (i + 1) * rows, :] = x_refs[i][:, :wide]
        out_ref[at : at + rows, ff:] = x_refs[i][:, wide:]

    def step(i, width):
        if fetch == "gate_up":
            fetched(i, width).wait()
        part = pl.ds(chunk_start(i, chunk), width)
        weight = w_ref[0, :, part, :].reshape(2 * width, wide)
        both = lax.dot_general(
            x_all[...], weight, (((1,), (1,)), ((), ())), preferred_element_type=jnp.float32
        )
        gate, up = both[:, :width], both[:, width:]
        gate = 0.5 * gate
        hidden = (gate * (1.0 + jnp.tanh(gate)) * up).astype(out_ref.dtype)
        for i, at in enumerate(places):
            out_ref[at : at + rows, part] = hidden[i * rows : (i + 1) * rows]

    def full_step(i):
        step(i, chunk)

    steps(whole, unroll, full_step)
    if rest:
        step(whole, rest)
    if fetch == "down":
        pltpu.make_async_copy(far_ref, down_ref, sems.at[0]).wait()


def hidden_call(
    blocks, places, gate_up_weight, hidden, all_rows, down_weight=None, last=False, unroll=False
):
    rows, width = blocks[0].shape
    ff, wide = gate_up_weight.shape[2:]
    count = len(blocks)
    chunk = 256
    here, far = pl.BlockSpec(memory_space=pltpu.VMEM), pl.BlockSpec(memory_space=pltpu.HBM)
    args, in_specs = [kept(block) for block in blocks], [here] * count
    out_shape, aliases = [pltpu.VMEM((all_rows, ff + width - wide), jnp.bfloat16)], {}
    scratch = [pltpu.VMEM((count * rows, wide), jnp.bfloat16)]
    fetch = None
    if hidden is None:
        fetch = "gate_up"
        args, in_specs = args + [distant(gate_up_weight)], in_specs + [far]
        out_shape.append(pltpu.VMEM(gate_up_weight.shape, gate_up_weight.dtype))
        scratch.append(pltpu.SemaphoreType.DMA((pl.cdiv(ff, chunk),)))
    else:
        args, in_specs = args + [kept(gate_up_weight), kept(hidden)], in_specs + [here, here]
        aliases = {count + 1: 0}
        if not last:
            out_shape.append(pltpu.VMEM(gate_up_weight.shape, gate_up_weight.dtype))
            aliases[count] = 1
        if down_weight is not None:
            fetch = "down"
            args, in_specs = args + [distant(down_weight)], in_specs + [far]
            out_shape.append(pltpu.VMEM(down_weight.shape, down_weight.dtype))
            scratch.append(pltpu.SemaphoreType.DMA((1,)))
    return pl.pallas_call(
        functools.partial(hidden_kernel, tuple(places), rows, chunk, fetch, unroll),
        in_specs=in_specs,
        out_specs=[here] * len(out_shape),
        out_shape=out_shape,
        scratch_shapes=scratch,
        input_output_aliases=aliases,
        compiler_params=pltpu.CompilerParams(vmem_limit_bytes=14 * 1024 * 1024),
        cost_estimate=pl.CostEstimate(
            flops=4 * count * rows * wide * ff,
            bytes_accessed=4 * ff * wide + 2 * count * rows * (wide + ff),
            transcendentals=count * rows * ff,
        ),
    )(*args)


def down_kernel(
    groups, rows, text_rows, seq_count, experts, chunk, unroll, places_ref, hidden_ref, w_ref, *refs
):
    out_refs, (column, picked, scale) = refs[:-3], refs[-3:]
    slots = [slot for group in groups for slot in group]
    image_rows = rows - text_rows
    slot_total = hidden_ref.shape[0] // rows
    ff = w_ref.shape[1]
    width = hidden_ref.shape[1] - ff
    expert = places_ref[0]
    lane = lax.broadcasted_iota(jnp.int32, (1, width), 1)
    is_gate = (lane == expert) | (lane == expert + experts) | (lane == expert + 2 * experts)
    place_of = jnp.where(lane == 3 * experts, float(image_rows), 0.0)
    place_of = jnp.where(lane == 3 * experts + 1, 1.0, place_of)
    wanted = lax.broadcasted_iota(jnp.int32, (1, image_rows), 1)
    for j, slot in enumerate(slots):
        at = slot * rows
        picked[j * rows : j * rows + text_rows, :] = hidden_ref[at : at + text_rows, :ff]
        for z in range(seq_count):
            source = places_ref[1 + slot_total + slot * seq_count + z]
            start = pl.multiple_of(source * rows + text_rows, 16)
            column[z * image_rows : (z + 1) * image_rows, :] = hidden_ref[
                pl.ds(start, image_rows), :
            ]
        place = column[:, ff:].astype(jnp.float32) * place_of
        place = jnp.sum(place, axis=1, keepdims=True)
        first = places_ref[1 + slot] * image_rows
        match = jnp.where(place == (wanted + first).astype(jnp.float32), 1.0, 0.0)
        rows_here = lax.dot_general(
            match.astype(jnp.bfloat16),
            column[:, :ff],
            (((0,), (0,)), ((), ())),
            preferred_element_type=jnp.float32,
        )
        picked[j * rows + text_rows : (j + 1) * rows, :] = rows_here.astype(jnp.bfloat16)
        gates = jnp.where(is_gate, hidden_ref[at : at + rows, ff:].astype(jnp.float32), 0.0)
        scale[j * rows : (j + 1) * rows, :] = jnp.sum(gates, axis=1, keepdims=True)

    def step(i):
        part = pl.ds(chunk_start(i, chunk), chunk)
        result = jnp.dot(picked[...], w_ref[0, :, part], preferred_element_type=jnp.float32)
        scaled = result.astype(jnp.bfloat16).astype(jnp.float32) * scale[...]
        scaled = scaled.astype(jnp.bfloat16)
        start = 0
        for out_ref in out_refs:
            out_ref[:, part] = scaled[start : start + out_ref.shape[0]]
            start += out_ref.shape[0]

    steps(w_ref.shape[2] // chunk, unroll, step)


def down_call(
    hidden, places, down_weight, groups, rows, text_rows, seq_count, experts, unroll
):
    _, ff, wide = down_weight.shape
    total = sum(len(group) for group in groups) * rows
    here = pl.BlockSpec(memory_space=pltpu.VMEM)
    return pl.pallas_call(
        functools.partial(
            down_kernel, groups, rows, text_rows, seq_count, experts, 512, unroll
        ),
        grid_spec=pltpu.PrefetchScalarGridSpec(
            num_scalar_prefetch=1,
            grid=(1,),
            in_specs=[here] * 2,
            out_specs=[here] * len(groups),
            scratch_shapes=[
                pltpu.VMEM((seq_count * (rows - text_rows), hidden.shape[1]), jnp.bfloat16),
                pltpu.VMEM((total, ff), jnp.bfloat16),
                pltpu.VMEM((total, 1), jnp.float32),
            ],
        ),
        out_shape=[pltpu.VMEM((len(group) * rows, wide), jnp.bfloat16) for group in groups],
        compiler_params=pltpu.CompilerParams(vmem_limit_bytes=14 * 1024 * 1024),
        cost_estimate=pl.CostEstimate(
            flops=2 * total * wide * ff,
            bytes_accessed=2 * ff * wide + 2 * total * wide,
            transcendentals=0,
        ),
    )(places, kept(hidden), kept(down_weight))


def add_up(*parts):
    total = parts[0].astype(jnp.float32)
    for part in parts[1:]:
        total = total + part.astype(jnp.float32)
    return total.astype(jnp.bfloat16)


def ring_shards(
    text_tokens, panels, panel_target, expert_ids, gate_weights, gate_up_weight, down_weight
):
    seq_count, expert_count = lax.axis_size("seq"), lax.axis_size("expert")
    ring = Ring(seq_count, expert_count)
    text_rows, tok_count = text_tokens.shape[0], expert_ids.shape[0]
    me = lax.axis_index(AXES)

    def along(array):
        return lax.ppermute(array, AXES, ring.step())

    def across(array):
        return lax.ppermute(array, AXES, ring.swap())

    own = pack_call(
        text_tokens, panels, panel_target, expert_ids, gate_weights, ring.devices, expert_count
    )
    seq_of = ring.owner_of // expert_count
    numbers = np.arange(ring.devices, dtype=np.int32)[:, None]
    places = np.concatenate([numbers, seq_of, ring.sources_of.reshape(ring.devices, -1)], axis=1)
    places = jnp.asarray(places)[me]

    all_rows = ring.slot_count * tok_count

    def tied(*values):
        return lax.optimization_barrier(values)

    def rows_of(*slots):
        return [slot * tok_count for slot in slots]

    lead = along(own)
    other = across(own)
    own, places = tied(own, places)
    hidden, gate_up = hidden_call([own, other], rows_of(0, 1), gate_up_weight, None, all_rows)
    trail = along(other)
    hidden, lead = tied(hidden, lead)
    hidden, trail = tied(hidden, trail)
    swapped = swapped_rows = None
    for s in range(1, ring.half):
        next_lead = along(lead)
        lead_across = across(lead)
        if swapped:
            hidden, gate_up = hidden_call(swapped, swapped_rows, gate_up, hidden, all_rows)
            hidden, trail = tied(hidden, trail)
        next_trail = along(trail) if s + 1 < ring.half else None
        trail_across = across(trail)
        extra = down_weight if s == 1 else None
        blocks, block_rows = [lead, trail], rows_of(4 * s, 4 * s + 1)
        at_last = s + 1 == ring.half
        if at_last:
            blocks, block_rows = blocks + [lead_across], block_rows + rows_of(4 * s + 3)
        hidden, gate_up, *down = hidden_call(
            blocks, block_rows, gate_up, hidden, all_rows, extra, unroll=at_last
        )
        if down:
            (down_here,) = down
        hidden, lead, lead_across, trail_across = tied(
            hidden, next_lead, lead_across, trail_across
        )
        trail = next_trail
        swapped, swapped_rows = [trail_across], rows_of(4 * s + 2)
        if not at_last:
            swapped, swapped_rows = swapped + [lead_across], swapped_rows + rows_of(4 * s + 3)
    hidden, gate_up = hidden_call(swapped, swapped_rows, gate_up, hidden, all_rows, unroll=True)
    far = [lead, across(lead)]
    (hidden,) = hidden_call(
        far, rows_of(2, 3), gate_up, hidden, all_rows, last=True, unroll=True
    )

    def outputs(hidden, *groups, unroll=False):
        return down_call(
            hidden, places, down_here, groups, tok_count, text_rows, seq_count, ring.devices, unroll
        )

    def for_other(hidden, s):
        groups = ((4 * s + 1,), (4 * s,)) if s else ((1,),)
        first, *rest = outputs(hidden, *groups, unroll=s + 2 >= ring.half)
        first, hidden = tied(first, hidden)
        return [first, *rest], hidden

    def for_own(hidden, s):
        groups = ((4 * s + 2,), (4 * s + 3,)) if s else ((0,),)
        first, *rest = outputs(hidden, *groups, unroll=s + 1 >= ring.half)
        first, hidden = tied(first, hidden)
        return [first, *rest], hidden

    def sent(hidden, *parts):
        total, hidden = tied(add_up(*parts), hidden)
        return along(total), hidden

    mine, others = outputs(hidden, (2,), (3,), unroll=True)
    mine, hidden = tied(mine, hidden)
    swapped, hidden = for_other(hidden, ring.half - 1)
    swapped = [across(array) for array in swapped]
    lead, hidden = sent(hidden, mine, across(others))
    mine, hidden = for_own(hidden, ring.half - 1)
    trail, hidden = sent(hidden, mine[1], swapped[1])
    for s in range(ring.half - 1, 0, -1):
        if s + 1 == ring.half:
            lead, hidden = sent(hidden, mine[0], swapped[0], lead)
        next_swapped, hidden = for_other(hidden, s - 1)
        if s > 1:
            next_swapped = [across(array) for array in next_swapped]
        if s + 1 < ring.half:
            lead, hidden = sent(hidden, mine[0], swapped[0], lead)
        mine, hidden = for_own(hidden, s - 1)
        swapped = next_swapped
        if s > 1:
            trail, hidden = sent(hidden, mine[1], swapped[1], trail)
    return add_up(mine[0], across(add_up(swapped[0], trail)), lead)


def solution(mesh):
    placed = (
        P(("groups", "seq", "expert"), "tensor"),
        P(("groups", "seq", "expert"), None, "tensor"),
        P(("groups", "seq", "expert")),
        P(("groups", "seq", "expert"), None),
        P(("groups", "seq", "expert"), None),
        P(("seq", "expert"), None, "tensor", None),
        P(("seq", "expert"), "tensor", None),
    )

    def chosen(*args):
        seq_count, expert_count = mesh.shape["seq"], mesh.shape["expert"]
        owners = seq_count * expert_count
        tok_count, top_count = args[3].shape[0] // (mesh.shape["groups"] * owners), args[3].shape[1]
        experts_all = args[5].shape[0]
        slot_rows = experts_all * slot_capacity(tok_count, top_count, experts_all)
        dense = owners * tok_count <= 2 * slot_rows
        ring = dense and mesh.shape["tensor"] == 1 and expert_count == 4 and experts_all == owners
        ring = ring and seq_count > 2
        body = ring_shards if ring else slot_shards
        return jax.shard_map(
            body,
            mesh=mesh,
            in_specs=placed,
            out_specs=P(("groups", "seq", "expert"), "tensor"),
            check_vma=False,
        )(*args)

    return chosen
```

```python
import functools

import jax
import jax.numpy as jnp
import numpy as np
from jax import lax
from jax.experimental import pallas as pl
from jax.experimental.pallas import tpu as pltpu
from jax.sharding import PartitionSpec as P

AXES = ("seq", "expert")


def slot_shards(
    text_tokens, panels, panel_target, expert_ids, gate_weights, gate_up_weight, down_weight
):
    seq_count = lax.axis_size("seq")
    expert_count = lax.axis_size("expert")
    owner_count = seq_count * expert_count
    pan_count = panels.shape[0]
    cap_panel = max(2, (3 * pan_count + 2 * seq_count - 1) // (2 * seq_count))
    slot_range = jnp.arange(pan_count, dtype=jnp.int32)
    owner_dev = panel_target // pan_count
    dest_seq = owner_dev // expert_count
    dest_slot = panel_target % pan_count
    onehot = (dest_seq[:, None] == jnp.arange(seq_count, dtype=jnp.int32)[None, :]).astype(
        jnp.int32
    )
    earlier = jnp.cumsum(onehot, axis=0) - onehot
    placing = dest_seq * cap_panel + jnp.sum(earlier * onehot, axis=1)
    outgoing = (
        jnp.zeros((seq_count * cap_panel,) + panels.shape[1:], panels.dtype).at[placing].set(panels)
    )
    labels = jnp.full((seq_count * cap_panel,), -1, jnp.int32).at[placing].set(dest_slot)
    arrived, arrived_labels = (
        lax.all_to_all(outgoing, "seq", split_axis=0, concat_axis=0, tiled=True),
        lax.all_to_all(labels, "seq", split_axis=0, concat_axis=0, tiled=True),
    )
    matches = (arrived_labels[None, :] == slot_range[:, None]).astype(jnp.bfloat16)
    image_rows = jnp.einsum(
        "qn,nrd->qrd", matches, arrived, preferred_element_type=jnp.float32
    ).astype(jnp.bfloat16)
    half_rows = jnp.concatenate([text_tokens, image_rows.reshape(-1, image_rows.shape[-1])], axis=0)
    tokens = lax.all_gather(half_rows, "tensor", axis=1, tiled=True)
    feature_width = tokens.shape[1]
    tok_count, top_count = expert_ids.shape
    experts_all = owner_count * gate_up_weight.shape[0]
    capacity = slot_capacity(tok_count, top_count, experts_all)
    flat_ids = expert_ids.reshape(-1)
    onehot_ids = (flat_ids[:, None] == jnp.arange(experts_all, dtype=jnp.int32)[None, :]).astype(
        jnp.int32
    )
    before = jnp.cumsum(onehot_ids, axis=0) - onehot_ids
    placing_ids = flat_ids * capacity + jnp.sum(before * onehot_ids, axis=1)
    source_rows = jnp.arange(tok_count * top_count, dtype=jnp.int32) // top_count
    outgoing_rows = (
        jnp.zeros((experts_all * capacity, feature_width), tokens.dtype)
        .at[placing_ids]
        .set(tokens[source_rows])
    )
    load_counts = jnp.sum(onehot_ids, axis=0).reshape(experts_all, 1)
    outgoing_rows = outgoing_rows.reshape(experts_all, capacity, feature_width)
    pair_weight = gate_up_weight[0]
    out_weight = down_weight[0]
    arrived_rows, arrived_loads = (
        lax.all_to_all(outgoing_rows, AXES, split_axis=0, concat_axis=0, tiled=True),
        lax.all_to_all(load_counts, AXES, split_axis=0, concat_axis=0, tiled=True),
    )
    arrived_rows = arrived_rows.reshape(-1, feature_width)
    slot_total = arrived_rows.shape[0]
    slot_index = jnp.arange(capacity, dtype=jnp.int32)
    is_live = (slot_index[None, :] < arrived_loads).reshape(-1)
    live_int = is_live.astype(jnp.int32)
    compact_at = jnp.cumsum(live_int) - live_int
    live_total = jnp.sum(live_int)
    compact_src = (
        jnp.zeros((slot_total,), jnp.int32)
        .at[jnp.where(is_live, compact_at, slot_total)]
        .set(jnp.arange(slot_total, dtype=jnp.int32), mode="drop")
    )

    def expert_block(block_no, partial_out):
        chosen = lax.dynamic_slice_in_dim(compact_src, block_no * 128, 128)
        block_rows = arrived_rows[chosen]
        gate_up = jnp.einsum(
            "rd,gfd->grf", block_rows, pair_weight, preferred_element_type=jnp.float32
        )
        hidden = (jax.nn.silu(gate_up[0]) * gate_up[1]).astype(jnp.bfloat16)
        result = jnp.dot(hidden, out_weight, preferred_element_type=jnp.float32)
        return lax.dynamic_update_slice_in_dim(partial_out, result, block_no * 128, 0)

    block_total = (live_total + 127) // 128
    padded_total = (slot_total + 127) // 128 * 128
    partial_out = lax.fori_loop(
        0, block_total, expert_block, jnp.zeros((padded_total, feature_width), jnp.float32)
    )
    summed = lax.psum_scatter(partial_out, "tensor", scatter_dimension=1, tiled=True).astype(
        jnp.bfloat16
    )
    out_width = summed.shape[1]
    returned = jnp.where(
        is_live[:, None], summed[jnp.where(is_live, compact_at, 0)], jnp.zeros((), jnp.bfloat16)
    )
    came_back = lax.all_to_all(
        returned.reshape(experts_all, capacity, out_width),
        AXES,
        split_axis=0,
        concat_axis=0,
        tiled=True,
    )
    half_width = came_back.shape[2]
    picked = came_back.reshape(-1, half_width)[placing_ids].reshape(
        tok_count, top_count, half_width
    )
    mixed_out = jnp.sum(gate_weights[:, :, None] * picked.astype(jnp.float32), axis=1)
    return mixed_out.astype(jnp.bfloat16)


def slot_capacity(tok_count, top_count, experts_all):
    return min(tok_count, (2 * tok_count * top_count // experts_all + 7) // 8 * 8)


class Ring:
    def __init__(self, seq_count, expert_count):
        self.seq, self.expert = seq_count, expert_count
        self.chips = 2 * seq_count
        self.half = seq_count
        self.devices = seq_count * expert_count
        self.slot_count = 4 * self.half
        self.owner_of = np.zeros((self.devices, self.slot_count), np.int32)
        self.sources_of = np.zeros((self.devices, self.slot_count, seq_count), np.int32)
        for d in range(self.devices):
            p, c = self.place(d)
            slots = [(0, 0), (0, 1), (self.half, 0), (self.half, 1)]
            for s in range(1, self.half):
                along = -s if c else s
                slots += [(-along, 0), (-along, 1), (along, 0), (along, 1)]
            slot_of = {(r % self.chips, k): i for i, (r, k) in enumerate(slots)}
            for i, (r, k) in enumerate(slots):
                q = (p + r) % self.chips
                self.owner_of[d, i] = self.device(q, c ^ k)
                x = q // seq_count
                for z in range(seq_count):
                    pos = z if x == 0 else self.chips - 1 - z
                    self.sources_of[d, i, z] = slot_of[((pos - p) % self.chips, k)]

    def place(self, d):
        z, e = divmod(d, self.expert)
        x, c = divmod(e, 2)
        return (z if x == 0 else self.chips - 1 - z), c

    def device(self, pos, c):
        x, z = (0, pos) if pos < self.seq else (1, self.chips - 1 - pos)
        return z * self.expert + x * 2 + c

    def step(self):
        pairs = []
        for d in range(self.devices):
            p, c = self.place(d)
            pairs.append((d, self.device((p + (-1 if c else 1)) % self.chips, c)))
        return pairs

    def swap(self):
        return [(d, d ^ 1) for d in range(self.devices)]


def kept(array):
    return pltpu.with_memory_space_constraint(array, pltpu.VMEM)


def distant(array):
    return pltpu.with_memory_space_constraint(array, pltpu.HBM)


def steps(count, unroll, body):
    if unroll:
        for i in range(count):
            body(i)
    else:
        pl.loop(0, count)(body)


def chunk_start(i, chunk):
    return i * chunk if isinstance(i, int) else pl.multiple_of(i * chunk, chunk)


def pack_kernel(
    experts, expert_count, text_ref, panels_ref, target_hbm, ids_hbm, gates_hbm, out_ref,
    target_ref, ids_ref, gates_ref, sems,
):
    text_rows, wide = text_ref.shape
    rows, width = out_ref.shape[0], out_ref.shape[1] - wide
    pan_count = target_ref.shape[1]
    panel_rows = (rows - text_rows) // pan_count
    copies = [
        pltpu.make_async_copy(text_ref, out_ref.at[:text_rows, :wide], sems.at[0]),
        pltpu.make_async_copy(panels_ref, out_ref.at[text_rows:, :wide], sems.at[1]),
    ]
    tables = [
        pltpu.make_async_copy(target_hbm, target_ref, sems.at[2]),
        pltpu.make_async_copy(ids_hbm, ids_ref, sems.at[3]),
        pltpu.make_async_copy(gates_hbm, gates_ref, sems.at[4]),
    ]
    for copy in tables + copies:
        copy.start()
    for copy in tables:
        copy.wait()
    lane = lax.broadcasted_iota(jnp.int32, (rows, width), 1)
    term = sum((lane >= i * experts).astype(jnp.int32) for i in range(1, 4))
    expert = (lane - term * experts).astype(jnp.float32)
    diagonal = lax.broadcasted_iota(jnp.int32, (rows, rows), 0) == lax.broadcasted_iota(
        jnp.int32, (rows, rows), 1
    )

    def upright(row):
        return jnp.sum(jnp.where(diagonal, row, 0.0), axis=1, keepdims=True)

    gate = jnp.zeros((rows, width), jnp.float32)
    for k in range(ids_ref.shape[0]):
        number = upright(ids_ref[k : k + 1, :].astype(jnp.float32))
        gate += jnp.where(number == expert, upright(gates_ref[k : k + 1, :]), 0.0)
    high = gate.astype(jnp.bfloat16).astype(jnp.float32)
    middle = (gate - high).astype(jnp.bfloat16).astype(jnp.float32)
    low = gate - high - middle
    panel = lax.broadcasted_iota(jnp.int32, (rows, pan_count), 1)
    row = lax.broadcasted_iota(jnp.int32, (rows, pan_count), 0) - text_rows
    past = row - panel * panel_rows
    mine = (past >= 0) & (past < panel_rows)
    target = jnp.sum(
        jnp.where(mine, target_ref[...].astype(jnp.float32), 0.0), axis=1, keepdims=True
    )
    within = jnp.sum(jnp.where(mine, past.astype(jnp.float32), 0.0), axis=1, keepdims=True)
    owner, seq = jnp.zeros_like(target), jnp.zeros_like(target)
    for i in range(1, experts):
        passed = jnp.where(target >= i * pan_count, 1.0, 0.0)
        owner += passed
        if i % expert_count == 0:
            seq += passed
    place = (target - owner * pan_count) * panel_rows + within
    tags = jnp.where(term == 0, high, jnp.where(term == 1, middle, jnp.where(term == 2, low, 0.0)))
    tags = jnp.where(lane == 3 * experts, seq, jnp.where(lane == 3 * experts + 1, place, tags))
    out_ref[:, wide:] = tags.astype(jnp.bfloat16)
    for copy in copies:
        copy.wait()


def pack_call(text_tokens, panels, panel_target, expert_ids, gate_weights, experts, expert_count):
    rows, wide = expert_ids.shape[0], text_tokens.shape[1]
    width = (3 * experts + 2 + 127) // 128 * 128
    here, far = pl.BlockSpec(memory_space=pltpu.VMEM), pl.BlockSpec(memory_space=pltpu.HBM)
    return pl.pallas_call(
        functools.partial(pack_kernel, experts, expert_count),
        in_specs=[far] * 5,
        out_specs=here,
        out_shape=pltpu.VMEM((rows, wide + width), jnp.bfloat16),
        scratch_shapes=[
            pltpu.VMEM((1, panel_target.shape[0]), jnp.int32),
            pltpu.VMEM(expert_ids.shape[::-1], jnp.int32),
            pltpu.VMEM(gate_weights.shape[::-1], jnp.float32),
            pltpu.SemaphoreType.DMA((5,)),
        ],
        compiler_params=pltpu.CompilerParams(vmem_limit_bytes=14 * 1024 * 1024),
    )(
        distant(text_tokens),
        distant(panels.reshape(-1, wide)),
        distant(panel_target[None, :]),
        distant(expert_ids.T),
        distant(gate_weights.T),
    )


def hidden_kernel(places, rows, chunk, fetch, unroll, *refs):
    x_refs, refs = refs[: len(places)], refs[len(places) :]
    if fetch == "gate_up":
        far_ref, out_ref, w_ref, x_all, sems = refs
    elif fetch == "down":
        w_ref, _, far_ref, out_ref, _, down_ref, x_all, sems = refs
    else:
        w_ref, _, out_ref, x_all = refs[0], refs[1], refs[2], refs[-1]
    ff, wide = w_ref.shape[2:]
    whole, rest = divmod(ff, chunk)

    def fetched(i, width):
        part = pl.ds(pl.multiple_of(i * chunk, chunk), width)
        return pltpu.make_async_copy(far_ref.at[0, :, part], w_ref.at[0, :, part], sems.at[i])

    if fetch == "gate_up":
        for i in range(whole):
            fetched(i, chunk).start()
        if rest:
            fetched(whole, rest).start()
    if fetch == "down":
        pltpu.make_async_copy(far_ref, down_ref, sems.at[0]).start()
    for i, at in enumerate(places):
        x_all[i * rows : (i + 1) * rows, :] = x_refs[i][:, :wide]
        out_ref[at : at + rows, ff:] = x_refs[i][:, wide:]

    def step(i, width):
        if fetch == "gate_up":
            fetched(i, width).wait()
        part = pl.ds(chunk_start(i, chunk), width)
        weight = w_ref[0, :, part, :].reshape(2 * width, wide)
        both = lax.dot_general(
            x_all[...], weight, (((1,), (1,)), ((), ())), preferred_element_type=jnp.float32
        )
        gate, up = both[:, :width], both[:, width:]
        gate = 0.5 * gate
        hidden = (gate * (1.0 + jnp.tanh(gate)) * up).astype(out_ref.dtype)
        for i, at in enumerate(places):
            out_ref[at : at + rows, part] = hidden[i * rows : (i + 1) * rows]

    def full_step(i):
        step(i, chunk)

    steps(whole, unroll, full_step)
    if rest:
        step(whole, rest)
    if fetch == "down":
        pltpu.make_async_copy(far_ref, down_ref, sems.at[0]).wait()


def hidden_call(
    blocks, places, gate_up_weight, hidden, all_rows, down_weight=None, last=False, unroll=False
):
    rows, width = blocks[0].shape
    ff, wide = gate_up_weight.shape[2:]
    count = len(blocks)
    chunk = 256
    here, far = pl.BlockSpec(memory_space=pltpu.VMEM), pl.BlockSpec(memory_space=pltpu.HBM)
    args, in_specs = [kept(block) for block in blocks], [here] * count
    out_shape, aliases = [pltpu.VMEM((all_rows, ff + width - wide), jnp.bfloat16)], {}
    scratch = [pltpu.VMEM((count * rows, wide), jnp.bfloat16)]
    fetch = None
    if hidden is None:
        fetch = "gate_up"
        args, in_specs = args + [distant(gate_up_weight)], in_specs + [far]
        out_shape.append(pltpu.VMEM(gate_up_weight.shape, gate_up_weight.dtype))
        scratch.append(pltpu.SemaphoreType.DMA((pl.cdiv(ff, chunk),)))
    else:
        args, in_specs = args + [kept(gate_up_weight), kept(hidden)], in_specs + [here, here]
        aliases = {count + 1: 0}
        if not last:
            out_shape.append(pltpu.VMEM(gate_up_weight.shape, gate_up_weight.dtype))
            aliases[count] = 1
        if down_weight is not None:
            fetch = "down"
            args, in_specs = args + [distant(down_weight)], in_specs + [far]
            out_shape.append(pltpu.VMEM(down_weight.shape, down_weight.dtype))
            scratch.append(pltpu.SemaphoreType.DMA((1,)))
    return pl.pallas_call(
        functools.partial(hidden_kernel, tuple(places), rows, chunk, fetch, unroll),
        in_specs=in_specs,
        out_specs=[here] * len(out_shape),
        out_shape=out_shape,
        scratch_shapes=scratch,
        input_output_aliases=aliases,
        compiler_params=pltpu.CompilerParams(vmem_limit_bytes=14 * 1024 * 1024),
        cost_estimate=pl.CostEstimate(
            flops=4 * count * rows * wide * ff,
            bytes_accessed=4 * ff * wide + 2 * count * rows * (wide + ff),
            transcendentals=count * rows * ff,
        ),
    )(*args)


def down_kernel(
    groups, rows, text_rows, seq_count, experts, chunk, unroll, places_ref, hidden_ref, w_ref, *refs
):
    out_refs, (column, picked, scale) = refs[:-3], refs[-3:]
    slots = [slot for group in groups for slot in group]
    image_rows = rows - text_rows
    slot_total = hidden_ref.shape[0] // rows
    ff = w_ref.shape[1]
    width = hidden_ref.shape[1] - ff
    expert = places_ref[0]
    lane = lax.broadcasted_iota(jnp.int32, (1, width), 1)
    is_gate = (lane == expert) | (lane == expert + experts) | (lane == expert + 2 * experts)
    place_of = jnp.where(lane == 3 * experts, float(image_rows), 0.0)
    place_of = jnp.where(lane == 3 * experts + 1, 1.0, place_of)
    wanted = lax.broadcasted_iota(jnp.int32, (1, image_rows), 1)
    for j, slot in enumerate(slots):
        at = slot * rows
        picked[j * rows : j * rows + text_rows, :] = hidden_ref[at : at + text_rows, :ff]
        for z in range(seq_count):
            source = places_ref[1 + slot_total + slot * seq_count + z]
            start = pl.multiple_of(source * rows + text_rows, 16)
            column[z * image_rows : (z + 1) * image_rows, :] = hidden_ref[
                pl.ds(start, image_rows), :
            ]
        place = column[:, ff:].astype(jnp.float32) * place_of
        place = jnp.sum(place, axis=1, keepdims=True)
        first = places_ref[1 + slot] * image_rows
        match = jnp.where(place == (wanted + first).astype(jnp.float32), 1.0, 0.0)
        rows_here = lax.dot_general(
            match.astype(jnp.bfloat16),
            column[:, :ff],
            (((0,), (0,)), ((), ())),
            preferred_element_type=jnp.float32,
        )
        picked[j * rows + text_rows : (j + 1) * rows, :] = rows_here.astype(jnp.bfloat16)
        gates = jnp.where(is_gate, hidden_ref[at : at + rows, ff:].astype(jnp.float32), 0.0)
        scale[j * rows : (j + 1) * rows, :] = jnp.sum(gates, axis=1, keepdims=True)

    def step(i):
        part = pl.ds(chunk_start(i, chunk), chunk)
        result = jnp.dot(picked[...], w_ref[0, :, part], preferred_element_type=jnp.float32)
        scaled = result.astype(jnp.bfloat16).astype(jnp.float32) * scale[...]
        scaled = scaled.astype(jnp.bfloat16)
        start = 0
        for out_ref in out_refs:
            out_ref[:, part] = scaled[start : start + out_ref.shape[0]]
            start += out_ref.shape[0]

    steps(w_ref.shape[2] // chunk, unroll, step)


def down_call(
    hidden, places, down_weight, groups, rows, text_rows, seq_count, experts, unroll
):
    _, ff, wide = down_weight.shape
    total = sum(len(group) for group in groups) * rows
    here = pl.BlockSpec(memory_space=pltpu.VMEM)
    return pl.pallas_call(
        functools.partial(
            down_kernel, groups, rows, text_rows, seq_count, experts, 512, unroll
        ),
        grid_spec=pltpu.PrefetchScalarGridSpec(
            num_scalar_prefetch=1,
            grid=(1,),
            in_specs=[here] * 2,
            out_specs=[here] * len(groups),
            scratch_shapes=[
                pltpu.VMEM((seq_count * (rows - text_rows), hidden.shape[1]), jnp.bfloat16),
                pltpu.VMEM((total, ff), jnp.bfloat16),
                pltpu.VMEM((total, 1), jnp.float32),
            ],
        ),
        out_shape=[pltpu.VMEM((len(group) * rows, wide), jnp.bfloat16) for group in groups],
        compiler_params=pltpu.CompilerParams(vmem_limit_bytes=14 * 1024 * 1024),
        cost_estimate=pl.CostEstimate(
            flops=2 * total * wide * ff,
            bytes_accessed=2 * ff * wide + 2 * total * wide,
            transcendentals=0,
        ),
    )(places, kept(hidden), kept(down_weight))


def add_up(*parts):
    total = parts[0].astype(jnp.float32)
    for part in parts[1:]:
        total = total + part.astype(jnp.float32)
    return total.astype(jnp.bfloat16)


def ring_shards(
    text_tokens, panels, panel_target, expert_ids, gate_weights, gate_up_weight, down_weight
):
    seq_count, expert_count = lax.axis_size("seq"), lax.axis_size("expert")
    ring = Ring(seq_count, expert_count)
    text_rows, tok_count = text_tokens.shape[0], expert_ids.shape[0]
    me = lax.axis_index(AXES)

    def along(array):
        return lax.ppermute(array, AXES, ring.step())

    def across(array):
        return lax.ppermute(array, AXES, ring.swap())

    own = pack_call(
        text_tokens, panels, panel_target, expert_ids, gate_weights, ring.devices, expert_count
    )
    seq_of = ring.owner_of // expert_count
    numbers = np.arange(ring.devices, dtype=np.int32)[:, None]
    places = np.concatenate([numbers, seq_of, ring.sources_of.reshape(ring.devices, -1)], axis=1)
    places = jnp.asarray(places)[me]

    all_rows = ring.slot_count * tok_count

    def tied(*values):
        return lax.optimization_barrier(values)

    def rows_of(*slots):
        return [slot * tok_count for slot in slots]

    lead = along(own)
    other = across(own)
    own, places = tied(own, places)
    hidden, gate_up = hidden_call([own, other], rows_of(0, 1), gate_up_weight, None, all_rows)
    trail = along(other)
    hidden, lead = tied(hidden, lead)
    hidden, trail = tied(hidden, trail)
    swapped = swapped_rows = None
    for s in range(1, ring.half):
        next_lead = along(lead)
        lead_across = across(lead)
        if swapped:
            hidden, gate_up = hidden_call(swapped, swapped_rows, gate_up, hidden, all_rows)
            hidden, trail = tied(hidden, trail)
        next_trail = along(trail) if s + 1 < ring.half else None
        trail_across = across(trail)
        extra = down_weight if s == 1 else None
        hidden, gate_up, *down = hidden_call(
            [lead, trail], rows_of(4 * s, 4 * s + 1), gate_up, hidden, all_rows, extra
        )
        if down:
            (down_here,) = down
        hidden, lead, lead_across, trail_across = tied(
            hidden, next_lead, lead_across, trail_across
        )
        trail = next_trail
        swapped, swapped_rows = [lead_across, trail_across], rows_of(4 * s + 3, 4 * s + 2)
    hidden, gate_up = hidden_call(swapped, swapped_rows, gate_up, hidden, all_rows, unroll=True)
    far = [lead, across(lead)]
    (hidden,) = hidden_call(
        far, rows_of(2, 3), gate_up, hidden, all_rows, last=True, unroll=True
    )

    def outputs(hidden, *groups, unroll=False):
        return down_call(
            hidden, places, down_here, groups, tok_count, text_rows, seq_count, ring.devices, unroll
        )

    def for_other(hidden, s):
        groups = ((4 * s + 1,), (4 * s,)) if s else ((1,),)
        first, *rest = outputs(hidden, *groups, unroll=s > 0)
        first, hidden = tied(first, hidden)
        return [first, *rest], hidden

    def for_own(hidden, s):
        groups = ((4 * s + 2,), (4 * s + 3,)) if s else ((0,),)
        first, *rest = outputs(hidden, *groups, unroll=s > 0)
        first, hidden = tied(first, hidden)
        return [first, *rest], hidden

    def sent(hidden, *parts):
        total, hidden = tied(add_up(*parts), hidden)
        return along(total), hidden

    mine, others = outputs(hidden, (2,), (3,), unroll=True)
    mine, hidden = tied(mine, hidden)
    swapped, hidden = for_other(hidden, ring.half - 1)
    swapped = [across(array) for array in swapped]
    lead, hidden = sent(hidden, mine, across(others))
    mine, hidden = for_own(hidden, ring.half - 1)
    trail, hidden = sent(hidden, mine[1], swapped[1])
    for s in range(ring.half - 1, 0, -1):
        if s + 1 == ring.half:
            lead, hidden = sent(hidden, mine[0], swapped[0], lead)
        next_swapped, hidden = for_other(hidden, s - 1)
        if s > 1:
            next_swapped = [across(array) for array in next_swapped]
        if s + 1 < ring.half:
            lead, hidden = sent(hidden, mine[0], swapped[0], lead)
        mine, hidden = for_own(hidden, s - 1)
        swapped = next_swapped
        if s > 1:
            trail, hidden = sent(hidden, mine[1], swapped[1], trail)
    return add_up(mine[0], across(add_up(swapped[0], trail)), lead)


def solution(mesh):
    placed = (
        P(("groups", "seq", "expert"), "tensor"),
        P(("groups", "seq", "expert"), None, "tensor"),
        P(("groups", "seq", "expert")),
        P(("groups", "seq", "expert"), None),
        P(("groups", "seq", "expert"), None),
        P(("seq", "expert"), None, "tensor", None),
        P(("seq", "expert"), "tensor", None),
    )

    def chosen(*args):
        seq_count, expert_count = mesh.shape["seq"], mesh.shape["expert"]
        owners = seq_count * expert_count
        tok_count, top_count = args[3].shape[0] // (mesh.shape["groups"] * owners), args[3].shape[1]
        experts_all = args[5].shape[0]
        slot_rows = experts_all * slot_capacity(tok_count, top_count, experts_all)
        dense = owners * tok_count <= 2 * slot_rows
        ring = dense and mesh.shape["tensor"] == 1 and expert_count == 4 and experts_all == owners
        ring = ring and seq_count > 2
        body = ring_shards if ring else slot_shards
        return jax.shard_map(
            body,
            mesh=mesh,
            in_specs=placed,
            out_specs=P(("groups", "seq", "expert"), "tensor"),
            check_vma=False,
        )(*args)

    return chosen
```

```python
import functools

import jax
import jax.numpy as jnp
import numpy as np
from jax import lax
from jax.experimental import pallas as pl
from jax.experimental.pallas import tpu as pltpu
from jax.sharding import PartitionSpec as P

AXES = ("seq", "expert")


def slot_shards(
    text_tokens, panels, panel_target, expert_ids, gate_weights, gate_up_weight, down_weight
):
    seq_count = lax.axis_size("seq")
    expert_count = lax.axis_size("expert")
    owner_count = seq_count * expert_count
    pan_count = panels.shape[0]
    cap_panel = max(2, (3 * pan_count + 2 * seq_count - 1) // (2 * seq_count))
    slot_range = jnp.arange(pan_count, dtype=jnp.int32)
    owner_dev = panel_target // pan_count
    dest_seq = owner_dev // expert_count
    dest_slot = panel_target % pan_count
    onehot = (dest_seq[:, None] == jnp.arange(seq_count, dtype=jnp.int32)[None, :]).astype(
        jnp.int32
    )
    earlier = jnp.cumsum(onehot, axis=0) - onehot
    placing = dest_seq * cap_panel + jnp.sum(earlier * onehot, axis=1)
    outgoing = (
        jnp.zeros((seq_count * cap_panel,) + panels.shape[1:], panels.dtype).at[placing].set(panels)
    )
    labels = jnp.full((seq_count * cap_panel,), -1, jnp.int32).at[placing].set(dest_slot)
    arrived, arrived_labels = (
        lax.all_to_all(outgoing, "seq", split_axis=0, concat_axis=0, tiled=True),
        lax.all_to_all(labels, "seq", split_axis=0, concat_axis=0, tiled=True),
    )
    matches = (arrived_labels[None, :] == slot_range[:, None]).astype(jnp.bfloat16)
    image_rows = jnp.einsum(
        "qn,nrd->qrd", matches, arrived, preferred_element_type=jnp.float32
    ).astype(jnp.bfloat16)
    half_rows = jnp.concatenate([text_tokens, image_rows.reshape(-1, image_rows.shape[-1])], axis=0)
    tokens = lax.all_gather(half_rows, "tensor", axis=1, tiled=True)
    feature_width = tokens.shape[1]
    tok_count, top_count = expert_ids.shape
    experts_all = owner_count * gate_up_weight.shape[0]
    capacity = slot_capacity(tok_count, top_count, experts_all)
    flat_ids = expert_ids.reshape(-1)
    onehot_ids = (flat_ids[:, None] == jnp.arange(experts_all, dtype=jnp.int32)[None, :]).astype(
        jnp.int32
    )
    before = jnp.cumsum(onehot_ids, axis=0) - onehot_ids
    placing_ids = flat_ids * capacity + jnp.sum(before * onehot_ids, axis=1)
    source_rows = jnp.arange(tok_count * top_count, dtype=jnp.int32) // top_count
    outgoing_rows = (
        jnp.zeros((experts_all * capacity, feature_width), tokens.dtype)
        .at[placing_ids]
        .set(tokens[source_rows])
    )
    load_counts = jnp.sum(onehot_ids, axis=0).reshape(experts_all, 1)
    outgoing_rows = outgoing_rows.reshape(experts_all, capacity, feature_width)
    pair_weight = gate_up_weight[0]
    out_weight = down_weight[0]
    arrived_rows, arrived_loads = (
        lax.all_to_all(outgoing_rows, AXES, split_axis=0, concat_axis=0, tiled=True),
        lax.all_to_all(load_counts, AXES, split_axis=0, concat_axis=0, tiled=True),
    )
    arrived_rows = arrived_rows.reshape(-1, feature_width)
    slot_total = arrived_rows.shape[0]
    slot_index = jnp.arange(capacity, dtype=jnp.int32)
    is_live = (slot_index[None, :] < arrived_loads).reshape(-1)
    live_int = is_live.astype(jnp.int32)
    compact_at = jnp.cumsum(live_int) - live_int
    live_total = jnp.sum(live_int)
    compact_src = (
        jnp.zeros((slot_total,), jnp.int32)
        .at[jnp.where(is_live, compact_at, slot_total)]
        .set(jnp.arange(slot_total, dtype=jnp.int32), mode="drop")
    )

    def expert_block(block_no, partial_out):
        chosen = lax.dynamic_slice_in_dim(compact_src, block_no * 128, 128)
        block_rows = arrived_rows[chosen]
        gate_up = jnp.einsum(
            "rd,gfd->grf", block_rows, pair_weight, preferred_element_type=jnp.float32
        )
        hidden = (jax.nn.silu(gate_up[0]) * gate_up[1]).astype(jnp.bfloat16)
        result = jnp.dot(hidden, out_weight, preferred_element_type=jnp.float32)
        return lax.dynamic_update_slice_in_dim(partial_out, result, block_no * 128, 0)

    block_total = (live_total + 127) // 128
    padded_total = (slot_total + 127) // 128 * 128
    partial_out = lax.fori_loop(
        0, block_total, expert_block, jnp.zeros((padded_total, feature_width), jnp.float32)
    )
    summed = lax.psum_scatter(partial_out, "tensor", scatter_dimension=1, tiled=True).astype(
        jnp.bfloat16
    )
    out_width = summed.shape[1]
    returned = jnp.where(
        is_live[:, None], summed[jnp.where(is_live, compact_at, 0)], jnp.zeros((), jnp.bfloat16)
    )
    came_back = lax.all_to_all(
        returned.reshape(experts_all, capacity, out_width),
        AXES,
        split_axis=0,
        concat_axis=0,
        tiled=True,
    )
    half_width = came_back.shape[2]
    picked = came_back.reshape(-1, half_width)[placing_ids].reshape(
        tok_count, top_count, half_width
    )
    mixed_out = jnp.sum(gate_weights[:, :, None] * picked.astype(jnp.float32), axis=1)
    return mixed_out.astype(jnp.bfloat16)


def slot_capacity(tok_count, top_count, experts_all):
    return min(tok_count, (2 * tok_count * top_count // experts_all + 7) // 8 * 8)


class Ring:
    def __init__(self, seq_count, expert_count):
        self.seq, self.expert = seq_count, expert_count
        self.chips = 2 * seq_count
        self.half = seq_count
        self.devices = seq_count * expert_count
        self.slot_count = 4 * self.half
        self.owner_of = np.zeros((self.devices, self.slot_count), np.int32)
        self.sources_of = np.zeros((self.devices, self.slot_count, seq_count), np.int32)
        for d in range(self.devices):
            p, c = self.place(d)
            slots = [(0, 0), (0, 1), (self.half, 0), (self.half, 1)]
            for s in range(1, self.half):
                along = -s if c else s
                slots += [(-along, 0), (-along, 1), (along, 0), (along, 1)]
            slot_of = {(r % self.chips, k): i for i, (r, k) in enumerate(slots)}
            for i, (r, k) in enumerate(slots):
                q = (p + r) % self.chips
                self.owner_of[d, i] = self.device(q, c ^ k)
                x = q // seq_count
                for z in range(seq_count):
                    pos = z if x == 0 else self.chips - 1 - z
                    self.sources_of[d, i, z] = slot_of[((pos - p) % self.chips, k)]

    def place(self, d):
        z, e = divmod(d, self.expert)
        x, c = divmod(e, 2)
        return (z if x == 0 else self.chips - 1 - z), c

    def device(self, pos, c):
        x, z = (0, pos) if pos < self.seq else (1, self.chips - 1 - pos)
        return z * self.expert + x * 2 + c

    def step(self):
        pairs = []
        for d in range(self.devices):
            p, c = self.place(d)
            pairs.append((d, self.device((p + (-1 if c else 1)) % self.chips, c)))
        return pairs

    def swap(self):
        return [(d, d ^ 1) for d in range(self.devices)]


def kept(array):
    return pltpu.with_memory_space_constraint(array, pltpu.VMEM)


def distant(array):
    return pltpu.with_memory_space_constraint(array, pltpu.HBM)


def steps(count, unroll, body):
    if unroll:
        for i in range(count):
            body(i)
    else:
        pl.loop(0, count)(body)


def chunk_start(i, chunk):
    return i * chunk if isinstance(i, int) else pl.multiple_of(i * chunk, chunk)


def pack_kernel(
    experts, expert_count, text_ref, panels_ref, target_hbm, ids_hbm, gates_hbm, out_ref,
    target_ref, ids_ref, gates_ref, sems,
):
    text_rows, wide = text_ref.shape
    rows, width = out_ref.shape[0], out_ref.shape[1] - wide
    pan_count = target_ref.shape[1]
    panel_rows = (rows - text_rows) // pan_count
    copies = [
        pltpu.make_async_copy(text_ref, out_ref.at[:text_rows, :wide], sems.at[0]),
        pltpu.make_async_copy(panels_ref, out_ref.at[text_rows:, :wide], sems.at[1]),
    ]
    tables = [
        pltpu.make_async_copy(target_hbm, target_ref, sems.at[2]),
        pltpu.make_async_copy(ids_hbm, ids_ref, sems.at[3]),
        pltpu.make_async_copy(gates_hbm, gates_ref, sems.at[4]),
    ]
    for copy in tables + copies:
        copy.start()
    for copy in tables:
        copy.wait()
    lane = lax.broadcasted_iota(jnp.int32, (rows, width), 1)
    term = sum((lane >= i * experts).astype(jnp.int32) for i in range(1, 4))
    expert = (lane - term * experts).astype(jnp.float32)
    diagonal = lax.broadcasted_iota(jnp.int32, (rows, rows), 0) == lax.broadcasted_iota(
        jnp.int32, (rows, rows), 1
    )

    def upright(row):
        return jnp.sum(jnp.where(diagonal, row, 0.0), axis=1, keepdims=True)

    gate = jnp.zeros((rows, width), jnp.float32)
    for k in range(ids_ref.shape[0]):
        number = upright(ids_ref[k : k + 1, :].astype(jnp.float32))
        gate += jnp.where(number == expert, upright(gates_ref[k : k + 1, :]), 0.0)
    high = gate.astype(jnp.bfloat16).astype(jnp.float32)
    middle = (gate - high).astype(jnp.bfloat16).astype(jnp.float32)
    low = gate - high - middle
    panel = lax.broadcasted_iota(jnp.int32, (rows, pan_count), 1)
    row = lax.broadcasted_iota(jnp.int32, (rows, pan_count), 0) - text_rows
    past = row - panel * panel_rows
    mine = (past >= 0) & (past < panel_rows)
    target = jnp.sum(
        jnp.where(mine, target_ref[...].astype(jnp.float32), 0.0), axis=1, keepdims=True
    )
    within = jnp.sum(jnp.where(mine, past.astype(jnp.float32), 0.0), axis=1, keepdims=True)
    owner, seq = jnp.zeros_like(target), jnp.zeros_like(target)
    for i in range(1, experts):
        passed = jnp.where(target >= i * pan_count, 1.0, 0.0)
        owner += passed
        if i % expert_count == 0:
            seq += passed
    place = (target - owner * pan_count) * panel_rows + within
    tags = jnp.where(term == 0, high, jnp.where(term == 1, middle, jnp.where(term == 2, low, 0.0)))
    tags = jnp.where(lane == 3 * experts, seq, jnp.where(lane == 3 * experts + 1, place, tags))
    out_ref[:, wide:] = tags.astype(jnp.bfloat16)
    for copy in copies:
        copy.wait()


def pack_call(text_tokens, panels, panel_target, expert_ids, gate_weights, experts, expert_count):
    rows, wide = expert_ids.shape[0], text_tokens.shape[1]
    width = (3 * experts + 2 + 127) // 128 * 128
    here, far = pl.BlockSpec(memory_space=pltpu.VMEM), pl.BlockSpec(memory_space=pltpu.HBM)
    return pl.pallas_call(
        functools.partial(pack_kernel, experts, expert_count),
        in_specs=[far] * 5,
        out_specs=here,
        out_shape=pltpu.VMEM((rows, wide + width), jnp.bfloat16),
        scratch_shapes=[
            pltpu.VMEM((1, panel_target.shape[0]), jnp.int32),
            pltpu.VMEM(expert_ids.shape[::-1], jnp.int32),
            pltpu.VMEM(gate_weights.shape[::-1], jnp.float32),
            pltpu.SemaphoreType.DMA((5,)),
        ],
        compiler_params=pltpu.CompilerParams(vmem_limit_bytes=14 * 1024 * 1024),
    )(
        distant(text_tokens),
        distant(panels.reshape(-1, wide)),
        distant(panel_target[None, :]),
        distant(expert_ids.T),
        distant(gate_weights.T),
    )


def hidden_kernel(places, rows, chunk, fetch, unroll, *refs):
    x_refs, refs = refs[: len(places)], refs[len(places) :]
    if fetch == "gate_up":
        far_ref, out_ref, w_ref, x_all, sems = refs
    elif fetch == "down":
        w_ref, _, far_ref, out_ref, _, down_ref, x_all, sems = refs
    else:
        w_ref, _, out_ref, x_all = refs[0], refs[1], refs[2], refs[-1]
    ff, wide = w_ref.shape[2:]
    whole, rest = divmod(ff, chunk)

    def fetched(i, width):
        part = pl.ds(pl.multiple_of(i * chunk, chunk), width)
        return pltpu.make_async_copy(far_ref.at[0, :, part], w_ref.at[0, :, part], sems.at[i])

    if fetch == "gate_up":
        for i in range(whole):
            fetched(i, chunk).start()
        if rest:
            fetched(whole, rest).start()
    if fetch == "down":
        pltpu.make_async_copy(far_ref, down_ref, sems.at[0]).start()
    for i, at in enumerate(places):
        x_all[i * rows : (i + 1) * rows, :] = x_refs[i][:, :wide]
        out_ref[at : at + rows, ff:] = x_refs[i][:, wide:]

    def step(i, width):
        if fetch == "gate_up":
            fetched(i, width).wait()
        part = pl.ds(chunk_start(i, chunk), width)
        weight = w_ref[0, :, part, :].reshape(2 * width, wide)
        both = lax.dot_general(
            x_all[...], weight, (((1,), (1,)), ((), ())), preferred_element_type=jnp.float32
        )
        gate, up = both[:, :width], both[:, width:]
        gate = 0.5 * gate
        hidden = (gate * (1.0 + jnp.tanh(gate)) * up).astype(out_ref.dtype)
        for i, at in enumerate(places):
            out_ref[at : at + rows, part] = hidden[i * rows : (i + 1) * rows]

    def full_step(i):
        step(i, chunk)

    steps(whole, unroll, full_step)
    if rest:
        step(whole, rest)
    if fetch == "down":
        pltpu.make_async_copy(far_ref, down_ref, sems.at[0]).wait()


def hidden_call(
    blocks, places, gate_up_weight, hidden, all_rows, down_weight=None, last=False, unroll=False
):
    rows, width = blocks[0].shape
    ff, wide = gate_up_weight.shape[2:]
    count = len(blocks)
    chunk = 256
    here, far = pl.BlockSpec(memory_space=pltpu.VMEM), pl.BlockSpec(memory_space=pltpu.HBM)
    args, in_specs = [kept(block) for block in blocks], [here] * count
    out_shape, aliases = [pltpu.VMEM((all_rows, ff + width - wide), jnp.bfloat16)], {}
    scratch = [pltpu.VMEM((count * rows, wide), jnp.bfloat16)]
    fetch = None
    if hidden is None:
        fetch = "gate_up"
        args, in_specs = args + [distant(gate_up_weight)], in_specs + [far]
        out_shape.append(pltpu.VMEM(gate_up_weight.shape, gate_up_weight.dtype))
        scratch.append(pltpu.SemaphoreType.DMA((pl.cdiv(ff, chunk),)))
    else:
        args, in_specs = args + [kept(gate_up_weight), kept(hidden)], in_specs + [here, here]
        aliases = {count + 1: 0}
        if not last:
            out_shape.append(pltpu.VMEM(gate_up_weight.shape, gate_up_weight.dtype))
            aliases[count] = 1
        if down_weight is not None:
            fetch = "down"
            args, in_specs = args + [distant(down_weight)], in_specs + [far]
            out_shape.append(pltpu.VMEM(down_weight.shape, down_weight.dtype))
            scratch.append(pltpu.SemaphoreType.DMA((1,)))
    return pl.pallas_call(
        functools.partial(hidden_kernel, tuple(places), rows, chunk, fetch, unroll),
        in_specs=in_specs,
        out_specs=[here] * len(out_shape),
        out_shape=out_shape,
        scratch_shapes=scratch,
        input_output_aliases=aliases,
        compiler_params=pltpu.CompilerParams(vmem_limit_bytes=14 * 1024 * 1024),
        cost_estimate=pl.CostEstimate(
            flops=4 * count * rows * wide * ff,
            bytes_accessed=4 * ff * wide + 2 * count * rows * (wide + ff),
            transcendentals=count * rows * ff,
        ),
    )(*args)


def down_kernel(
    groups, rows, text_rows, seq_count, experts, chunk, unroll, places_ref, hidden_ref, w_ref, *refs
):
    out_refs, (column, picked, scale) = refs[:-3], refs[-3:]
    slots = [slot for group in groups for slot in group]
    image_rows = rows - text_rows
    slot_total = hidden_ref.shape[0] // rows
    ff = w_ref.shape[1]
    width = hidden_ref.shape[1] - ff
    expert = places_ref[0]
    lane = lax.broadcasted_iota(jnp.int32, (1, width), 1)
    is_gate = (lane == expert) | (lane == expert + experts) | (lane == expert + 2 * experts)
    place_of = jnp.where(lane == 3 * experts, float(image_rows), 0.0)
    place_of = jnp.where(lane == 3 * experts + 1, 1.0, place_of)
    wanted = lax.broadcasted_iota(jnp.int32, (1, image_rows), 1)
    for j, slot in enumerate(slots):
        at = slot * rows
        picked[j * rows : j * rows + text_rows, :] = hidden_ref[at : at + text_rows, :ff]
        for z in range(seq_count):
            source = places_ref[1 + slot_total + slot * seq_count + z]
            start = pl.multiple_of(source * rows + text_rows, 16)
            column[z * image_rows : (z + 1) * image_rows, :] = hidden_ref[
                pl.ds(start, image_rows), :
            ]
        place = column[:, ff:].astype(jnp.float32) * place_of
        place = jnp.sum(place, axis=1, keepdims=True)
        first = places_ref[1 + slot] * image_rows
        match = jnp.where(place == (wanted + first).astype(jnp.float32), 1.0, 0.0)
        rows_here = lax.dot_general(
            match.astype(jnp.bfloat16),
            column[:, :ff],
            (((0,), (0,)), ((), ())),
            preferred_element_type=jnp.float32,
        )
        picked[j * rows + text_rows : (j + 1) * rows, :] = rows_here.astype(jnp.bfloat16)
        gates = jnp.where(is_gate, hidden_ref[at : at + rows, ff:].astype(jnp.float32), 0.0)
        scale[j * rows : (j + 1) * rows, :] = jnp.sum(gates, axis=1, keepdims=True)

    def step(i):
        part = pl.ds(chunk_start(i, chunk), chunk)
        result = jnp.dot(picked[...], w_ref[0, :, part], preferred_element_type=jnp.float32)
        scaled = result.astype(jnp.bfloat16).astype(jnp.float32) * scale[...]
        scaled = scaled.astype(jnp.bfloat16)
        start = 0
        for out_ref in out_refs:
            out_ref[:, part] = scaled[start : start + out_ref.shape[0]]
            start += out_ref.shape[0]

    steps(w_ref.shape[2] // chunk, unroll, step)


def down_call(
    hidden, places, down_weight, groups, rows, text_rows, seq_count, experts, unroll
):
    _, ff, wide = down_weight.shape
    total = sum(len(group) for group in groups) * rows
    here = pl.BlockSpec(memory_space=pltpu.VMEM)
    return pl.pallas_call(
        functools.partial(
            down_kernel, groups, rows, text_rows, seq_count, experts, 512, unroll
        ),
        grid_spec=pltpu.PrefetchScalarGridSpec(
            num_scalar_prefetch=1,
            grid=(1,),
            in_specs=[here] * 2,
            out_specs=[here] * len(groups),
            scratch_shapes=[
                pltpu.VMEM((seq_count * (rows - text_rows), hidden.shape[1]), jnp.bfloat16),
                pltpu.VMEM((total, ff), jnp.bfloat16),
                pltpu.VMEM((total, 1), jnp.float32),
            ],
        ),
        out_shape=[pltpu.VMEM((len(group) * rows, wide), jnp.bfloat16) for group in groups],
        compiler_params=pltpu.CompilerParams(vmem_limit_bytes=14 * 1024 * 1024),
        cost_estimate=pl.CostEstimate(
            flops=2 * total * wide * ff,
            bytes_accessed=2 * ff * wide + 2 * total * wide,
            transcendentals=0,
        ),
    )(places, kept(hidden), kept(down_weight))


def add_up(*parts):
    total = parts[0].astype(jnp.float32)
    for part in parts[1:]:
        total = total + part.astype(jnp.float32)
    return total.astype(jnp.bfloat16)


def ring_shards(
    text_tokens, panels, panel_target, expert_ids, gate_weights, gate_up_weight, down_weight
):
    seq_count, expert_count = lax.axis_size("seq"), lax.axis_size("expert")
    ring = Ring(seq_count, expert_count)
    text_rows, tok_count = text_tokens.shape[0], expert_ids.shape[0]
    me = lax.axis_index(AXES)

    def along(array):
        return lax.ppermute(array, AXES, ring.step())

    def across(array):
        return lax.ppermute(array, AXES, ring.swap())

    own = pack_call(
        text_tokens, panels, panel_target, expert_ids, gate_weights, ring.devices, expert_count
    )
    seq_of = ring.owner_of // expert_count
    numbers = np.arange(ring.devices, dtype=np.int32)[:, None]
    places = np.concatenate([numbers, seq_of, ring.sources_of.reshape(ring.devices, -1)], axis=1)
    places = jnp.asarray(places)[me]

    all_rows = ring.slot_count * tok_count

    def tied(*values):
        return lax.optimization_barrier(values)

    def rows_of(*slots):
        return [slot * tok_count for slot in slots]

    lead = along(own)
    other = across(own)
    own, places = tied(own, places)
    hidden, gate_up = hidden_call([own, other], rows_of(0, 1), gate_up_weight, None, all_rows)
    trail = along(other)
    hidden, lead = tied(hidden, lead)
    hidden, trail = tied(hidden, trail)
    swapped = swapped_rows = None
    for s in range(1, ring.half):
        next_lead = along(lead)
        lead_across = across(lead)
        if swapped:
            hidden, gate_up = hidden_call(swapped, swapped_rows, gate_up, hidden, all_rows)
            hidden, trail = tied(hidden, trail)
        next_trail = along(trail) if s + 1 < ring.half else None
        trail_across = across(trail)
        extra = down_weight if s == 1 else None
        hidden, gate_up, *down = hidden_call(
            [lead, trail], rows_of(4 * s, 4 * s + 1), gate_up, hidden, all_rows, extra
        )
        if down:
            (down_here,) = down
        hidden, lead, lead_across, trail_across = tied(
            hidden, next_lead, lead_across, trail_across
        )
        trail = next_trail
        swapped, swapped_rows = [lead_across, trail_across], rows_of(4 * s + 3, 4 * s + 2)
    hidden, gate_up = hidden_call(swapped, swapped_rows, gate_up, hidden, all_rows, unroll=True)
    far = [lead, across(lead)]
    (hidden,) = hidden_call(
        far, rows_of(2, 3), gate_up, hidden, all_rows, last=True, unroll=True
    )

    def outputs(hidden, *groups, unroll=False):
        return down_call(
            hidden, places, down_here, groups, tok_count, text_rows, seq_count, ring.devices, unroll
        )

    def for_other(hidden, s):
        groups = ((4 * s + 1,), (4 * s,)) if s else ((1,),)
        first, *rest = outputs(hidden, *groups, unroll=s > 1)
        first, hidden = tied(first, hidden)
        return [first, *rest], hidden

    def for_own(hidden, s):
        groups = ((4 * s + 2,), (4 * s + 3,)) if s else ((0,),)
        first, *rest = outputs(hidden, *groups, unroll=s > 1)
        first, hidden = tied(first, hidden)
        return [first, *rest], hidden

    def sent(hidden, *parts):
        total, hidden = tied(add_up(*parts), hidden)
        return along(total), hidden

    mine, others = outputs(hidden, (2,), (3,), unroll=True)
    mine, hidden = tied(mine, hidden)
    swapped, hidden = for_other(hidden, ring.half - 1)
    swapped = [across(array) for array in swapped]
    lead, hidden = sent(hidden, mine, across(others))
    mine, hidden = for_own(hidden, ring.half - 1)
    trail, hidden = sent(hidden, mine[1], swapped[1])
    for s in range(ring.half - 1, 0, -1):
        if s + 1 == ring.half:
            lead, hidden = sent(hidden, mine[0], swapped[0], lead)
        next_swapped, hidden = for_other(hidden, s - 1)
        if s > 1:
            next_swapped = [across(array) for array in next_swapped]
        if s + 1 < ring.half:
            lead, hidden = sent(hidden, mine[0], swapped[0], lead)
        mine, hidden = for_own(hidden, s - 1)
        swapped = next_swapped
        if s > 1:
            trail, hidden = sent(hidden, mine[1], swapped[1], trail)
    return add_up(mine[0], across(add_up(swapped[0], trail)), lead)


def solution(mesh):
    placed = (
        P(("groups", "seq", "expert"), "tensor"),
        P(("groups", "seq", "expert"), None, "tensor"),
        P(("groups", "seq", "expert")),
        P(("groups", "seq", "expert"), None),
        P(("groups", "seq", "expert"), None),
        P(("seq", "expert"), None, "tensor", None),
        P(("seq", "expert"), "tensor", None),
    )

    def chosen(*args):
        seq_count, expert_count = mesh.shape["seq"], mesh.shape["expert"]
        owners = seq_count * expert_count
        tok_count, top_count = args[3].shape[0] // (mesh.shape["groups"] * owners), args[3].shape[1]
        experts_all = args[5].shape[0]
        slot_rows = experts_all * slot_capacity(tok_count, top_count, experts_all)
        dense = owners * tok_count <= 2 * slot_rows
        ring = dense and mesh.shape["tensor"] == 1 and expert_count == 4 and experts_all == owners
        ring = ring and seq_count > 2
        body = ring_shards if ring else slot_shards
        return jax.shard_map(
            body,
            mesh=mesh,
            in_specs=placed,
            out_specs=P(("groups", "seq", "expert"), "tensor"),
            check_vma=False,
        )(*args)

    return chosen
```

```python
import functools

import jax
import jax.numpy as jnp
import numpy as np
from jax import lax
from jax.experimental import pallas as pl
from jax.experimental.pallas import tpu as pltpu
from jax.sharding import PartitionSpec as P

AXES = ("seq", "expert")


def slot_shards(
    text_tokens, panels, panel_target, expert_ids, gate_weights, gate_up_weight, down_weight
):
    seq_count = lax.axis_size("seq")
    expert_count = lax.axis_size("expert")
    owner_count = seq_count * expert_count
    pan_count = panels.shape[0]
    cap_panel = max(2, (3 * pan_count + 2 * seq_count - 1) // (2 * seq_count))
    slot_range = jnp.arange(pan_count, dtype=jnp.int32)
    owner_dev = panel_target // pan_count
    dest_seq = owner_dev // expert_count
    dest_slot = panel_target % pan_count
    onehot = (dest_seq[:, None] == jnp.arange(seq_count, dtype=jnp.int32)[None, :]).astype(
        jnp.int32
    )
    earlier = jnp.cumsum(onehot, axis=0) - onehot
    placing = dest_seq * cap_panel + jnp.sum(earlier * onehot, axis=1)
    outgoing = (
        jnp.zeros((seq_count * cap_panel,) + panels.shape[1:], panels.dtype).at[placing].set(panels)
    )
    labels = jnp.full((seq_count * cap_panel,), -1, jnp.int32).at[placing].set(dest_slot)
    arrived, arrived_labels = (
        lax.all_to_all(outgoing, "seq", split_axis=0, concat_axis=0, tiled=True),
        lax.all_to_all(labels, "seq", split_axis=0, concat_axis=0, tiled=True),
    )
    matches = (arrived_labels[None, :] == slot_range[:, None]).astype(jnp.bfloat16)
    image_rows = jnp.einsum(
        "qn,nrd->qrd", matches, arrived, preferred_element_type=jnp.float32
    ).astype(jnp.bfloat16)
    half_rows = jnp.concatenate([text_tokens, image_rows.reshape(-1, image_rows.shape[-1])], axis=0)
    tokens = lax.all_gather(half_rows, "tensor", axis=1, tiled=True)
    feature_width = tokens.shape[1]
    tok_count, top_count = expert_ids.shape
    experts_all = owner_count * gate_up_weight.shape[0]
    capacity = slot_capacity(tok_count, top_count, experts_all)
    flat_ids = expert_ids.reshape(-1)
    onehot_ids = (flat_ids[:, None] == jnp.arange(experts_all, dtype=jnp.int32)[None, :]).astype(
        jnp.int32
    )
    before = jnp.cumsum(onehot_ids, axis=0) - onehot_ids
    placing_ids = flat_ids * capacity + jnp.sum(before * onehot_ids, axis=1)
    source_rows = jnp.arange(tok_count * top_count, dtype=jnp.int32) // top_count
    outgoing_rows = (
        jnp.zeros((experts_all * capacity, feature_width), tokens.dtype)
        .at[placing_ids]
        .set(tokens[source_rows])
    )
    load_counts = jnp.sum(onehot_ids, axis=0).reshape(experts_all, 1)
    outgoing_rows = outgoing_rows.reshape(experts_all, capacity, feature_width)
    pair_weight = gate_up_weight[0]
    out_weight = down_weight[0]
    arrived_rows, arrived_loads = (
        lax.all_to_all(outgoing_rows, AXES, split_axis=0, concat_axis=0, tiled=True),
        lax.all_to_all(load_counts, AXES, split_axis=0, concat_axis=0, tiled=True),
    )
    arrived_rows = arrived_rows.reshape(-1, feature_width)
    slot_total = arrived_rows.shape[0]
    slot_index = jnp.arange(capacity, dtype=jnp.int32)
    is_live = (slot_index[None, :] < arrived_loads).reshape(-1)
    live_int = is_live.astype(jnp.int32)
    compact_at = jnp.cumsum(live_int) - live_int
    live_total = jnp.sum(live_int)
    compact_src = (
        jnp.zeros((slot_total,), jnp.int32)
        .at[jnp.where(is_live, compact_at, slot_total)]
        .set(jnp.arange(slot_total, dtype=jnp.int32), mode="drop")
    )

    def expert_block(block_no, partial_out):
        chosen = lax.dynamic_slice_in_dim(compact_src, block_no * 128, 128)
        block_rows = arrived_rows[chosen]
        gate_up = jnp.einsum(
            "rd,gfd->grf", block_rows, pair_weight, preferred_element_type=jnp.float32
        )
        hidden = (jax.nn.silu(gate_up[0]) * gate_up[1]).astype(jnp.bfloat16)
        result = jnp.dot(hidden, out_weight, preferred_element_type=jnp.float32)
        return lax.dynamic_update_slice_in_dim(partial_out, result, block_no * 128, 0)

    block_total = (live_total + 127) // 128
    padded_total = (slot_total + 127) // 128 * 128
    partial_out = lax.fori_loop(
        0, block_total, expert_block, jnp.zeros((padded_total, feature_width), jnp.float32)
    )
    summed = lax.psum_scatter(partial_out, "tensor", scatter_dimension=1, tiled=True).astype(
        jnp.bfloat16
    )
    out_width = summed.shape[1]
    returned = jnp.where(
        is_live[:, None], summed[jnp.where(is_live, compact_at, 0)], jnp.zeros((), jnp.bfloat16)
    )
    came_back = lax.all_to_all(
        returned.reshape(experts_all, capacity, out_width),
        AXES,
        split_axis=0,
        concat_axis=0,
        tiled=True,
    )
    half_width = came_back.shape[2]
    picked = came_back.reshape(-1, half_width)[placing_ids].reshape(
        tok_count, top_count, half_width
    )
    mixed_out = jnp.sum(gate_weights[:, :, None] * picked.astype(jnp.float32), axis=1)
    return mixed_out.astype(jnp.bfloat16)


def slot_capacity(tok_count, top_count, experts_all):
    return min(tok_count, (2 * tok_count * top_count // experts_all + 7) // 8 * 8)


class Ring:
    def __init__(self, seq_count, expert_count):
        self.seq, self.expert = seq_count, expert_count
        self.chips = 2 * seq_count
        self.half = seq_count
        self.devices = seq_count * expert_count
        self.slot_count = 4 * self.half
        self.owner_of = np.zeros((self.devices, self.slot_count), np.int32)
        self.sources_of = np.zeros((self.devices, self.slot_count, seq_count), np.int32)
        for d in range(self.devices):
            p, c = self.place(d)
            slots = [(0, 0), (0, 1), (self.half, 0), (self.half, 1)]
            for s in range(1, self.half):
                along = -s if c else s
                slots += [(-along, 0), (-along, 1), (along, 0), (along, 1)]
            slot_of = {(r % self.chips, k): i for i, (r, k) in enumerate(slots)}
            for i, (r, k) in enumerate(slots):
                q = (p + r) % self.chips
                self.owner_of[d, i] = self.device(q, c ^ k)
                x = q // seq_count
                for z in range(seq_count):
                    pos = z if x == 0 else self.chips - 1 - z
                    self.sources_of[d, i, z] = slot_of[((pos - p) % self.chips, k)]

    def place(self, d):
        z, e = divmod(d, self.expert)
        x, c = divmod(e, 2)
        return (z if x == 0 else self.chips - 1 - z), c

    def device(self, pos, c):
        x, z = (0, pos) if pos < self.seq else (1, self.chips - 1 - pos)
        return z * self.expert + x * 2 + c

    def step(self):
        pairs = []
        for d in range(self.devices):
            p, c = self.place(d)
            pairs.append((d, self.device((p + (-1 if c else 1)) % self.chips, c)))
        return pairs

    def swap(self):
        return [(d, d ^ 1) for d in range(self.devices)]


def kept(array):
    return pltpu.with_memory_space_constraint(array, pltpu.VMEM)


def distant(array):
    return pltpu.with_memory_space_constraint(array, pltpu.HBM)


def steps(count, unroll, body):
    if unroll:
        for i in range(count):
            body(i)
    else:
        pl.loop(0, count)(body)


def chunk_start(i, chunk):
    return i * chunk if isinstance(i, int) else pl.multiple_of(i * chunk, chunk)


def pack_kernel(
    experts, expert_count, text_ref, panels_ref, target_hbm, ids_hbm, gates_hbm, out_ref,
    target_ref, ids_ref, gates_ref, sems,
):
    text_rows, wide = text_ref.shape
    rows, width = out_ref.shape[0], out_ref.shape[1] - wide
    pan_count = target_ref.shape[1]
    panel_rows = (rows - text_rows) // pan_count
    copies = [
        pltpu.make_async_copy(text_ref, out_ref.at[:text_rows, :wide], sems.at[0]),
        pltpu.make_async_copy(panels_ref, out_ref.at[text_rows:, :wide], sems.at[1]),
    ]
    tables = [
        pltpu.make_async_copy(target_hbm, target_ref, sems.at[2]),
        pltpu.make_async_copy(ids_hbm, ids_ref, sems.at[3]),
        pltpu.make_async_copy(gates_hbm, gates_ref, sems.at[4]),
    ]
    for copy in tables + copies:
        copy.start()
    for copy in tables:
        copy.wait()
    lane = lax.broadcasted_iota(jnp.int32, (rows, width), 1)
    term = sum((lane >= i * experts).astype(jnp.int32) for i in range(1, 4))
    expert = (lane - term * experts).astype(jnp.float32)
    diagonal = lax.broadcasted_iota(jnp.int32, (rows, rows), 0) == lax.broadcasted_iota(
        jnp.int32, (rows, rows), 1
    )

    def upright(row):
        return jnp.sum(jnp.where(diagonal, row, 0.0), axis=1, keepdims=True)

    gate = jnp.zeros((rows, width), jnp.float32)
    for k in range(ids_ref.shape[0]):
        number = upright(ids_ref[k : k + 1, :].astype(jnp.float32))
        gate += jnp.where(number == expert, upright(gates_ref[k : k + 1, :]), 0.0)
    high = gate.astype(jnp.bfloat16).astype(jnp.float32)
    middle = (gate - high).astype(jnp.bfloat16).astype(jnp.float32)
    low = gate - high - middle
    panel = lax.broadcasted_iota(jnp.int32, (rows, pan_count), 1)
    row = lax.broadcasted_iota(jnp.int32, (rows, pan_count), 0) - text_rows
    past = row - panel * panel_rows
    mine = (past >= 0) & (past < panel_rows)
    target = jnp.sum(
        jnp.where(mine, target_ref[...].astype(jnp.float32), 0.0), axis=1, keepdims=True
    )
    within = jnp.sum(jnp.where(mine, past.astype(jnp.float32), 0.0), axis=1, keepdims=True)
    owner, seq = jnp.zeros_like(target), jnp.zeros_like(target)
    for i in range(1, experts):
        passed = jnp.where(target >= i * pan_count, 1.0, 0.0)
        owner += passed
        if i % expert_count == 0:
            seq += passed
    place = (target - owner * pan_count) * panel_rows + within
    tags = jnp.where(term == 0, high, jnp.where(term == 1, middle, jnp.where(term == 2, low, 0.0)))
    tags = jnp.where(lane == 3 * experts, seq, jnp.where(lane == 3 * experts + 1, place, tags))
    out_ref[:, wide:] = tags.astype(jnp.bfloat16)
    for copy in copies:
        copy.wait()


def pack_call(text_tokens, panels, panel_target, expert_ids, gate_weights, experts, expert_count):
    rows, wide = expert_ids.shape[0], text_tokens.shape[1]
    width = (3 * experts + 2 + 127) // 128 * 128
    here, far = pl.BlockSpec(memory_space=pltpu.VMEM), pl.BlockSpec(memory_space=pltpu.HBM)
    return pl.pallas_call(
        functools.partial(pack_kernel, experts, expert_count),
        in_specs=[far] * 5,
        out_specs=here,
        out_shape=pltpu.VMEM((rows, wide + width), jnp.bfloat16),
        scratch_shapes=[
            pltpu.VMEM((1, panel_target.shape[0]), jnp.int32),
            pltpu.VMEM(expert_ids.shape[::-1], jnp.int32),
            pltpu.VMEM(gate_weights.shape[::-1], jnp.float32),
            pltpu.SemaphoreType.DMA((5,)),
        ],
        compiler_params=pltpu.CompilerParams(vmem_limit_bytes=14 * 1024 * 1024),
    )(
        distant(text_tokens),
        distant(panels.reshape(-1, wide)),
        distant(panel_target[None, :]),
        distant(expert_ids.T),
        distant(gate_weights.T),
    )


def hidden_kernel(places, rows, chunk, fetch, unroll, *refs):
    x_refs, refs = refs[: len(places)], refs[len(places) :]
    if fetch == "gate_up":
        far_ref, out_ref, w_ref, x_all, sems = refs
    elif fetch == "down":
        w_ref, _, far_ref, out_ref, _, down_ref, x_all, sems = refs
    else:
        w_ref, _, out_ref, x_all = refs[0], refs[1], refs[2], refs[-1]
    ff, wide = w_ref.shape[2:]
    whole, rest = divmod(ff, chunk)

    def fetched(i, width):
        part = pl.ds(pl.multiple_of(i * chunk, chunk), width)
        return pltpu.make_async_copy(far_ref.at[0, :, part], w_ref.at[0, :, part], sems.at[i])

    if fetch == "gate_up":
        for i in range(whole):
            fetched(i, chunk).start()
        if rest:
            fetched(whole, rest).start()
    if fetch == "down":
        pltpu.make_async_copy(far_ref, down_ref, sems.at[0]).start()
    for i, at in enumerate(places):
        x_all[i * rows : (i + 1) * rows, :] = x_refs[i][:, :wide]
        out_ref[at : at + rows, ff:] = x_refs[i][:, wide:]

    def step(i, width):
        if fetch == "gate_up":
            fetched(i, width).wait()
        part = pl.ds(chunk_start(i, chunk), width)
        weight = w_ref[0, :, part, :].reshape(2 * width, wide)
        both = lax.dot_general(
            x_all[...], weight, (((1,), (1,)), ((), ())), preferred_element_type=jnp.float32
        )
        gate, up = both[:, :width], both[:, width:]
        gate = 0.5 * gate
        hidden = (gate * (1.0 + jnp.tanh(gate)) * up).astype(out_ref.dtype)
        for i, at in enumerate(places):
            out_ref[at : at + rows, part] = hidden[i * rows : (i + 1) * rows]

    def full_step(i):
        step(i, chunk)

    steps(whole, unroll, full_step)
    if rest:
        step(whole, rest)
    if fetch == "down":
        pltpu.make_async_copy(far_ref, down_ref, sems.at[0]).wait()


def hidden_call(
    blocks, places, gate_up_weight, hidden, all_rows, down_weight=None, last=False, unroll=False
):
    rows, width = blocks[0].shape
    ff, wide = gate_up_weight.shape[2:]
    count = len(blocks)
    chunk = 256
    here, far = pl.BlockSpec(memory_space=pltpu.VMEM), pl.BlockSpec(memory_space=pltpu.HBM)
    args, in_specs = [kept(block) for block in blocks], [here] * count
    out_shape, aliases = [pltpu.VMEM((all_rows, ff + width - wide), jnp.bfloat16)], {}
    scratch = [pltpu.VMEM((count * rows, wide), jnp.bfloat16)]
    fetch = None
    if hidden is None:
        fetch = "gate_up"
        args, in_specs = args + [distant(gate_up_weight)], in_specs + [far]
        out_shape.append(pltpu.VMEM(gate_up_weight.shape, gate_up_weight.dtype))
        scratch.append(pltpu.SemaphoreType.DMA((pl.cdiv(ff, chunk),)))
    else:
        args, in_specs = args + [kept(gate_up_weight), kept(hidden)], in_specs + [here, here]
        aliases = {count + 1: 0}
        if not last:
            out_shape.append(pltpu.VMEM(gate_up_weight.shape, gate_up_weight.dtype))
            aliases[count] = 1
        if down_weight is not None:
            fetch = "down"
            args, in_specs = args + [distant(down_weight)], in_specs + [far]
            out_shape.append(pltpu.VMEM(down_weight.shape, down_weight.dtype))
            scratch.append(pltpu.SemaphoreType.DMA((1,)))
    return pl.pallas_call(
        functools.partial(hidden_kernel, tuple(places), rows, chunk, fetch, unroll),
        in_specs=in_specs,
        out_specs=[here] * len(out_shape),
        out_shape=out_shape,
        scratch_shapes=scratch,
        input_output_aliases=aliases,
        compiler_params=pltpu.CompilerParams(vmem_limit_bytes=14 * 1024 * 1024),
        cost_estimate=pl.CostEstimate(
            flops=4 * count * rows * wide * ff,
            bytes_accessed=4 * ff * wide + 2 * count * rows * (wide + ff),
            transcendentals=count * rows * ff,
        ),
    )(*args)


def down_kernel(
    groups, rows, text_rows, seq_count, experts, chunk, unroll, places_ref, hidden_ref, w_ref, *refs
):
    out_refs, (column, picked, scale) = refs[:-3], refs[-3:]
    slots = [slot for group in groups for slot in group]
    image_rows = rows - text_rows
    slot_total = hidden_ref.shape[0] // rows
    ff = w_ref.shape[1]
    width = hidden_ref.shape[1] - ff
    expert = places_ref[0]
    lane = lax.broadcasted_iota(jnp.int32, (1, width), 1)
    is_gate = (lane == expert) | (lane == expert + experts) | (lane == expert + 2 * experts)
    place_of = jnp.where(lane == 3 * experts, float(image_rows), 0.0)
    place_of = jnp.where(lane == 3 * experts + 1, 1.0, place_of)
    wanted = lax.broadcasted_iota(jnp.int32, (1, image_rows), 1)
    for j, slot in enumerate(slots):
        at = slot * rows
        picked[j * rows : j * rows + text_rows, :] = hidden_ref[at : at + text_rows, :ff]
        for z in range(seq_count):
            source = places_ref[1 + slot_total + slot * seq_count + z]
            start = pl.multiple_of(source * rows + text_rows, 16)
            column[z * image_rows : (z + 1) * image_rows, :] = hidden_ref[
                pl.ds(start, image_rows), :
            ]
        place = column[:, ff:].astype(jnp.float32) * place_of
        place = jnp.sum(place, axis=1, keepdims=True)
        first = places_ref[1 + slot] * image_rows
        match = jnp.where(place == (wanted + first).astype(jnp.float32), 1.0, 0.0)
        rows_here = lax.dot_general(
            match.astype(jnp.bfloat16),
            column[:, :ff],
            (((0,), (0,)), ((), ())),
            preferred_element_type=jnp.float32,
        )
        picked[j * rows + text_rows : (j + 1) * rows, :] = rows_here.astype(jnp.bfloat16)
        gates = jnp.where(is_gate, hidden_ref[at : at + rows, ff:].astype(jnp.float32), 0.0)
        scale[j * rows : (j + 1) * rows, :] = jnp.sum(gates, axis=1, keepdims=True)

    def step(i):
        part = pl.ds(chunk_start(i, chunk), chunk)
        result = jnp.dot(picked[...], w_ref[0, :, part], preferred_element_type=jnp.float32)
        scaled = result.astype(jnp.bfloat16).astype(jnp.float32) * scale[...]
        scaled = scaled.astype(jnp.bfloat16)
        start = 0
        for out_ref in out_refs:
            out_ref[:, part] = scaled[start : start + out_ref.shape[0]]
            start += out_ref.shape[0]

    steps(w_ref.shape[2] // chunk, unroll, step)


def down_call(
    hidden, places, down_weight, groups, rows, text_rows, seq_count, experts, unroll
):
    _, ff, wide = down_weight.shape
    total = sum(len(group) for group in groups) * rows
    here = pl.BlockSpec(memory_space=pltpu.VMEM)
    return pl.pallas_call(
        functools.partial(
            down_kernel, groups, rows, text_rows, seq_count, experts, 640, unroll
        ),
        grid_spec=pltpu.PrefetchScalarGridSpec(
            num_scalar_prefetch=1,
            grid=(1,),
            in_specs=[here] * 2,
            out_specs=[here] * len(groups),
            scratch_shapes=[
                pltpu.VMEM((seq_count * (rows - text_rows), hidden.shape[1]), jnp.bfloat16),
                pltpu.VMEM((total, ff), jnp.bfloat16),
                pltpu.VMEM((total, 1), jnp.float32),
            ],
        ),
        out_shape=[pltpu.VMEM((len(group) * rows, wide), jnp.bfloat16) for group in groups],
        compiler_params=pltpu.CompilerParams(vmem_limit_bytes=14 * 1024 * 1024),
        cost_estimate=pl.CostEstimate(
            flops=2 * total * wide * ff,
            bytes_accessed=2 * ff * wide + 2 * total * wide,
            transcendentals=0,
        ),
    )(places, kept(hidden), kept(down_weight))


def add_up(*parts):
    total = parts[0].astype(jnp.float32)
    for part in parts[1:]:
        total = total + part.astype(jnp.float32)
    return total.astype(jnp.bfloat16)


def ring_shards(
    text_tokens, panels, panel_target, expert_ids, gate_weights, gate_up_weight, down_weight
):
    seq_count, expert_count = lax.axis_size("seq"), lax.axis_size("expert")
    ring = Ring(seq_count, expert_count)
    text_rows, tok_count = text_tokens.shape[0], expert_ids.shape[0]
    me = lax.axis_index(AXES)

    def along(array):
        return lax.ppermute(array, AXES, ring.step())

    def across(array):
        return lax.ppermute(array, AXES, ring.swap())

    own = pack_call(
        text_tokens, panels, panel_target, expert_ids, gate_weights, ring.devices, expert_count
    )
    seq_of = ring.owner_of // expert_count
    numbers = np.arange(ring.devices, dtype=np.int32)[:, None]
    places = np.concatenate([numbers, seq_of, ring.sources_of.reshape(ring.devices, -1)], axis=1)
    places = jnp.asarray(places)[me]

    all_rows = ring.slot_count * tok_count

    def tied(*values):
        return lax.optimization_barrier(values)

    def rows_of(*slots):
        return [slot * tok_count for slot in slots]

    lead = along(own)
    other = across(own)
    own, places = tied(own, places)
    hidden, gate_up = hidden_call([own, other], rows_of(0, 1), gate_up_weight, None, all_rows)
    trail = along(other)
    hidden, lead = tied(hidden, lead)
    hidden, trail = tied(hidden, trail)
    swapped = swapped_rows = None
    for s in range(1, ring.half):
        next_lead = along(lead)
        lead_across = across(lead)
        if swapped:
            hidden, gate_up = hidden_call(swapped, swapped_rows, gate_up, hidden, all_rows)
            hidden, trail = tied(hidden, trail)
        next_trail = along(trail) if s + 1 < ring.half else None
        trail_across = across(trail)
        extra = down_weight if s == 1 else None
        hidden, gate_up, *down = hidden_call(
            [lead, trail], rows_of(4 * s, 4 * s + 1), gate_up, hidden, all_rows, extra
        )
        if down:
            (down_here,) = down
        hidden, lead, lead_across, trail_across = tied(
            hidden, next_lead, lead_across, trail_across
        )
        trail = next_trail
        swapped, swapped_rows = [lead_across, trail_across], rows_of(4 * s + 3, 4 * s + 2)
    hidden, gate_up = hidden_call(swapped, swapped_rows, gate_up, hidden, all_rows, unroll=True)
    far = [lead, across(lead)]
    (hidden,) = hidden_call(
        far, rows_of(2, 3), gate_up, hidden, all_rows, last=True, unroll=True
    )

    def outputs(hidden, *groups, unroll=False):
        return down_call(
            hidden, places, down_here, groups, tok_count, text_rows, seq_count, ring.devices, unroll
        )

    def for_other(hidden, s):
        groups = ((4 * s + 1,), (4 * s,)) if s else ((1,),)
        first, *rest = outputs(hidden, *groups, unroll=s > 1)
        first, hidden = tied(first, hidden)
        return [first, *rest], hidden

    def for_own(hidden, s):
        groups = ((4 * s + 2,), (4 * s + 3,)) if s else ((0,),)
        first, *rest = outputs(hidden, *groups, unroll=s > 1)
        first, hidden = tied(first, hidden)
        return [first, *rest], hidden

    def sent(hidden, *parts):
        total, hidden = tied(add_up(*parts), hidden)
        return along(total), hidden

    mine, others = outputs(hidden, (2,), (3,), unroll=True)
    mine, hidden = tied(mine, hidden)
    swapped, hidden = for_other(hidden, ring.half - 1)
    swapped = [across(array) for array in swapped]
    lead, hidden = sent(hidden, mine, across(others))
    mine, hidden = for_own(hidden, ring.half - 1)
    trail, hidden = sent(hidden, mine[1], swapped[1])
    for s in range(ring.half - 1, 0, -1):
        if s + 1 == ring.half:
            lead, hidden = sent(hidden, mine[0], swapped[0], lead)
        next_swapped, hidden = for_other(hidden, s - 1)
        if s > 1:
            next_swapped = [across(array) for array in next_swapped]
        if s + 1 < ring.half:
            lead, hidden = sent(hidden, mine[0], swapped[0], lead)
        mine, hidden = for_own(hidden, s - 1)
        swapped = next_swapped
        if s > 1:
            trail, hidden = sent(hidden, mine[1], swapped[1], trail)
    return add_up(mine[0], across(add_up(swapped[0], trail)), lead)


def solution(mesh):
    placed = (
        P(("groups", "seq", "expert"), "tensor"),
        P(("groups", "seq", "expert"), None, "tensor"),
        P(("groups", "seq", "expert")),
        P(("groups", "seq", "expert"), None),
        P(("groups", "seq", "expert"), None),
        P(("seq", "expert"), None, "tensor", None),
        P(("seq", "expert"), "tensor", None),
    )

    def chosen(*args):
        seq_count, expert_count = mesh.shape["seq"], mesh.shape["expert"]
        owners = seq_count * expert_count
        tok_count, top_count = args[3].shape[0] // (mesh.shape["groups"] * owners), args[3].shape[1]
        experts_all = args[5].shape[0]
        slot_rows = experts_all * slot_capacity(tok_count, top_count, experts_all)
        dense = owners * tok_count <= 2 * slot_rows
        ring = dense and mesh.shape["tensor"] == 1 and expert_count == 4 and experts_all == owners
        ring = ring and seq_count > 2
        body = ring_shards if ring else slot_shards
        return jax.shard_map(
            body,
            mesh=mesh,
            in_specs=placed,
            out_specs=P(("groups", "seq", "expert"), "tensor"),
            check_vma=False,
        )(*args)

    return chosen
```
